32 devices in a mesh: wide: 16 (over z, y, x), narrow: 2 (over core).
Axes of the slice: x: 2, y: 2, z: 4, core: 2. Of those that a mesh axis runs over, the one named last changes fastest.
Arguments:
- tag_inputs: bfloat16 [49152, 512], P(('wide', 'narrow')), may hold values from -7 to 7
- image_inputs: bfloat16 [75264, 512], P(('wide', 'narrow')), may hold values from -14 to 14
- tag_counts: int32 [96], P(('wide', 'narrow')), may hold values from 1 to 512, as said below
- cotangent: bfloat16 [49152, 512], P(('wide', 'narrow')), may hold values from -6 to 6
- weight_qkv: float32 [512, 1536], P(('wide', 'narrow')), may hold values from -0.25 to 0.25
- weight_out: float32 [512, 512], P(('wide', 'narrow')), may hold values from -6 to 6
- weight_up: float32 [512, 1024], P(('wide', 'narrow')), may hold values from -0.25 to 0.25
- weight_down: float32 [1024, 512], P(('wide', 'narrow')), may hold values from -0.1875 to 0.1875
- norm_params: float32 [6, 512], P(None, ('wide', 'narrow')), may hold values from -1.2 to 1.9
- first_qkv: float32 [512, 1536], P(('wide', 'narrow')), may hold values from -0.00048828125 to 0.00048828125
- first_out: float32 [512, 512], P(('wide', 'narrow')), may hold values from -3.0517578e-05 to 3.0517578e-05
- first_up: float32 [512, 1024], P(('wide', 'narrow')), may hold values from -0.00048828125 to 0.00048828125
- first_down: float32 [1024, 512], P(('wide', 'narrow')), may hold values from -0.00048828125 to 0.00048828125
- first_norm: float32 [6, 512], P(None, ('wide', 'narrow')), may hold values from -0.00048828125 to 0.00048828125
- second_qkv: float32 [512, 1536], P(('wide', 'narrow')), may hold values from 2.384186e-10 to 3.8146974e-09
- second_out: float32 [512, 512], P(('wide', 'narrow')), may hold values from 9.313226e-13 to 1.4901162e-11
- second_up: float32 [512, 1024], P(('wide', 'narrow')), may hold values from 2.384186e-10 to 3.8146974e-09
- second_down: float32 [1024, 512], P(('wide', 'narrow')), may hold values from 2.384186e-10 to 3.8146974e-09
- second_norm: float32 [6, 512], P(None, ('wide', 'narrow')), may hold values from 2.384186e-10 to 3.8146974e-09
Outputs:
- mixed: bfloat16 [49152, 512], P(('wide', 'narrow'))
- grad_tags: float32 [49152, 512], P(('wide', 'narrow'))
- grad_image: float32 [75264, 512], P(('wide', 'narrow'))
- total_norm: float32 [], replicated
- clipped_qkv: float32 [512, 1536], P(('wide', 'narrow'))
- clipped_out: float32 [512, 512], P(('wide', 'narrow'))
- clipped_up: float32 [512, 1024], P(('wide', 'narrow'))
- clipped_down: float32 [1024, 512], P(('wide', 'narrow'))
- clipped_norm: float32 [6, 512], P(None, ('wide', 'narrow'))
- moment_qkv: float32 [512, 1536], P(('wide', 'narrow'))
- moment_out: float32 [512, 512], P(('wide', 'narrow'))
- moment_up: float32 [512, 1024], P(('wide', 'narrow'))
- moment_down: float32 [1024, 512], P(('wide', 'narrow'))
- moment_norm: float32 [6, 512], P(None, ('wide', 'narrow'))
- square_qkv: float32 [512, 1536], P(('wide', 'narrow'))
- square_out: float32 [512, 512], P(('wide', 'narrow'))
- square_up: float32 [512, 1024], P(('wide', 'narrow'))
- square_down: float32 [1024, 512], P(('wide', 'narrow'))
- square_norm: float32 [6, 512], P(None, ('wide', 'narrow'))
- updated_qkv: float32 [512, 1536], P(('wide', 'narrow'))
- updated_out: float32 [512, 512], P(('wide', 'narrow'))
- updated_up: float32 [512, 1024], P(('wide', 'narrow'))
- updated_down: float32 [1024, 512], P(('wide', 'narrow'))
- updated_norm: float32 [6, 512], P(None, ('wide', 'narrow'))
- copied_qkv: bfloat16 [512, 1536], P(('wide', 'narrow'))
- copied_out: bfloat16 [512, 512], P(('wide', 'narrow'))
- copied_up: bfloat16 [512, 1024], P(('wide', 'narrow'))
- copied_down: bfloat16 [1024, 512], P(('wide', 'narrow'))
- copied_norm: bfloat16 [6, 512], P(None, ('wide', 'narrow'))
The draws below stay inside these ranges and needn't reach their ends.
Inputs may be any that keep to these rules, and one draw needn't show every extreme that they name: `tag_counts`: at least one table has exactly 512 tags.
All inputs are finite; a program needn't handle non-finite values.
Results may differ from the reference program's by a relative error of at most 0.014.
The reference program's roundings to bfloat16 on the way count: a program that leaves them out, or rounds other values in their place, can miss the bound.
Values may be sent and summed in bfloat16 or wider, within the bound.
A program may use at most 192 MiB of HBM per device.

```python
import math
import jax
import jax.numpy as jnp
from jax import lax

D = 512
HEADS = 8
FF = 1024
TAGS = 512
IMG = 784
STEP = 10
TABLES = 96


def rising(length, low_end, high_end):
    return low_end + (high_end - low_end) * jnp.arange(length, dtype=jnp.float32) / max(length - 1, 1)


def draw_tag_counts(key, part):
    key = jax.random.fold_in(key, 1)
    first_key, second_key = jax.random.split(key)
    counts = jax.random.randint(first_key, (TABLES,), 1, TAGS + 1)
    chosen = jax.random.randint(second_key, (), 0, TABLES)
    return jnp.where(jnp.arange(TABLES) == chosen, TAGS, counts).astype(jnp.int32)


def draw_tag_inputs(key, part):
    key = jax.random.fold_in(key, 2)
    base_draw = jax.random.truncated_normal(key, -4.0, 4.0, (TABLES * TAGS, D), jnp.float32)
    column = rising(D, 1.0, 1.75)
    return (base_draw * column[None, :]).astype(jnp.bfloat16)


def draw_image_inputs(key, part):
    key = jax.random.fold_in(key, 3)
    first_key, second_key = jax.random.split(key)
    offset = 0.5 * jax.random.truncated_normal(second_key, -4.0, 4.0, (1, D), jnp.float32)
    base_draw = jax.random.truncated_normal(first_key, -4.0, 4.0, (TABLES * IMG, D), jnp.float32)
    table_scale = rising(TABLES, 1.0, 1.75)
    row_scale = jnp.repeat(table_scale, IMG)[:, None]
    return (row_scale * (base_draw + offset)).astype(jnp.bfloat16)


def draw_norm_params(key, part):
    key = jax.random.fold_in(key, 4)
    first_key, second_key = jax.random.split(key)
    rough_factor = jax.random.uniform(first_key, (6, D), jnp.float32, 0.8, 1.25)
    shifts = 0.3 * jax.random.truncated_normal(second_key, -4.0, 4.0, (6, D), jnp.float32)
    gain_rows = rising(D, 0.6, 1.4)[None, :] * rough_factor
    is_gain = (jnp.arange(6) % 2 == 0)[:, None]
    return jnp.where(is_gain, gain_rows, shifts)


def block_levels(rng, dims, cuts, low, high):
    loudness, own = 1.0, jax.random.fold_in(rng, 6)
    for dim, blocks in cuts:
        steps = jnp.exp(jax.random.uniform(jax.random.fold_in(own, dim), (blocks,), jnp.float32, low / len(cuts), high / len(cuts)))
        loudness = loudness * jnp.repeat(steps, dims[dim] // blocks).reshape([-1 if axis == dim else 1 for axis in range(len(dims))])
    return loudness


def scatter_about(stream_key, extent, deviation, most, shards=(), kind=jnp.bfloat16):
    array = jax.random.normal(stream_key, extent, jnp.float32) * deviation
    if len(shards) > 0:
        array = block_levels(stream_key, extent, shards, -0.22, 0.18) * array
    return jnp.clip(array, min=-most, max=most).astype(kind)


def setup_inputs(seed: int = 0) -> dict:
    keys = jax.random.split(jax.random.key(seed), 20)
    tag_inputs = draw_tag_inputs(jax.random.fold_in(keys[19], 71), 0)
    image_inputs = draw_image_inputs(jax.random.fold_in(keys[19], 71), 0)
    tag_counts = draw_tag_counts(jax.random.fold_in(keys[19], 71), 0)
    cotangent = scatter_about(keys[3], (TABLES * TAGS, D), 1.0, 6.0, ((0, 32),))
    weight_qkv = scatter_about(keys[4], (D, 3 * D), D ** -0.5, 0.25, ((0, 32),), jnp.float32)
    weight_out = scatter_about(keys[5], (D, D), (max(D * 3 // (IMG + TAGS), 1)) ** -0.5, 6.0, ((0, 32),), jnp.float32)
    weight_up = scatter_about(keys[6], (D, FF), D ** -0.5, 0.25, ((0, 32),), jnp.float32)
    weight_down = scatter_about(keys[7], (FF, D), FF ** -0.5, 0.1875, ((0, 32),), jnp.float32)
    norm_params = draw_norm_params(jax.random.fold_in(keys[19], 71), 0)
    first_qkv = scatter_about(keys[9], (D, 3 * D), (0.11 / (4 * D * D + 2 * D * FF) ** 0.5), 0.00048828125, ((0, 32),), jnp.float32)
    first_out = scatter_about(keys[10], (D, D), (0.11 / (16 * (4 * D * D + 2 * D * FF) ** 0.5)), 3.0517578125e-05, ((0, 32),), jnp.float32)
    first_up = scatter_about(keys[11], (D, FF), (0.11 / (4 * D * D + 2 * D * FF) ** 0.5), 0.00048828125, ((0, 32),), jnp.float32)
    first_down = scatter_about(keys[12], (FF, D), (0.11 / (4 * D * D + 2 * D * FF) ** 0.5), 0.00048828125, ((0, 32),), jnp.float32)
    first_norm = scatter_about(keys[13], (6, D), (0.11 / (4 * D * D + 2 * D * FF) ** 0.5), 0.00048828125, ((1, 32),), jnp.float32)
    second_qkv = jnp.clip(jnp.exp(math.log(3.814697446813398e-09) - 2.7725887 * jax.random.uniform(keys[14], (D, 3 * D), jnp.float32) ** block_levels(keys[14], (D, 3 * D), ((0, 32),), -0.2, 0.2)), 2.3841859042583735e-10, 3.814697446813398e-09)
    second_out = jnp.clip(jnp.exp(math.log(1.4901161901614834e-11) - 2.7725887 * jax.random.uniform(keys[15], (D, D), jnp.float32) ** block_levels(keys[15], (D, D), ((0, 32),), -0.2, 0.2)), 9.313226188509272e-13, 1.4901161901614834e-11)
    second_up = jnp.clip(jnp.exp(math.log(3.814697446813398e-09) - 2.7725887 * jax.random.uniform(keys[16], (D, FF), jnp.float32) ** block_levels(keys[16], (D, FF), ((0, 32),), -0.2, 0.2)), 2.3841859042583735e-10, 3.814697446813398e-09)
    second_down = jnp.clip(jnp.exp(math.log(3.814697446813398e-09) - 2.7725887 * jax.random.uniform(keys[17], (FF, D), jnp.float32) ** block_levels(keys[17], (FF, D), ((0, 32),), -0.2, 0.2)), 2.3841859042583735e-10, 3.814697446813398e-09)
    second_norm = jnp.clip(jnp.exp(math.log(3.814697446813398e-09) - 2.7725887 * jax.random.uniform(keys[18], (6, D), jnp.float32) ** block_levels(keys[18], (6, D), ((1, 32),), -0.2, 0.2)), 2.3841859042583735e-10, 3.814697446813398e-09)
    return {"tag_inputs": tag_inputs, "image_inputs": image_inputs, "tag_counts": tag_counts, "cotangent": cotangent, "weight_qkv": weight_qkv, "weight_out": weight_out, "weight_up": weight_up, "weight_down": weight_down, "norm_params": norm_params, "first_qkv": first_qkv, "first_out": first_out, "first_up": first_up, "first_down": first_down, "first_norm": first_norm, "second_qkv": second_qkv, "second_out": second_out, "second_up": second_up, "second_down": second_down, "second_norm": second_norm}


@jax.custom_vjp
def low(v):
    return lax.optimization_barrier(v.astype(jnp.bfloat16)).astype(jnp.float32)

@jax.custom_vjp
def low_back(v):
    return v

def low_keep(v):
    return (low(v), None)

def low_pass(kept, grad):
    return (grad,)

def back_keep(v):
    return (v, None)

def back_low(kept, grad):
    return (low(grad),)
low.defvjp(low_keep, low_pass)
low_back.defvjp(back_keep, back_low)
EPS_NORM = 1e-05
NEG_BIG = -1000000000.0
CLIP_AT = 1.0
BETA_FIRST = 0.9
BETA_SECOND = 0.999
ADAM_EPS = 1e-08
RATE_MATRIX = 0.05
RATE_OUTPUT = 1.0
RATE_NORMS = 0.5
DECAY_RATE = 0.1

def highest(left, right):
    return jnp.dot(left, right, precision=lax.Precision.HIGHEST)

def row_norm(values, gain, shift):
    centred = values - lax.optimization_barrier(jnp.mean(values, -1, keepdims=True))
    spread = lax.optimization_barrier(jnp.mean(centred * centred, -1, keepdims=True))
    return centred * lax.rsqrt(spread + EPS_NORM) * gain + shift

def allowed_keys(tag_count):
    row_ids = lax.broadcasted_iota(jnp.int32, (TAGS, IMG + TAGS), 0)
    col_ids = lax.broadcasted_iota(jnp.int32, (TAGS, IMG + TAGS), 1) - IMG
    return (col_ids < 0) | (col_ids <= row_ids) & (col_ids < tag_count)

def attend(table_item):
    queries, key_rows, value_rows, tag_count = table_item
    head_size = D // HEADS
    queries = queries.reshape(TAGS, HEADS, head_size)
    key_rows = key_rows.reshape(IMG + TAGS, HEADS, head_size)
    value_rows = value_rows.reshape(IMG + TAGS, HEADS, head_size)
    raw_scores = jnp.einsum('qhd,khd->hqk', queries, key_rows, precision=lax.Precision.HIGHEST) * (1.0 / math.sqrt(head_size))
    raw_scores = low_back(raw_scores)
    raw_scores = jnp.where(allowed_keys(tag_count)[None], raw_scores, NEG_BIG)
    row_top = lax.optimization_barrier(jnp.max(raw_scores, -1, keepdims=True))
    exponent = jnp.exp(raw_scores - row_top)
    soft_weights = exponent / lax.optimization_barrier(jnp.sum(exponent, -1, keepdims=True))
    mixed_heads = jnp.einsum('hqk,khd->qhd', low(soft_weights), value_rows, precision=lax.Precision.HIGHEST)
    return mixed_heads.reshape(TAGS, D)

def forward(tag_values, image_values, low_qkv, low_out, low_up, low_down, low_norm, tag_counts):
    centred = image_values - lax.optimization_barrier(jnp.mean(image_values, 0))
    spread = lax.optimization_barrier(jnp.mean(centred * centred, 0))
    img_normed = centred * lax.rsqrt(spread + EPS_NORM)
    img_low = low(img_normed * low_norm[4] + low_norm[5])
    kv_image = low_back(low(highest(img_low, low_qkv[:, D:])))
    qkv_tags = low_back(low(highest(tag_values, low_qkv)))
    queries = qkv_tags[:, :D].reshape(TABLES, TAGS, D)
    key_rows = jnp.concatenate([kv_image[:, :D].reshape(TABLES, IMG, D), qkv_tags[:, D:2 * D].reshape(TABLES, TAGS, D)], 1)
    value_rows = jnp.concatenate([kv_image[:, D:].reshape(TABLES, IMG, D), qkv_tags[:, 2 * D:].reshape(TABLES, TAGS, D)], 1)
    attended = lax.map(jax.checkpoint(attend), (queries, key_rows, value_rows, tag_counts))
    attended = low_back(low(attended.reshape(TABLES * TAGS, D)))
    hidden_pre = tag_values + low_back(highest(attended, low_out))
    hidden = row_norm(hidden_pre, low_norm[0], low_norm[1])
    pre_act = low_back(highest(low(hidden), low_up))
    activated = low(jax.nn.gelu(pre_act, approximate=True))
    resid = hidden + low_back(highest(activated, low_down))
    return row_norm(resid, low_norm[2], low_norm[3])

def reference(tag_inputs, image_inputs, tag_counts, cotangent, weight_qkv, weight_out, weight_up, weight_down, norm_params, first_qkv, first_out, first_up, first_down, first_norm, second_qkv, second_out, second_up, second_down, second_norm):
    masters = (weight_qkv, weight_out, weight_up, weight_down, norm_params)
    firsts = (first_qkv, first_out, first_up, first_down, first_norm)
    seconds = (second_qkv, second_out, second_up, second_down, second_norm)
    rates = (RATE_MATRIX, RATE_OUTPUT, RATE_MATRIX, RATE_MATRIX)
    copies = tuple((low(master) for master in masters))
    tag_values = tag_inputs.astype(jnp.float32)
    image_values = image_inputs.astype(jnp.float32)

    def closed(tag_part, image_part, low_qkv, low_out, low_up, low_down, low_norm):
        return forward(tag_part, image_part, low_qkv, low_out, low_up, low_down, low_norm, tag_counts)
    output, pullback = jax.vjp(closed, tag_values, image_values, *copies)
    valid = (lax.broadcasted_iota(jnp.int32, (TABLES, TAGS), 1) < tag_counts[:, None]).reshape(TABLES * TAGS, 1)
    grad_out = jnp.where(valid, cotangent.astype(jnp.float32), 0.0)
    cotangents = pullback(grad_out)
    grad_tags = cotangents[0]
    grad_image = cotangents[1]
    gradients = cotangents[2:]
    total_norm = jnp.sqrt(sum((jnp.sum(gradient * gradient) for gradient in gradients)))
    factor = CLIP_AT / jnp.maximum(total_norm, CLIP_AT)
    clipped, moments, squares, updated, copied = ([], [], [], [], [])
    for position in range(5):
        master = masters[position]
        clip_grad = factor * gradients[position]
        moment = BETA_FIRST * firsts[position] + (1.0 - BETA_FIRST) * clip_grad
        square = BETA_SECOND * seconds[position] + (1.0 - BETA_SECOND) * clip_grad * clip_grad
        direction = moment / (1.0 - BETA_FIRST ** STEP) / (jnp.sqrt(square / (1.0 - BETA_SECOND ** STEP)) + ADAM_EPS)
        if position < 4:
            new_weight = master - rates[position] * (direction + DECAY_RATE * master)
        else:
            new_weight = master - RATE_NORMS * direction
        clipped.append(clip_grad)
        moments.append(moment)
        squares.append(square)
        updated.append(new_weight)
        copied.append(new_weight.astype(jnp.bfloat16))
    return (output.astype(jnp.bfloat16), grad_tags, grad_image, total_norm, clipped[0], clipped[1], clipped[2], clipped[3], clipped[4], moments[0], moments[1], moments[2], moments[3], moments[4], squares[0], squares[1], squares[2], squares[3], squares[4], updated[0], updated[1], updated[2], updated[3], updated[4], copied[0], copied[1], copied[2], copied[3], copied[4])
```

```python
import functools
import math

import jax
import jax.numpy as jnp
from jax import lax
from jax.experimental import pallas as pl
from jax.experimental.pallas import tpu as pltpu
from jax.sharding import PartitionSpec as P

f32 = jnp.float32
bf = jnp.bfloat16
MESH = pl.DeviceIdType.MESH
HEADS = 8
STEP = 10
EPS = 1e-05
NEG = -1000000000.0
CLIP_AT = 1.0
BETA_FIRST = 0.9
BETA_SECOND = 0.999
ADAM_EPS = 1e-08
RATE_MATRIX = 0.05
RATE_OUTPUT = 1.0
RATE_NORMS = 0.5
DECAY_RATE = 0.1
GC = math.sqrt(2 / math.pi)
GA = 0.044715
AXES = ("wide", "narrow")
VM = pl.BlockSpec(memory_space=pltpu.VMEM)


def dg(a, b, ca, cb):
    return lax.dot_general(a, b, (((ca,), (cb,)), ((), ())), preferred_element_type=f32)


class Place:
    def __init__(self):
        self.w = lax.axis_index("wide")
        self.c = lax.axis_index("narrow")
        self.x = lax.rem(self.w, 2)
        self.y = lax.rem(self.w // 2, 2)
        self.z = self.w // 4
        self.d = self.w * 2 + self.c
        self.to_x = (self.w + 1 - 2 * self.x, self.c)
        self.to_y = (self.w + 2 - 4 * self.y, self.c)
        self.sib = (self.w, 1 - self.c)

    def to_z(self, k):
        return (lax.rem(self.w + 4 * k, 16), self.c)

    def peer(self, k):
        d = lax.rem(self.d + k, 32)
        return (d // 2, lax.rem(d, 2))


def greet_all(me):
    bar = pltpu.get_barrier_semaphore()
    for k in range(1, 32):
        pl.semaphore_signal(bar, inc=1, device_id=me.peer(k), device_id_type=MESH)
    pl.semaphore_wait(bar, 31)


def remote(src, dst, ss, rs, dev):
    return pltpu.make_async_remote_copy(
        src_ref=src, dst_ref=dst, send_sem=ss, recv_sem=rs, device_id=dev, device_id_type=MESH
    )


def push_all(me, src, dst, ss, rs):
    cps = []
    for k in range(1, 32):
        cp = remote(src, dst.at[me.d], ss.at[k], rs.at[k], me.peer(k))
        cp.start()
        cps.append(cp)
    return cps


class Gather:
    SLOTS = 35

    def __init__(self, me, g, ss, rs, split):
        self.me, self.g, self.ss, self.rs = me, g, ss, rs
        n = g.shape[-1]
        self.h = n // 2 if split else n
        self.split = split
        self.sent = []

    def blk(self, kz, pos):
        me = self.me
        z = lax.rem(me.z + 4 - kz, 4)
        y = me.y if pos in (0, 1) else 1 - me.y
        x = me.x if pos in (0, 2) else 1 - me.x
        return z, y, x

    def ref(self, kz, pos, lanes=None, c=None):
        z, y, x = self.blk(kz, pos)
        c = self.me.c if c is None else c
        if lanes is None:
            return self.g.at[z, y, x, c]
        return self.g.at[z, y, x, c, :, lanes]

    def go(self, ref, slot, dev):
        cp = remote(ref, ref, self.ss.at[slot], self.rs.at[slot], dev)
        cp.start()
        self.sent.append(cp)

    def got(self, ref, slot):
        remote(ref, ref, self.ss.at[slot], self.rs.at[slot], self.me.sib).wait_recv()

    def start(self):
        me = self.me
        own = self.ref(0, 0)
        for k in (1, 2, 3):
            self.go(own, k - 1, me.to_z(k))
        self.go(own, 3, me.to_x)
        self.go(own, 7, me.to_y)
        self.go(own, 19, me.sib)

    def column(self):
        me = self.me
        for k in (1, 3, 2):
            r = self.ref(k, 0)
            self.got(r, k - 1)
            self.go(r, 3 + k, me.to_x)
            self.go(r, 7 + k, me.to_y)
            self.go(r, 19 + k, me.sib)

    def plane(self):
        me = self.me
        for k in (0, 1, 3, 2):
            r = self.ref(k, 1)
            self.got(r, 3 + k)
            self.go(self.ref(k, 1, pl.ds(0, self.h)), 11 + k, me.to_y)
            self.go(r, 23 + k, me.sib)
            r = self.ref(k, 2)
            self.got(r, 7 + k)
            if self.split:
                self.go(self.ref(k, 2, pl.ds(self.h, self.h)), 15 + k, me.to_x)
            self.go(r, 27 + k, me.sib)

    def corner(self):
        me = self.me
        for k in (0, 1, 3, 2):
            self.got(self.ref(k, 3, pl.ds(0, self.h)), 11 + k)
            if self.split:
                self.got(self.ref(k, 3, pl.ds(self.h, self.h)), 15 + k)
            self.go(self.ref(k, 3), 31 + k, me.sib)

    def finish(self):
        for pos in range(4):
            for k in range(4):
                self.got(self.ref(k, pos, c=1 - self.me.c), 19 + 4 * pos + k)
        for cp in self.sent:
            cp.wait_send()


def gather_kernel(
    img_ref, wqkv_ref, wout_ref, wup_ref, wdn_ref, norm_ref,
    gq, gr, gd, stats_ref, gains_ref,
    gn, st, sq_s, sq_r, sr_s, sr_r, sd_s, sd_r, sn_s, sn_r, st_s, st_r,
):
    me = Place()
    D = wqkv_ref.shape[1] // 3
    F = wup_ref.shape[1]
    own = (me.z, me.y, me.x, me.c)
    gq[own] = wqkv_ref[...].astype(bf)
    gr[own + (slice(None), pl.ds(0, D))] = wout_ref[...].astype(bf)
    gr[own + (slice(None), pl.ds(D, F))] = wup_ref[...].astype(bf)
    gd[own] = wdn_ref[...].astype(bf)
    lane = lax.broadcasted_iota(jnp.int32, (16, 128), 1)
    unit = lax.broadcasted_iota(jnp.int32, (16, 128), 0)
    at = (lane == unit + 16 * lax.rem(me.d, 8)).astype(bf)
    tile = dg(norm_ref[...].astype(bf), at, 1, 0)
    gn[own] = jnp.concatenate([tile, jnp.zeros((10, 128), f32)], 0).astype(bf)
    greet_all(me)
    q = Gather(me, gq, sq_s, sq_r, True)
    n = Gather(me, gn, sn_s, sn_r, False)
    r = Gather(me, gr, sr_s, sr_r, True)
    dn = Gather(me, gd, sd_s, sd_r, True)
    q.start()
    n.start()
    rows = img_ref.shape[0]
    step = rows // 3
    total = jnp.zeros((1, D), f32)
    for i in range(3):
        total += jnp.sum(img_ref[i * step : (i + 1) * step, :].astype(f32), 0, keepdims=True)
    mean_d = total / rows
    m2 = jnp.zeros((1, D), f32)
    for i in range(3):
        cen = img_ref[i * step : (i + 1) * step, :].astype(f32) - mean_d
        m2 += jnp.sum(cen * cen, 0, keepdims=True)
    mine = jnp.concatenate(
        [mean_d[:, g * 128 : (g + 1) * 128] for g in range(4)] + [m2[:, g * 128 : (g + 1) * 128] for g in range(4)], 0
    )
    st[me.d] = mine
    cps = push_all(me, st.at[me.d], st, st_s, st_r)
    q.column()
    n.column()
    r.start()
    dn.start()
    q.plane()
    n.plane()
    q.corner()
    n.corner()
    r.column()
    dn.column()
    r.plane()
    dn.plane()
    r.corner()
    dn.corner()
    for k in range(1, 32):
        cps[k - 1].wait_send()
        src = lax.rem(me.d + 32 - k, 32)
        remote(st.at[src], st.at[src], st_s.at[k], st_r.at[k], me.sib).wait_recv()
    mean = jnp.sum(st[:, 0:4, :], 0) / 32
    off = st[:, 0:4, :] - mean[None]
    spread = (jnp.sum(st[:, 4:8, :], 0) + rows * jnp.sum(off * off, 0)) / (rows * 32)
    inv = lax.rsqrt(spread + EPS)
    for g in range(4):
        stats_ref[0:1, g * 128 : (g + 1) * 128] = mean[g : g + 1, :]
        stats_ref[1:2, g * 128 : (g + 1) * 128] = inv[g : g + 1, :]
    for part in (q, n, r, dn):
        part.finish()
    for z in range(4):
        acc = jnp.zeros((16, 128), f32)
        for y in range(2):
            for x in range(2):
                for c in range(2):
                    acc += gn[z, y, x, c].astype(f32)
        gains_ref[:, z * 128 : (z + 1) * 128] = acc[0:8, :]


def gather(img, wqkv, wout, wup, wdn, norm):
    D = img.shape[1]
    F = wup.shape[1]
    R, RD = wqkv.shape[0], wdn.shape[0]
    dims = (4, 2, 2, 2)
    dma = pltpu.SemaphoreType.DMA
    S = Gather.SLOTS
    outs = pl.pallas_call(
        gather_kernel,
        out_shape=[
            jax.ShapeDtypeStruct(dims + (R, 3 * D), bf),
            jax.ShapeDtypeStruct(dims + (R, D + F), bf),
            jax.ShapeDtypeStruct(dims + (RD, D), bf),
            jax.ShapeDtypeStruct((2, D), f32),
            jax.ShapeDtypeStruct((8, D), f32),
        ],
        in_specs=[VM] * 6,
        out_specs=[VM] * 5,
        scratch_shapes=[pltpu.VMEM(dims + (16, 128), bf), pltpu.VMEM((32, 8, 128), f32)]
        + [dma((S,))] * 8
        + [dma((32,))] * 2,
        compiler_params=pltpu.CompilerParams(collective_id=0, has_side_effects=True, vmem_limit_bytes=40 * 2**20),
        name="gather",
    )(img, wqkv, wout, wup, wdn, norm)
    gq, gr, gd, stats, gains = outs
    return gq.reshape(D, 3 * D), gr.reshape(D, D + F), gd.reshape(F, D), stats, gains


class Scatter:
    SLOTS = 8

    def __init__(self, me, g, out, bufs, ss, rs):
        self.me, self.g, self.out, self.ss, self.rs = me, g, out, ss, rs
        self.r0, self.s0, self.r1a, self.r1b, self.s1a, self.s1b, self.r2a, self.r2b, self.s2, self.r3 = bufs
        self.h = g.shape[-1] // 2
        self.sent = []

    @staticmethod
    def bufs(R, N):
        h = N // 2
        v = lambda *s: pltpu.VMEM(s, bf)
        return [
            v(4, 2, 2, R, N), v(4, 2, 2, R, N), v(4, 2, R, h), v(4, 2, R, h), v(4, 2, R, h), v(4, 2, R, h),
            v(4, R, h), v(4, R, h), v(4, R, N), v(3, R, N),
        ]

    def go(self, src, dst, slot, dev):
        cp = remote(src, dst, self.ss.at[slot], self.rs.at[slot], dev)
        cp.start()
        self.sent.append(cp)

    def got(self, dst, slot):
        remote(dst, dst, self.ss.at[slot], self.rs.at[slot], self.me.sib).wait_recv()

    def core(self):
        me = self.me
        self.go(self.g.at[:, :, :, 1 - me.c], self.r0, 0, me.sib)

    def plane1(self):
        me, h = self.me, self.h
        self.got(self.r0, 0)

        def add(i, _):
            k = (i // 4, lax.rem(i // 2, 2), lax.rem(i, 2))
            self.s0[k] = (self.g[k + (me.c,)].astype(f32) + self.r0[k].astype(f32)).astype(bf)
            return 0

        lax.fori_loop(0, 16, add, 0)
        self.go(self.s0.at[:, :, 1 - me.x, :, pl.ds(0, h)], self.r1a, 1, me.to_x)
        self.go(self.s0.at[:, 1 - me.y, :, :, pl.ds(h, h)], self.r1b, 2, me.to_y)

    def plane2(self):
        me, h = self.me, self.h
        self.got(self.r1a, 1)
        self.got(self.r1b, 2)

        def add(i, _):
            z, k = i // 2, lax.rem(i, 2)
            a = self.s0[z, k, me.x, :, pl.ds(0, h)].astype(f32) + self.r1a[z, k].astype(f32)
            self.s1a[z, k] = a.astype(bf)
            b = self.s0[z, me.y, k, :, pl.ds(h, h)].astype(f32) + self.r1b[z, k].astype(f32)
            self.s1b[z, k] = b.astype(bf)
            return 0

        lax.fori_loop(0, 8, add, 0)
        self.go(self.s1a.at[:, 1 - me.y], self.r2a, 3, me.to_y)
        self.go(self.s1b.at[:, 1 - me.x], self.r2b, 4, me.to_x)

    def column(self):
        me, h = self.me, self.h
        self.got(self.r2a, 3)
        self.got(self.r2b, 4)
        for z in range(4):
            self.s2[z, :, 0:h] = (self.s1a[z, me.y].astype(f32) + self.r2a[z].astype(f32)).astype(bf)
            self.s2[z, :, h:] = (self.s1b[z, me.x].astype(f32) + self.r2b[z].astype(f32)).astype(bf)
        for k in (2, 1, 3):
            self.go(self.s2.at[lax.rem(me.z + k, 4)], self.r3.at[k - 1], 4 + k, me.to_z(k))

    def finish(self):
        me = self.me
        acc = self.s2[me.z].astype(f32)
        for k in (1, 2, 3):
            self.got(self.r3.at[k - 1], 4 + k)
            acc += self.r3[k - 1].astype(f32)
        self.out[...] = acc
        for cp in self.sent:
            cp.wait_send()
        return jnp.sum(acc * acc)


def scatter_kernel(gq, gr, gd, terms, bnsum, oq, orr, od, small, nsq, *rest):
    bq, br, bd = rest[0:10], rest[10:20], rest[20:30]
    tb, nb, q_s, q_r, r_s, r_r, d_s, d_r, t_s, t_r, n_s, n_r = rest[30:]
    me = Place()
    D = terms.shape[1]
    tb[0, 0:4, :] = terms[...]
    tb[0, 4:6, :] = bnsum[...]
    tb[0, 6:8, :] = jnp.zeros((2, D), f32)
    greet_all(me)
    d = Scatter(me, gd, od, bd, d_s, d_r)
    r = Scatter(me, gr, orr, br, r_s, r_r)
    q = Scatter(me, gq, oq, bq, q_s, q_r)
    tsent = []

    def tgo(src, dst, slot, dev):
        cp = remote(tb.at[src], tb.at[dst], t_s.at[slot], t_r.at[slot], dev)
        cp.start()
        tsent.append(cp)

    def tgot(dst, slot):
        remote(tb.at[dst], tb.at[dst], t_s.at[slot], t_r.at[slot], me.sib).wait_recv()

    tgo(0, 1, 0, me.sib)
    for a in (d, r, q):
        a.core()
    tgot(1, 0)
    tb[2] = tb[0] + tb[1]
    tgo(2, 3, 1, me.to_x)
    d.plane1()
    r.plane1()
    tgot(3, 1)
    tb[4] = tb[2] + tb[3]
    tgo(4, 5, 2, me.to_y)
    d.plane2()
    q.plane1()
    tgot(5, 2)
    tb[6 + me.z] = tb[4] + tb[5]
    for k in (1, 2, 3):
        tgo(6 + me.z, 6 + me.z, 2 + k, me.to_z(k))
    d.column()
    r.plane2()
    q.plane2()
    r.column()
    q.column()
    sq = d.finish()
    for k in (1, 2, 3):
        tgot(6 + lax.rem(me.z + 4 - k, 4), 2 + k)
    tot = (tb[6] + tb[7]) + (tb[8] + tb[9])
    small[...] = tot
    sq += r.finish()
    sq += q.finish()
    for cp in tsent:
        cp.wait_send()
    nb[me.d] = jnp.full((8, 128), sq, f32)
    cps = push_all(me, nb.at[me.d], nb, n_s, n_r)
    for k in range(1, 32):
        cps[k - 1].wait_send()
        src = lax.rem(me.d + 32 - k, 32)
        remote(nb.at[src], nb.at[src], n_s.at[k], n_r.at[k], me.sib).wait_recv()
    nsq[...] = jnp.sum(nb[...], 0) + jnp.sum(tot * tot)


def scatter(gq, gr, gd, terms, bnsum):
    D, F = terms.shape[1], gd.shape[0]
    R, RD = D // 32, F // 32
    dims = (4, 2, 2, 2)
    dma = pltpu.SemaphoreType.DMA
    return pl.pallas_call(
        scatter_kernel,
        out_shape=[
            jax.ShapeDtypeStruct((R, 3 * D), f32),
            jax.ShapeDtypeStruct((R, D + F), f32),
            jax.ShapeDtypeStruct((RD, D), f32),
            jax.ShapeDtypeStruct((8, D), f32),
            jax.ShapeDtypeStruct((8, 128), f32),
        ],
        in_specs=[VM] * 5,
        out_specs=[VM] * 5,
        scratch_shapes=Scatter.bufs(R, 3 * D)
        + Scatter.bufs(R, D + F)
        + Scatter.bufs(RD, D)
        + [pltpu.VMEM((10, 8, D), f32), pltpu.VMEM((32, 8, 128), f32)]
        + [dma((Scatter.SLOTS,))] * 6
        + [dma((6,))] * 2
        + [dma((32,))] * 2,
        compiler_params=pltpu.CompilerParams(collective_id=1, has_side_effects=True, vmem_limit_bytes=40 * 2**20),
        name="scatter",
    )(
        gq.reshape(dims + (R, 3 * D)), gr.reshape(dims + (R, D + F)), gd.reshape(dims + (RD, D)), terms, bnsum
    )


def k2_body(counts, tag_ref, img_ref, cot_ref, stats_ref, wqkv_ref, wr_ref, wdn_ref, gains_ref,
            mixed_ref, gtags_ref, gz_ref, gqkv_ref, gr_ref, gdn_ref, terms_ref, bnsum_ref,
            imglow_s, kall, vall, kT, vT, q_s, qT, bias_s, s_s, e_s, attT, oT_s, rl_s,
            hidlow_s, act_s, rlow_s, plow_s, hplow_s, ghp_s, dqkv_s, dkvi_s, dqT_s, dO_s, dOT_s, del_s,
            aqkv, aout, aup, adn):
    t = pl.program_id(0)
    T, D = tag_ref.shape
    I = img_ref.shape[0]
    NK = T + I
    hd = D // HEADS
    F = wdn_ref.shape[0]
    wout_ref = wr_ref.at[:, 0:D]
    wup_ref = wr_ref.at[:, D:D + F]
    count = counts[t]

    @pl.when(t == 0)
    def _():
        aqkv[...] = jnp.zeros_like(aqkv); aout[...] = jnp.zeros_like(aout)
        aup[...] = jnp.zeros_like(aup); adn[...] = jnp.zeros_like(adn)
        terms_ref[...] = jnp.zeros_like(terms_ref); bnsum_ref[...] = jnp.zeros_like(bnsum_ref)

    mean = stats_ref[0:1, :]; inv = stats_ref[1:2, :]
    g1 = gains_ref[0:1, :]; b1 = gains_ref[1:2, :]; g2 = gains_ref[2:3, :]; b2 = gains_ref[3:4, :]
    gb = gains_ref[4:5, :]; bb = gains_ref[5:6, :]

    x = tag_ref[...]
    for r0, rl in ((0, 256), (256, 256), (512, I - 512)):
        img_hat = (img_ref[r0:r0 + rl, :].astype(f32) - mean) * inv
        imglow_s[r0:r0 + rl, :] = (img_hat * gb + bb).astype(bf)
    for r0 in range(0, T, 256):
        q = dg(tag_ref[r0:r0 + 256, :], wqkv_ref[:, 0:D], 1, 0).astype(bf) * bf(1.0 / math.sqrt(hd))
        q_s[r0:r0 + 256, :] = q
        qT[:, r0:r0 + 256] = q.T
    for j,(dst, dstT) in enumerate(((kall, kT), (vall, vT))):
        w = wqkv_ref[:, (j + 1) * D:(j + 2) * D]
        for r0 in range(0, T, 256):
            a = dg(tag_ref[r0:r0 + 256, :], w, 1, 0).astype(bf)
            dst[r0:r0 + 256, :] = a
            dstT[:, r0:r0 + 256] = a.T
        for r0, rl in ((0, 256), (256, 256), (512, I - 512)):
            a = dg(imglow_s[r0:r0 + rl, :], w, 1, 0).astype(bf)
            dst[T + r0:T + r0 + rl, :] = a
            dstT[:, T + r0:T + r0 + rl] = a.T
    ji = lax.broadcasted_iota(jnp.int32, (T, T), 0); ii = lax.broadcasted_iota(jnp.int32, (T, T), 1)
    bias_s[...] = jnp.where((ji <= ii) & (ji < count), 3e38, NEG)

    chunks = [(0, 256, 0), (256, 256, 256), (512, 256, 0), (768, 256, 0), (1024, NK - 1024, 0)]
    row64 = lax.broadcasted_iota(jnp.int32, (2 * hd, 1), 0)
    lane64 = lax.broadcasted_iota(jnp.int32, (1, 2 * hd), 1)
    def own_rows(a, h):
        keep = (row64 < hd) if h % 2 == 0 else (row64 >= hd)
        return jnp.where(keep, a, jnp.zeros_like(a))
    def own_lanes(a, h):
        keep = (lane64 < hd) if h % 2 == 0 else (lane64 >= hd)
        return jnp.where(keep, a, jnp.zeros_like(a))
    def pr(h): return slice(h // 2 * 2 * hd, (h // 2 + 1) * 2 * hd)

    def fullq(a, q0, fill):
        if q0 == 0: return a
        return jnp.concatenate([jnp.full((a.shape[0], q0), fill, a.dtype), a], 1)

    def A(h, c, qz):
        k0, kl, q0 = chunks[c]
        s = dg(kall[k0:k0 + kl, pr(h)], qz[:, q0:], 1, 0)
        if k0 < T:
            s = jnp.minimum(s, bias_s[k0:k0 + kl, q0:])
        s_s[h % 2, k0:k0 + kl, q0:] = s
        return fullq(jnp.max(s, 0, keepdims=True), q0, NEG)
    def B(h, c, m):
        k0, kl, q0 = chunks[c]
        e = jnp.exp(s_s[h % 2, k0:k0 + kl, q0:] - m[:, q0:])
        l = jnp.sum(e, 0, keepdims=True)
        e = e.astype(bf)
        e_s[h, k0:k0 + kl, q0:] = e
        o = dg(vT[h * hd:(h + 1) * hd, k0:k0 + kl], e, 1, 0)
        return fullq(o, q0, 0.0), fullq(l, q0, 0.0)
    nc = len(chunks)
    def fwd_pair(p, _):
        ps = pl.ds(pl.multiple_of(p * 2 * hd, 2 * hd), 2 * hd)
        qzs = [own_rows(qT[ps, :], b) for b in range(2)]
        def A(b, c):
            k0, kl, q0 = chunks[c]
            s = dg(kall[k0:k0 + kl, ps], qzs[b][:, q0:], 1, 0)
            if k0 < T:
                s = jnp.minimum(s, bias_s[k0:k0 + kl, q0:])
            s_s[b, k0:k0 + kl, q0:] = s
            return fullq(jnp.max(s, 0, keepdims=True), q0, NEG)
        def B(b, c, m):
            k0, kl, q0 = chunks[c]
            e = jnp.exp(s_s[b, k0:k0 + kl, q0:] - m[:, q0:])
            l = jnp.sum(e, 0, keepdims=True)
            e = e.astype(bf)
            e_s[2 * p + b, k0:k0 + kl, q0:] = e
            o = dg(vT[pl.ds(pl.multiple_of(p * 2 * hd + b * hd, hd), hd), k0:k0 + kl], e, 1, 0)
            return fullq(o, q0, 0.0), fullq(l, q0, 0.0)
        def done(b, o, l):
            rl = 1.0 / l
            o = o * rl
            hs = pl.ds(pl.multiple_of(p * 2 * hd + b * hd, hd), hd)
            oT_s[hs, :] = o
            attT[hs, :] = o.astype(bf)
            rl_s[2 * p + b] = rl
        m0 = None
        for c in range(nc):
            mc = A(0, c); m0 = mc if m0 is None else jnp.maximum(m0, mc)
        m1 = None; o = None
        for c in range(nc):
            mc = A(1, c); m1 = mc if m1 is None else jnp.maximum(m1, mc)
            oc, lc = B(0, c, m0)
            o, l = (oc, lc) if o is None else (o + oc, l + lc)
        done(0, o, l)
        o = None
        for c in range(nc):
            oc, lc = B(1, c, m1)
            o, l = (oc, lc) if o is None else (o + oc, l + lc)
        done(1, o, l)
        return 0
    lax.fori_loop(0, HEADS // 2, fwd_pair, 0)

    tg2 = jnp.zeros((1, D), f32); tb2 = tg2; tg1 = tg2; tb1 = tg2
    RC = 128
    def rows_part(i, tg):
        tg1, tb1, tg2, tb2 = tg
        r0 = pl.multiple_of(i * RC, RC)
        rs = pl.ds(r0, RC)
        hp = tag_ref[rs, :].astype(f32) + dg(attT[:, rs], wout_ref[...], 0, 0)
        c = hp - jnp.mean(hp, -1, keepdims=True)
        inv1 = lax.rsqrt(jnp.mean(c * c, -1, keepdims=True) + EPS)
        hat1 = c * inv1
        hidden = hat1 * g1 + b1
        hl = hidden.astype(bf)
        hidlow_s[rs, :] = hl
        pre = dg(hl, wup_ref[...], 1, 0)
        p2 = pre * pre
        th = jnp.tanh(GC * (pre + GA * (p2 * pre)))
        act = (0.5 * pre * (1.0 + th)).astype(bf)
        act_s[rs, :] = act
        gp = 0.5 * (1.0 + th) + 0.5 * pre * (1.0 - th * th) * (GC * (1.0 + 3 * GA * p2))
        resid = hidden + dg(act, wdn_ref[...], 1, 0)
        c = resid - jnp.mean(resid, -1, keepdims=True)
        inv2 = lax.rsqrt(jnp.mean(c * c, -1, keepdims=True) + EPS)
        hat2 = c * inv2
        mixed_ref[rs, :] = (hat2 * g2 + b2).astype(bf)
        rows = r0 + lax.broadcasted_iota(jnp.int32, (RC, 1), 0)
        go = jnp.where(rows < count, cot_ref[rs, :].astype(f32), 0.0)
        tg2 += jnp.sum(go * hat2, 0, keepdims=True); tb2 += jnp.sum(go, 0, keepdims=True)
        s = go * g2
        gr = inv2 * (s - jnp.mean(s, -1, keepdims=True) - hat2 * jnp.mean(s * hat2, -1, keepdims=True))
        rlow = gr.astype(bf)
        rlow_s[rs, :] = rlow
        plow = (dg(rlow, wdn_ref[...], 1, 1) * gp).astype(bf)
        plow_s[rs, :] = plow
        gh = gr + dg(plow, wup_ref[...], 1, 1)
        tg1 += jnp.sum(gh * hat1, 0, keepdims=True); tb1 += jnp.sum(gh, 0, keepdims=True)
        s = gh * g1
        ghp = inv1 * (s - jnp.mean(s, -1, keepdims=True) - hat1 * jnp.mean(s * hat1, -1, keepdims=True))
        ghp_s[rs, :] = ghp
        hpl = ghp.astype(bf)
        hplow_s[rs, :] = hpl
        dO = dg(hpl, wout_ref[...], 1, 1).astype(bf)
        dOT_s[:, rs] = dO.T
        return tg1, tb1, tg2, tb2
    tg1, tb1, tg2, tb2 = lax.fori_loop(0, T // RC, rows_part, (tg1, tb1, tg2, tb2))
    terms_ref[0:1, :] += tg1; terms_ref[1:2, :] += tb1; terms_ref[2:3, :] += tg2; terms_ref[3:4, :] += tb2
    for h in range(HEADS):
        hs = slice(h * hd, (h + 1) * hd)
        d = dOT_s[hs, :].astype(f32) * rl_s[h]
        dOT_s[hs, :] = d.astype(bf)
        del_s[h] = jnp.sum(d * oT_s[hs, :], 0, keepdims=True)
    dO_s[...] = dOT_s[...].T

    for r0 in range(0, D, 256):
        aout[r0:r0 + 256, :] += dg(attT[r0:r0 + 256, :], hplow_s[...], 1, 0)
        for c0 in range(0, F, 512):
            aup[r0:r0 + 256, c0:c0 + 512] += dg(hidlow_s[:, r0:r0 + 256], plow_s[:, c0:c0 + 512], 0, 0)
    for r0 in range(0, F, 256):
        adn[r0:r0 + 256, :] += dg(act_s[:, r0:r0 + 256], rlow_s[...], 0, 0)

    def bwd_pair(p, _):
        p128 = pl.multiple_of(p * 2 * hd, 2 * hd)
        ps = pl.ds(p128, 2 * hd)
        dq = [None, None]
        ops = []
        for b in range(2):
            ops.append((own_rows(dOT_s[ps, :], b), own_lanes(dO_s[:, ps], b), own_lanes(q_s[:, ps], b)))
        for c in range(nc):
            k0, kl, q0 = chunks[c]
            ks = slice(k0, k0 + kl)
            dk = None
            for b in range(2):
                h = 2 * p + b
                hs = pl.ds(pl.multiple_of(p * 2 * hd + b * hd, hd), hd)
                dOz, dOl, ql = ops[b]
                dp = dg(vall[ks, ps], dOz[:, q0:], 1, 0)
                e = e_s[h, ks, q0:]
                ds = (e.astype(f32) * (dp - del_s[h][:, q0:])).astype(bf)
                dvc = dg(e, dOl[q0:, :], 1, 0)
                dkc = dg(ds, ql[q0:, :], 1, 0)
                dqc = fullq(dg(kT[hs, ks], ds, 1, 0), q0, 0.0)
                dk, dv = (dkc, dvc) if dk is None else (dk + dkc, dv + dvc)
                dq[b] = dqc if dq[b] is None else dq[b] + dqc
            kc = pl.ds(pl.multiple_of(D + p128, 128), 2 * hd); vc = pl.ds(pl.multiple_of(2 * D + p128, 128), 2 * hd)
            if k0 < T:
                dqkv_s[ks, kc] = dk.astype(bf)
                dqkv_s[ks, vc] = dv.astype(bf)
            else:
                si = slice(k0 - T, k0 - T + kl)
                dkvi_s[si, ps] = dk.astype(bf)
                dkvi_s[si, kc] = dv.astype(bf)
        for b in range(2):
            hs = pl.ds(pl.multiple_of(p * 2 * hd + b * hd, hd), hd)
            dqT_s[hs, :] = (dq[b] * (1.0 / math.sqrt(hd))).astype(bf)
        return 0
    lax.fori_loop(0, HEADS // 2, bwd_pair, 0)
    dqkv_s[:, 0:D] = dqT_s[...].T

    for r0 in range(0, T, 256):
        gtags_ref[r0:r0 + 256, :] = ghp_s[r0:r0 + 256, :] + dg(dqkv_s[r0:r0 + 256, :], wqkv_ref[...], 1, 1)
    sg = jnp.zeros((1, D), f32); sb = sg
    for r0, rl in ((0, 256), (256, 256), (512, I - 512)):
        rs = slice(r0, r0 + rl)
        gz = dg(dkvi_s[rs, :], wqkv_ref[:, D:], 1, 1)
        gz_ref[rs, :] = gz
        hat = (img_ref[rs, :].astype(f32) - mean) * inv
        sg += jnp.sum(gz * hat, 0, keepdims=True); sb += jnp.sum(gz, 0, keepdims=True)
    bnsum_ref[0:1, :] += sg; bnsum_ref[1:2, :] += sb
    for r0 in range(0, D, 256):
        rs = slice(r0, r0 + 256)
        aqkv[rs, 0:D] += dg(tag_ref[:, rs], dqkv_s[:, 0:D], 0, 0)
        for c0 in range(D, 3 * D, 512):
            aqkv[rs, c0:c0 + 512] += dg(tag_ref[:, rs], dqkv_s[:, c0:c0 + 512], 0, 0) + dg(imglow_s[:, rs], dkvi_s[:, c0 - D:c0 - D + 512], 0, 0)

    @pl.when(t == pl.num_programs(0) - 1)
    def _():
        gqkv_ref[...] = aqkv[...].astype(bf); gr_ref[:, 0:D] = aout[...].astype(bf)
        gr_ref[:, D:D + F] = aup[...].astype(bf); gdn_ref[...] = adn[...].astype(bf)

def tables_call(counts, tag, img, cot, stats, wqkv, wr, wdn, gains):
    n = counts.shape[0]
    T = tag.shape[0] // n; I = img.shape[0] // n; D = tag.shape[1]; F = wdn.shape[0]; NK = T + I
    V = lambda *s, d=bf: pltpu.VMEM(s, d)
    def row(r, c): return pl.BlockSpec((r, c), lambda t, *_: (t, 0))
    def whole(a): return pl.BlockSpec(a.shape, lambda t, *_: (0, 0), pipeline_mode=pl.Buffered(1))
    def wholeo(r, c): return pl.BlockSpec((r, c), lambda t, *_: (0, 0))
    outs = [((n * T, D), bf, row(T, D)), ((n * T, D), f32, row(T, D)), ((n * I, D), f32, row(I, D)),
            ((D, 3 * D), bf, wholeo(D, 3 * D)), ((D, D + F), bf, wholeo(D, D + F)), ((F, D), bf, wholeo(F, D)),
            ((4, D), f32, wholeo(4, D)), ((2, D), f32, wholeo(2, D))]
    return pl.pallas_call(
        k2_body,
        out_shape=[jax.ShapeDtypeStruct(s, d) for s, d, _ in outs],
        grid_spec=pltpu.PrefetchScalarGridSpec(
            num_scalar_prefetch=1, grid=(n,),
            in_specs=[row(T, D), row(I, D), row(T, D)] + [whole(a) for a in (stats, wqkv, wr, wdn, gains)],
            out_specs=[s for _, _, s in outs],
            scratch_shapes=[V(I, D), V(NK, D), V(NK, D), V(D, NK), V(D, NK), V(T, D), V(D, T), V(T, T, d=f32),
                V(2, NK, T, d=f32), V(HEADS, NK, T), V(D, T), V(D, T, d=f32), V(HEADS, 1, T, d=f32),
                V(T, D), V(T, F), V(T, D), V(T, F), V(T, D), V(T, D, d=f32), V(T, 3 * D), V(I, 2 * D), V(D, T), V(T, D), V(D, T),
                V(HEADS, 1, T, d=f32),
                V(D, 3 * D, d=f32), V(D, D, d=f32), V(D, F, d=f32), V(F, D, d=f32)]),
        compiler_params=pltpu.CompilerParams(vmem_limit_bytes=62 * 2**20),
        name="tables",
    )(counts, tag, img, cot, stats, wqkv, wr, wdn, gains)


def update_kernel(
    place, gz_ref, img_ref, stats_ref, gains_ref, small_ref, nsq_ref, oq, orr, od,
    w0, w1, w2, w3, w4, f0, f1, f2, f3, f4, v0, v1, v2, v3, v4,
    gimg_ref, norm_ref, *outs
):
    D = gz_ref.shape[1]
    total_rows = place[1].astype(f32)
    gb = gains_ref[4:5, :]
    k = stats_ref[1:2, :] * gb
    gsum = small_ref[4:5, :]
    bsum = small_ref[5:6, :]
    hat = (img_ref[...].astype(f32) - stats_ref[0:1, :]) * stats_ref[1:2, :]
    gimg_ref[...] = k * (gz_ref[...] - bsum / total_rows - hat * (gsum / total_rows))

    @pl.when(pl.program_id(0) == 0)
    def _():
        total_norm = jnp.sqrt(nsq_ref[0:1, 0:1])
        norm_ref[...] = total_norm
        factor = CLIP_AT / jnp.maximum(total_norm, CLIP_AT)
        cols = w4.shape[1]
        row = lax.broadcasted_iota(jnp.int32, (D, cols), 0)
        col = lax.broadcasted_iota(jnp.int32, (D, cols), 1)
        pick = (row == col + place[0] * cols).astype(f32)
        own = lax.dot_general(
            small_ref[...], pick, (((1,), (0,)), ((), ())), precision=lax.Precision.HIGHEST, preferred_element_type=f32
        )[0:6]
        grads = (oq[...], orr[:, 0:D], orr[:, D:], od[...], own)
        rates = (RATE_MATRIX, RATE_OUTPUT, RATE_MATRIX, RATE_MATRIX, RATE_NORMS)
        for i, (g, w, f, v) in enumerate(zip(grads, (w0, w1, w2, w3, w4), (f0, f1, f2, f3, f4), (v0, v1, v2, v3, v4))):
            clip = g * factor
            moment = BETA_FIRST * f[...] + (1.0 - BETA_FIRST) * clip
            square = BETA_SECOND * v[...] + (1.0 - BETA_SECOND) * clip * clip
            u = (moment / (1.0 - BETA_FIRST**STEP)) / (jnp.sqrt(square / (1.0 - BETA_SECOND**STEP)) + ADAM_EPS)
            if i < 4:
                new = w[...] - rates[i] * (u + DECAY_RATE * w[...])
            else:
                new = w[...] - rates[i] * u
            outs[i][...] = clip
            outs[5 + i][...] = moment
            outs[10 + i][...] = square
            outs[15 + i][...] = new
            outs[20 + i][...] = new.astype(bf)


def update(place, gz, img, stats, gains, small, nsq, owned, masters, firsts, seconds, steps):
    rows, D = gz.shape
    block = rows // steps

    def whole(a):
        return pl.BlockSpec(a.shape, lambda t, *_: (0, 0))

    tile = pl.BlockSpec((block, D), lambda t, *_: (t, 0))
    small_in = (stats, gains, small, nsq) + tuple(owned) + tuple(masters) + tuple(firsts) + tuple(seconds)
    shapes = [jax.ShapeDtypeStruct(m.shape, f32) for m in masters] * 4 + [jax.ShapeDtypeStruct(m.shape, bf) for m in masters]
    one = jax.ShapeDtypeStruct((1, 1), f32)
    return pl.pallas_call(
        update_kernel,
        out_shape=[jax.ShapeDtypeStruct((rows, D), f32), one] + shapes,
        grid_spec=pltpu.PrefetchScalarGridSpec(
            num_scalar_prefetch=1,
            grid=(steps,),
            in_specs=[tile, tile] + [whole(a) for a in small_in],
            out_specs=[tile, whole(one)] + [whole(a) for a in shapes],
        ),
        compiler_params=pltpu.CompilerParams(vmem_limit_bytes=40 * 2**20),
        name="update",
    )(place, gz, img, *small_in)


def gather_any(img, wqkv, wout, wup, wdn, norm):
    full = lambda a, axis: lax.all_gather(a.astype(bf), AXES, axis=axis, tiled=True)
    gr = jnp.concatenate([full(wout, 0), full(wup, 0)], 1)
    gains = jnp.concatenate([full(norm, 1).astype(f32), jnp.zeros((2, img.shape[1]), f32)], 0)
    values = img.astype(f32)
    total = img.shape[0] * lax.axis_size(AXES)
    mean = lax.psum(jnp.sum(values, 0), AXES) / total
    centred = values - mean
    spread = lax.psum(jnp.sum(centred * centred, 0), AXES) / total
    return full(wqkv, 0), gr, full(wdn, 0), jnp.stack([mean, lax.rsqrt(spread + EPS)]), gains


def scatter_any(gq, gr, gd, terms, bnsum):
    part = lambda a: lax.psum_scatter(a.astype(f32), AXES, scatter_dimension=0, tiled=True)
    oq, orr, od = part(gq), part(gr), part(gd)
    small = lax.psum(jnp.concatenate([terms, bnsum, jnp.zeros_like(bnsum)], 0), AXES)
    local = jnp.sum(oq * oq) + jnp.sum(orr * orr) + jnp.sum(od * od)
    nsq = lax.psum(local, AXES) + jnp.sum(small * small)
    return oq, orr, od, small, jnp.full((8, 128), nsq, f32)


def shards(direct, tag_inputs, image_inputs, tag_counts, cotangent, *params):
    masters, firsts, seconds = params[0:5], params[5:10], params[10:15]
    tables = tag_counts.shape[0]
    devices = lax.axis_size(AXES)
    total_rows = image_inputs.shape[0] * devices
    wq, wr, wd, stats, gains = (gather if direct else gather_any)(image_inputs, *masters)
    mixed, gtags, gz, gq, gr, gd, terms, bnsum = tables_call(
        tag_counts, tag_inputs, image_inputs, cotangent, stats, wq, wr, wd, gains
    )
    oq, orr, od, small, nsq = (scatter if direct else scatter_any)(gq, gr, gd, terms, bnsum)
    place = jnp.stack([lax.axis_index(AXES), jnp.int32(total_rows)])
    gimg, norm, *rest = update(
        place, gz, image_inputs, stats, gains, small, nsq, (oq, orr, od), masters, firsts, seconds, tables
    )
    return (mixed, gtags, gimg, norm.reshape(()), *rest)


def solution(mesh):
    rows = P(AXES, None)
    state = (rows, rows, rows, rows, P(None, AXES))
    direct = dict(mesh.shape) == {"wide": 16, "narrow": 2}
    return jax.shard_map(
        functools.partial(shards, direct),
        mesh=mesh,
        in_specs=(rows, rows, P(AXES), rows) + state * 3,
        out_specs=(rows, rows, rows, P()) + state * 5,
        check_vma=False,
    )
```

```python
import functools
import math

import jax
import jax.numpy as jnp
from jax import lax
from jax.experimental import pallas as pl
from jax.experimental.pallas import tpu as pltpu
from jax.sharding import PartitionSpec as P

f32 = jnp.float32
bf = jnp.bfloat16
MESH = pl.DeviceIdType.MESH
HEADS = 8
STEP = 10
EPS = 1e-05
NEG = -1000000000.0
CLIP_AT = 1.0
BETA_FIRST = 0.9
BETA_SECOND = 0.999
ADAM_EPS = 1e-08
RATE_MATRIX = 0.05
RATE_OUTPUT = 1.0
RATE_NORMS = 0.5
DECAY_RATE = 0.1
GC = math.sqrt(2 / math.pi)
GA = 0.044715
AXES = ("wide", "narrow")
VM = pl.BlockSpec(memory_space=pltpu.VMEM)


def dg(a, b, ca, cb):
    return lax.dot_general(a, b, (((ca,), (cb,)), ((), ())), preferred_element_type=f32)


class Place:
    def __init__(self):
        self.w = lax.axis_index("wide")
        self.c = lax.axis_index("narrow")
        self.x = lax.rem(self.w, 2)
        self.y = lax.rem(self.w // 2, 2)
        self.z = self.w // 4
        self.d = self.w * 2 + self.c
        self.to_x = (self.w + 1 - 2 * self.x, self.c)
        self.to_y = (self.w + 2 - 4 * self.y, self.c)
        self.sib = (self.w, 1 - self.c)

    def to_z(self, k):
        return (lax.rem(self.w + 4 * k, 16), self.c)

    def peer(self, k):
        d = lax.rem(self.d + k, 32)
        return (d // 2, lax.rem(d, 2))


def greet_all(me):
    bar = pltpu.get_barrier_semaphore()
    for k in range(1, 32):
        pl.semaphore_signal(bar, inc=1, device_id=me.peer(k), device_id_type=MESH)
    pl.semaphore_wait(bar, 31)


def remote(src, dst, ss, rs, dev):
    return pltpu.make_async_remote_copy(
        src_ref=src, dst_ref=dst, send_sem=ss, recv_sem=rs, device_id=dev, device_id_type=MESH
    )


def mo(a, n):
    return pl.multiple_of(a, n)


class Gather:
    SLOTS = 35

    def __init__(self, me, g, ss, rs, split):
        self.me, self.g, self.ss, self.rs = me, g, ss, rs
        self.rows = g.shape[0] // 32
        n = g.shape[1]
        self.h = n // 2 if split else n
        self.split = split
        self.sent = []

    def ref(self, kz, pos, part=None, c=None):
        me = self.me
        z = lax.rem(me.z + 4 - kz, 4)
        y = me.y if pos in (0, 1) else 1 - me.y
        x = me.x if pos in (0, 2) else 1 - me.x
        d = z * 8 + y * 4 + x * 2 + (me.c if c is None else c)
        rows = pl.ds(mo(d * self.rows, self.rows), self.rows)
        if part is None:
            return self.g.at[rows]
        return self.g.at[rows, pl.ds(part * self.h, self.h)]

    def go(self, kz, pos, part, slot, dev):
        ref = self.ref(kz, pos, part)
        remote(ref, ref, self.ss.at[slot], self.rs.at[slot], dev).start()
        self.sent.append((kz, pos, part, slot))

    def got(self, slot, *key, **kw):
        ref = self.ref(*key, **kw)
        remote(ref, ref, self.ss.at[slot], self.rs.at[slot], self.me.sib).wait_recv()

    def start(self):
        me = self.me
        for k in (2, 1, 3):
            self.go(0, 0, None, k - 1, me.to_z(k))
        self.go(0, 0, None, 3, me.to_x)
        self.go(0, 0, None, 7, me.to_y)
        self.go(0, 0, None, 19, me.sib)

    def column(self):
        me = self.me
        for k in (1, 3, 2):
            self.got(k - 1, k, 0)
            self.go(k, 0, None, 3 + k, me.to_x)
            self.go(k, 0, None, 7 + k, me.to_y)
            self.go(k, 0, None, 19 + k, me.sib)

    def plane(self):
        me = self.me
        for k in (0, 1, 3, 2):
            self.got(3 + k, k, 1)
            self.go(k, 1, 0, 11 + k, me.to_y)
            self.go(k, 1, None, 23 + k, me.sib)
            self.got(7 + k, k, 2)
            if self.split:
                self.go(k, 2, 1, 15 + k, me.to_x)
            self.go(k, 2, None, 27 + k, me.sib)

    def corner(self):
        me = self.me
        for k in (0, 1, 3, 2):
            self.got(11 + k, k, 3, 0)
            if self.split:
                self.got(15 + k, k, 3, 1)
            self.go(k, 3, None, 31 + k, me.sib)

    def finish(self):
        for pos in range(4):
            for k in range(4):
                self.got(19 + 4 * pos + k, k, pos, c=1 - self.me.c)
        for kz, pos, part, slot in self.sent:
            ref = self.ref(kz, pos, part)
            remote(ref, ref, self.ss.at[slot], self.rs.at[slot], self.me.sib).wait_send()


def push_all(me, g, ss, rs):
    for k in range(1, 32):
        remote(g.at[me.d], g.at[me.d], ss.at[k], rs.at[k], me.peer(k)).start()


def push_done(me, g, ss, rs):
    for k in range(1, 32):
        remote(g.at[me.d], g.at[me.d], ss.at[k], rs.at[k], me.sib).wait_send()
        src = lax.rem(me.d + 32 - k, 32)
        remote(g.at[src], g.at[src], ss.at[k], rs.at[k], me.sib).wait_recv()


class Scatter:
    SLOTS = 8

    def __init__(self, me, g, out, bufs, ss, rs):
        self.me, self.g, self.out, self.ss, self.rs = me, g, out, ss, rs
        self.r0, self.r1a, self.r1b, self.r2a, self.r2b, self.s2, self.r3 = bufs
        self.s0, self.s1a, self.s1b = self.r0, self.r1a, self.r1b
        self.h = g.shape[-1] // 2

    @staticmethod
    def bufs(R, N):
        h = N // 2
        v = lambda *s: pltpu.VMEM(s, bf)
        return [
            v(4, 2, 2, R, N), v(4, 2, R, h), v(4, 2, R, h), v(4, R, h), v(4, R, h), v(4, R, N), v(3, R, N),
        ]

    def hop(self, slot):
        me, h = self.me, self.h
        if slot == 0:
            src, dst, dev = self.g.at[:, :, :, 1 - me.c], self.r0, me.sib
        elif slot == 1:
            src, dst, dev = self.s0.at[:, :, 1 - me.x, :, pl.ds(0, h)], self.r1a, me.to_x
        elif slot == 2:
            src, dst, dev = self.s0.at[:, 1 - me.y, :, :, pl.ds(h, h)], self.r1b, me.to_y
        elif slot == 3:
            src, dst, dev = self.s1a.at[:, 1 - me.y], self.r2a, me.to_y
        elif slot == 4:
            src, dst, dev = self.s1b.at[:, 1 - me.x], self.r2b, me.to_x
        else:
            k = slot - 4
            src, dst, dev = self.s2.at[lax.rem(me.z + k, 4)], self.r3.at[k - 1], me.to_z(k)
        return remote(src, dst, self.ss.at[slot], self.rs.at[slot], dev)

    def core(self):
        self.hop(0).start()

    def plane1(self):
        me = self.me
        self.hop(0).wait_recv()

        def add(i, _):
            k = (i // 4, lax.rem(i // 2, 2), lax.rem(i, 2))
            self.s0[k] = (self.g[k + (me.c,)].astype(f32) + self.r0[k].astype(f32)).astype(bf)
            return 0

        lax.fori_loop(0, 16, add, 0)
        self.hop(1).start()
        self.hop(2).start()

    def plane2(self):
        me, h = self.me, self.h
        self.hop(1).wait_recv()
        self.hop(2).wait_recv()

        def add(i, _):
            z, k = i // 2, lax.rem(i, 2)
            a = self.s0[z, k, me.x, :, pl.ds(0, h)].astype(f32) + self.r1a[z, k].astype(f32)
            self.s1a[z, k] = a.astype(bf)
            b = self.s0[z, me.y, k, :, pl.ds(h, h)].astype(f32) + self.r1b[z, k].astype(f32)
            self.s1b[z, k] = b.astype(bf)
            return 0

        lax.fori_loop(0, 8, add, 0)
        self.hop(3).start()
        self.hop(4).start()

    def column(self):
        me, h = self.me, self.h
        self.hop(3).wait_recv()
        self.hop(4).wait_recv()
        for z in range(4):
            self.s2[z, :, 0:h] = (self.s1a[z, me.y].astype(f32) + self.r2a[z].astype(f32)).astype(bf)
            self.s2[z, :, h:] = (self.s1b[z, me.x].astype(f32) + self.r2b[z].astype(f32)).astype(bf)
        for k in (2, 1, 3):
            self.hop(4 + k).start()

    def finish(self):
        acc = self.s2[self.me.z].astype(f32)
        for k in (1, 2, 3):
            self.hop(4 + k).wait_recv()
            acc += self.r3[k - 1].astype(f32)
        self.out[...] = acc
        for slot in range(8):
            self.hop(slot).wait_send()
        return jnp.sum(acc * acc)


class Sums:
    def __init__(self, me, tb, ss, rs):
        self.me, self.tb, self.ss, self.rs = me, tb, ss, rs

    def hop(self, slot):
        me = self.me
        src, dst, dev = ((0, 1, me.sib), (2, 3, me.to_x), (4, 5, me.to_y))[slot] if slot < 3 else (
            6 + me.z, 6 + me.z, me.to_z(slot - 2)
        )
        return remote(self.tb.at[src], self.tb.at[dst], self.ss.at[slot], self.rs.at[slot], dev)

    def step(self, i):
        tb = self.tb
        if i > 0:
            self.hop(i - 1).wait_recv()
            at = 2 * i if i < 3 else 6 + self.me.z
            tb[at] = tb[2 * i - 2] + tb[2 * i - 1]
        for slot in (i,) if i < 3 else (3, 4, 5):
            self.hop(slot).start()

    def finish(self):
        tb = self.tb
        for k in (1, 2, 3):
            at = tb.at[6 + lax.rem(self.me.z + 4 - k, 4)]
            remote(at, at, self.ss.at[2 + k], self.rs.at[2 + k], self.me.sib).wait_recv()
        for slot in range(6):
            self.hop(slot).wait_send()
        return (tb[6] + tb[7]) + (tb[8] + tb[9])


class Refs:
    pass


def tables_kernel(direct, names, *refs):
    r = Refs()
    for name, ref in zip(names, refs, strict=True):
        setattr(r, name, ref)
    t = pl.program_id(0)
    first = t == 0
    last = t == pl.num_programs(0) - 1
    T, D = r.tag.shape
    I = r.imglow.shape[0]
    NK = T + I
    hd = D // HEADS
    F = r.act.shape[1]
    count = r.counts[t]
    half = HEADS // 4
    HC = D // 2
    if direct:
        me = Place()
        gat = [
            Gather(me, r.wq, r.gs.at[0], r.gs.at[1], True),
            Gather(me, r.wn, r.gs.at[2], r.gs.at[3], False),
            Gather(me, r.wr, r.gs.at[4], r.gs.at[5], True),
            Gather(me, r.wd, r.gs.at[6], r.gs.at[7], True),
        ]
        sq0 = Scatter(me, r.gq0, r.oq0, r.bq0, r.cs.at[0], r.cs.at[1])
        sq1 = Scatter(me, r.gq1, r.oq1, r.bq1, r.cs.at[2], r.cs.at[3])
        sr = Scatter(me, r.gr, r.orr, r.br, r.cs.at[4], r.cs.at[5])
        sd = Scatter(me, r.gd, r.od, r.bd, r.cs.at[6], r.cs.at[7])
        sm = Sums(me, r.tb, r.cs.at[8], r.cs.at[9])
    wout_ref = r.wr.at[:, 0:D]
    wup_ref = r.wr.at[:, D : D + F]

    @pl.when(first)
    def _():
        r.aqkv[...] = jnp.zeros_like(r.aqkv)
        r.aout[...] = jnp.zeros_like(r.aout)
        r.aup[...] = jnp.zeros_like(r.aup)
        r.adn[...] = jnp.zeros_like(r.adn)
        r.terms[...] = jnp.zeros_like(r.terms)

    if direct:

        @pl.when(first)
        def _():
            img_in = pltpu.make_async_copy(r.img_hbm, r.img, r.isem)
            img_in.start()
            R, RD = r.pqkv.shape[0], r.pdn.shape[0]
            own = pl.ds(mo(me.d * R, R), R)
            r.wq[own, :] = r.pqkv[...].astype(bf)
            r.wr[own, pl.ds(0, D)] = r.pout[...].astype(bf)
            r.wr[own, pl.ds(D, F)] = r.pup[...].astype(bf)
            r.wd[pl.ds(mo(me.d * RD, RD), RD), :] = r.pdn[...].astype(bf)
            lane = lax.broadcasted_iota(jnp.int32, (16, 128), 1)
            unit = lax.broadcasted_iota(jnp.int32, (16, 128), 0)
            at = (lane == unit + 16 * lax.rem(me.d, 8)).astype(bf)
            tile = dg(r.pnorm[...].astype(bf), at, 1, 0)
            r.wn[pl.ds(mo(me.d * 16, 16), 16), :] = jnp.concatenate([tile, jnp.zeros((10, 128), f32)], 0).astype(bf)
            greet_all(me)
            gat[0].start()
            gat[1].start()
            img_in.wait()
            rows = r.img.shape[0]
            step = rows // 3
            total = jnp.zeros((1, D), f32)
            for i in range(3):
                total += jnp.sum(r.img[i * step : (i + 1) * step, :].astype(f32), 0, keepdims=True)
            mean_d = total / rows
            m2 = jnp.zeros((1, D), f32)
            for i in range(3):
                cen = r.img[i * step : (i + 1) * step, :].astype(f32) - mean_d
                m2 += jnp.sum(cen * cen, 0, keepdims=True)
            for g in range(4):
                r.st[me.d, g : g + 1, :] = mean_d[:, g * 128 : (g + 1) * 128]
                r.st[me.d, g + 4 : g + 5, :] = m2[:, g * 128 : (g + 1) * 128]
            push_all(me, r.st, r.ps.at[0], r.ps.at[1])
            gat[0].column()
            gat[1].column()
            gat[2].start()
            gat[3].start()
            gat[0].plane()
            gat[1].plane()
            gat[0].corner()
            gat[1].corner()
            push_done(me, r.st, r.ps.at[0], r.ps.at[1])
            mean = jnp.sum(r.st[:, 0:4, :], 0) / 32
            off = r.st[:, 0:4, :] - mean[None]
            spread = (jnp.sum(r.st[:, 4:8, :], 0) + rows * jnp.sum(off * off, 0)) / (rows * 32)
            inv = lax.rsqrt(spread + EPS)
            for g in range(4):
                r.stats[0:1, g * 128 : (g + 1) * 128] = mean[g : g + 1, :]
                r.stats[1:2, g * 128 : (g + 1) * 128] = inv[g : g + 1, :]
            gat[1].finish()
            for z in range(4):
                acc = jnp.zeros((8, 128), f32)
                for k in range(8):
                    acc += r.wn[(z * 8 + k) * 16 : (z * 8 + k) * 16 + 16, :].astype(f32)[0:8]
                r.gains[:, z * 128 : (z + 1) * 128] = acc
            gat[0].finish()

    img_ref = r.img.at[pl.ds(mo(t * I, 16), I)] if direct else r.img
    mean = r.stats[0:1, :]
    inv = r.stats[1:2, :]
    g1, b1, g2 = r.gains[0:1, :], r.gains[1:2, :], r.gains[2:3, :]
    b2, gb, bb = r.gains[3:4, :], r.gains[4:5, :], r.gains[5:6, :]
    img_parts = ((0, 256), (256, 256), (512, I - 512))

    for r0, rl in img_parts:
        img_hat = (img_ref[r0 : r0 + rl, :].astype(f32) - mean) * inv
        r.imglow[r0 : r0 + rl, :] = (img_hat * gb + bb).astype(bf)
    for r0 in range(0, T, 256):
        q = dg(r.tag[r0 : r0 + 256, :], r.wq[:, 0:D], 1, 0).astype(bf) * bf(1.0 / math.sqrt(hd))
        r.q[r0 : r0 + 256, :] = q
        r.qT[:, r0 : r0 + 256] = q.T
    for j, (dst, dstT) in enumerate(((r.kall, r.kT), (r.vall, r.vT))):
        w = r.wq[:, (j + 1) * D : (j + 2) * D]
        for r0 in range(0, T, 256):
            a = dg(r.tag[r0 : r0 + 256, :], w, 1, 0).astype(bf)
            dst[r0 : r0 + 256, :] = a
            dstT[:, r0 : r0 + 256] = a.T
        for r0, rl in img_parts:
            a = dg(r.imglow[r0 : r0 + rl, :], w, 1, 0).astype(bf)
            dst[T + r0 : T + r0 + rl, :] = a
            dstT[:, T + r0 : T + r0 + rl] = a.T
    ji = lax.broadcasted_iota(jnp.int32, (T, T), 0)
    ii = lax.broadcasted_iota(jnp.int32, (T, T), 1)
    r.bias[...] = jnp.where((ji <= ii) & (ji < count), 3e38, NEG)

    chunks = [(0, 256, 0), (256, 256, 256), (512, 256, 0), (768, 256, 0), (1024, NK - 1024, 0)]
    nc = len(chunks)
    row64 = lax.broadcasted_iota(jnp.int32, (2 * hd, 1), 0)
    lane64 = lax.broadcasted_iota(jnp.int32, (1, 2 * hd), 1)

    def own_rows(a, b):
        return jnp.where((row64 < hd) if b == 0 else (row64 >= hd), a, jnp.zeros_like(a))

    def own_lanes(a, b):
        return jnp.where((lane64 < hd) if b == 0 else (lane64 >= hd), a, jnp.zeros_like(a))

    def fullq(a, q0, fill):
        if q0 == 0:
            return a
        return jnp.concatenate([jnp.full((a.shape[0], q0), fill, a.dtype), a], 1)

    def e_at(h, c):
        k0, kl, q0 = chunks[c]
        if q0:
            return r.e1.at[h]
        return r.e.at[h, 0:kl] if k0 == 0 else r.e.at[h, k0 - 256 : k0 - 256 + kl]

    def fwd_pair(p, _):
        ps = pl.ds(mo(p * 2 * hd, 2 * hd), 2 * hd)
        qzs = [own_rows(r.qT[ps, :], b) for b in range(2)]

        def A(b, c):
            k0, kl, q0 = chunks[c]
            s = dg(r.kall[k0 : k0 + kl, ps], qzs[b][:, q0:], 1, 0)
            if k0 < T:
                s = jnp.minimum(s, r.bias[k0 : k0 + kl, q0:])
            r.s[k0 : k0 + kl, q0:] = s
            return fullq(jnp.max(s, 0, keepdims=True), q0, NEG)

        def B(b, c, m):
            k0, kl, q0 = chunks[c]
            e = jnp.exp(r.s[k0 : k0 + kl, q0:] - m[:, q0:])
            l = jnp.sum(e, 0, keepdims=True)
            e = e.astype(bf)
            e_at(2 * p + b, c)[...] = e
            o = dg(r.vT[pl.ds(mo(p * 2 * hd + b * hd, hd), hd), k0 : k0 + kl], e, 1, 0)
            return fullq(o, q0, 0.0), fullq(l, q0, 0.0)

        def done(b, o, l):
            rl = 1.0 / l
            o = o * rl
            hs = pl.ds(mo(p * 2 * hd + b * hd, hd), hd)
            r.oT[hs, :] = o
            r.attT[hs, :] = o.astype(bf)
            r.rl[2 * p + b] = rl

        m0 = None
        for c in range(nc):
            mc = A(0, c)
            m0 = mc if m0 is None else jnp.maximum(m0, mc)
        m1 = None
        o = None
        for c in range(nc):
            oc, lc = B(0, c, m0)
            o, l = (oc, lc) if o is None else (o + oc, l + lc)
            mc = A(1, c)
            m1 = mc if m1 is None else jnp.maximum(m1, mc)
        done(0, o, l)
        o = None
        for c in range(nc):
            oc, lc = B(1, c, m1)
            o, l = (oc, lc) if o is None else (o + oc, l + lc)
        done(1, o, l)
        if direct:

            @pl.when(first & (p == 0))
            def _():
                gat[2].column()
                gat[3].column()

            @pl.when(first & (p == 1))
            def _():
                gat[2].plane()
                gat[3].plane()

            @pl.when(first & (p == 2))
            def _():
                gat[2].corner()
                gat[3].corner()

            @pl.when(first & (p == 3))
            def _():
                gat[2].finish()
                gat[3].finish()

        return 0

    lax.fori_loop(0, HEADS // 2, fwd_pair, 0)

    RC = 128
    zero = jnp.zeros((1, D), f32)

    def rows_part(i, tg):
        tg1, tb1, tg2, tb2 = tg
        r0 = mo(i * RC, RC)
        rs = pl.ds(r0, RC)
        hp = r.tag[rs, :].astype(f32) + dg(r.attT[:, rs], wout_ref[...], 0, 0)
        c = hp - jnp.mean(hp, -1, keepdims=True)
        inv1 = lax.rsqrt(jnp.mean(c * c, -1, keepdims=True) + EPS)
        hat1 = c * inv1
        hidden = hat1 * g1 + b1
        hl = hidden.astype(bf)
        r.hidlow[rs, :] = hl
        pre = dg(hl, wup_ref[...], 1, 0)
        p2 = pre * pre
        th = jnp.tanh(GC * (pre + GA * (p2 * pre)))
        act = (0.5 * pre * (1.0 + th)).astype(bf)
        r.act[rs, :] = act
        gp = 0.5 * (1.0 + th) + 0.5 * pre * (1.0 - th * th) * (GC * (1.0 + 3 * GA * p2))
        resid = hidden + dg(act, r.wd[...], 1, 0)
        c = resid - jnp.mean(resid, -1, keepdims=True)
        inv2 = lax.rsqrt(jnp.mean(c * c, -1, keepdims=True) + EPS)
        hat2 = c * inv2
        r.mixed[rs, :] = (hat2 * g2 + b2).astype(bf)
        rows = r0 + lax.broadcasted_iota(jnp.int32, (RC, 1), 0)
        go = jnp.where(rows < count, r.cot[rs, :].astype(f32), 0.0)
        tg2 += jnp.sum(go * hat2, 0, keepdims=True)
        tb2 += jnp.sum(go, 0, keepdims=True)
        s = go * g2
        gr = inv2 * (s - jnp.mean(s, -1, keepdims=True) - hat2 * jnp.mean(s * hat2, -1, keepdims=True))
        rlow = gr.astype(bf)
        r.rlow[rs, :] = rlow
        plow = (dg(rlow, r.wd[...], 1, 1) * gp).astype(bf)
        r.plow[rs, :] = plow
        gh = gr + dg(plow, wup_ref[...], 1, 1)
        tg1 += jnp.sum(gh * hat1, 0, keepdims=True)
        tb1 += jnp.sum(gh, 0, keepdims=True)
        s = gh * g1
        ghp = inv1 * (s - jnp.mean(s, -1, keepdims=True) - hat1 * jnp.mean(s * hat1, -1, keepdims=True))
        r.gtags[rs, :] = ghp
        hpl = ghp.astype(bf)
        r.hplow[rs, :] = hpl
        r.dOT[:, rs] = dg(hpl, wout_ref[...], 1, 1).astype(bf).T
        return tg1, tb1, tg2, tb2

    tg1, tb1, tg2, tb2 = lax.fori_loop(0, T // RC, rows_part, (zero,) * 4)
    r.terms[0:1, :] += tg1
    r.terms[1:2, :] += tb1
    r.terms[2:3, :] += tg2
    r.terms[3:4, :] += tb2
    for h in range(HEADS):
        hs = slice(h * hd, (h + 1) * hd)
        d = r.dOT[hs, :].astype(f32) * r.rl[h]
        r.dOT[hs, :] = d.astype(bf)
        r.delta[h] = jnp.sum(d * r.oT[hs, :], 0, keepdims=True)
    r.dO[...] = r.dOT[...].T

    def put(dst, acc, r0, rn, c0, cn, add, col=None):
        new = acc[r0 : r0 + rn, c0 : c0 + cn] + add
        acc[r0 : r0 + rn, c0 : c0 + cn] = new
        col = c0 if col is None else col
        low = new.astype(bf)
        if direct:
            R = dst.shape[4]
            nz = rn // (8 * R)
            z0 = r0 // (8 * R)
            dst[z0 : z0 + nz, :, :, :, :, col : col + cn] = low.reshape(nz, 2, 2, 2, R, cn)
        else:
            dst[r0 : r0 + rn, col : col + cn] = low

    for r0 in range(0, D, 256):
        put(r.gr, r.aout, r0, 256, 0, D, dg(r.attT[r0 : r0 + 256, :], r.hplow[...], 1, 0))
        for c0 in range(0, F, 512):
            put(r.gr, r.aup, r0, 256, c0, 512, dg(r.hidlow[:, r0 : r0 + 256], r.plow[:, c0 : c0 + 512], 0, 0), D + c0)
    for r0 in range(0, F, 256):
        put(r.gd, r.adn, r0, 256, 0, D, dg(r.act[:, r0 : r0 + 256], r.rlow[...], 0, 0))
    if direct:

        @pl.when(last)
        def _():
            sd.core()
            sr.core()

    def bwd_pair(p, _):
        p128 = mo(p * 2 * hd, 2 * hd)
        ps = pl.ds(p128, 2 * hd)
        dq = [None, None]
        ops = [(own_rows(r.dOT[ps, :], b), own_lanes(r.dO[:, ps], b), own_lanes(r.q[:, ps], b)) for b in range(2)]
        kc = pl.ds(mo(D + p128, 128), 2 * hd)
        vc = pl.ds(mo(2 * D + p128, 128), 2 * hd)
        for c in range(nc):
            k0, kl, q0 = chunks[c]
            ks = slice(k0, k0 + kl)
            dk = None
            for b in range(2):
                h = 2 * p + b
                hs = pl.ds(mo(p * 2 * hd + b * hd, hd), hd)
                dOz, dOl, ql = ops[b]
                dp = dg(r.vall[ks, ps], dOz[:, q0:], 1, 0)
                e = e_at(h, c)[...]
                ds = (e.astype(f32) * (dp - r.delta[h][:, q0:])).astype(bf)
                dvc = dg(e, dOl[q0:, :], 1, 0)
                dkc = dg(ds, ql[q0:, :], 1, 0)
                dqc = fullq(dg(r.kT[hs, ks], ds, 1, 0), q0, 0.0)
                dk, dv = (dkc, dvc) if dk is None else (dk + dkc, dv + dvc)
                dq[b] = dqc if dq[b] is None else dq[b] + dqc
            if k0 < T:
                r.dqkv[ks, kc] = dk.astype(bf)
                r.dqkv[ks, vc] = dv.astype(bf)
            else:
                si = slice(k0 - T, k0 - T + kl)
                r.dkvi[si, ps] = dk.astype(bf)
                r.dkvi[si, kc] = dv.astype(bf)
        for b in range(2):
            hs = pl.ds(mo(p * 2 * hd + b * hd, hd), hd)
            r.dqT[hs, :] = (dq[b] * (1.0 / math.sqrt(hd))).astype(bf)
        if direct:

            @pl.when(last & (p == 0))
            def _():
                sd.plane1()
                sr.plane1()

            @pl.when(last & (p == 1))
            def _():
                sd.plane2()

            @pl.when(last & (p == 2))
            def _():
                sd.column()
                sq0.plane1()

            @pl.when(last & (p == 3))
            def _():
                sr.column()
                sq0.plane2()

        return 0

    for i, gq in enumerate((r.gq0, r.gq1)):
        lax.fori_loop(i * half, (i + 1) * half, bwd_pair, 0)
        hc = slice(i * HC, (i + 1) * HC)
        r.dqkv[:, hc] = r.dqT[hc, :].T
        if i == 1:
            sg = jnp.zeros((1, D), f32)
            sb = sg
            for r0, rl in img_parts:
                rs = slice(r0, r0 + rl)
                gz = dg(r.dkvi[rs, :], r.wq[:, D:], 1, 1)
                r.gz[rs, :] = gz.astype(bf)
                hat = (img_ref[rs, :].astype(f32) - mean) * inv
                sg += jnp.sum(gz * hat, 0, keepdims=True)
                sb += jnp.sum(gz, 0, keepdims=True)
            r.terms[4:5, :] += sg
            r.terms[5:6, :] += sb
            if direct:

                @pl.when(last)
                def _():
                    r.tb[0] = r.terms[...]
                    sm.step(0)

        for r0 in range(0, D, 256):
            rs = slice(r0, r0 + 256)
            x = r.tag[:, rs]
            put(gq, r.aqkv, r0, 256, i * HC, HC, dg(x, r.dqkv[:, hc], 0, 0), 0)
            for j in (1, 2):
                cs = slice(j * D + i * HC, j * D + (i + 1) * HC)
                ci = slice(cs.start - D, cs.stop - D)
                add = dg(x, r.dqkv[:, cs], 0, 0) + dg(r.imglow[:, rs], r.dkvi[:, ci], 0, 0)
                put(gq, r.aqkv, r0, 256, cs.start, HC, add, j * HC)
        if direct and i == 0:

            @pl.when(last)
            def _():
                sq0.core()
                sr.plane2()

    if direct:

        @pl.when(last)
        def _():
            sq1.core()

    for r0 in range(0, T, 256):
        r.gtags[r0 : r0 + 256, :] += dg(r.dqkv[r0 : r0 + 256, :], r.wq[...], 1, 1)

    if direct:

        @pl.when(last)
        def _():
            sm.step(1)
            sq1.plane1()
            sq0.column()
            sq = sd.finish()
            sm.step(2)
            sq1.plane2()
            sq += sr.finish()
            sm.step(3)
            sq1.column()
            sq += sq0.finish()
            tot = sm.finish()
            r.small[...] = tot
            sq += sq1.finish()
            r.st[me.d] = jnp.full((8, 128), sq, f32)
            push_all(me, r.st, r.ps.at[2], r.ps.at[3])
            push_done(me, r.st, r.ps.at[2], r.ps.at[3])
            r.nsq[...] = jnp.sum(r.st[...], 0) + jnp.sum(tot * tot)


def tables_call(direct, counts, tag, img, cot, params):
    n = counts.shape[0]
    T, I, D = tag.shape[0] // n, img.shape[0] // n, tag.shape[1]
    NK = T + I
    HC = D // 2
    V = lambda *s, d=bf: pltpu.VMEM(s, d)
    S = jax.ShapeDtypeStruct

    def row(a, b):
        return pl.BlockSpec((a, b), lambda t, *_: (t, 0))

    def whole(shape, **kw):
        return pl.BlockSpec(shape, lambda t, *_: (0,) * len(shape), **kw)

    one = dict(pipeline_mode=pl.Buffered(1))
    if direct:
        F = params[2].shape[1]
        R, RD = params[0].shape[0], params[3].shape[0]
        ins = [("tag", row(T, D)), ("img_hbm", pl.BlockSpec(memory_space=pl.ANY)), ("cot", row(T, D))]
        ins += [(k, whole(a.shape, **one)) for k, a in zip(("pqkv", "pout", "pup", "pdn", "pnorm"), params)]
    else:
        F = params[4].shape[0]
        ins = [("tag", row(T, D)), ("img", row(I, D)), ("cot", row(T, D))]
        ins += [(k, whole(a.shape, **one)) for k, a in zip(("stats", "gains", "wq", "wr", "wd"), params)]
    outs = [
        ("mixed", S((n * T, D), bf), row(T, D)),
        ("gtags", S((n * T, D), f32), row(T, D)),
        ("gz", S((n * I, D), bf), row(I, D)),
    ]
    scratch = [
        ("imglow", V(I, D)), ("kall", V(NK, D)), ("vall", V(NK, D)), ("kT", V(D, NK)), ("vT", V(D, NK)),
        ("q", V(T, D)), ("qT", V(D, T)), ("bias", V(T, T, d=f32)), ("s", V(NK, T, d=f32)),
        ("e", V(HEADS, NK - 256, T)), ("e1", V(HEADS, 256, T - 256)), ("attT", V(D, T)), ("oT", V(D, T, d=f32)),
        ("rl", V(HEADS, 1, T, d=f32)), ("hidlow", V(T, D)), ("act", V(T, F)), ("rlow", V(T, D)), ("plow", V(T, F)),
        ("hplow", V(T, D)), ("dqkv", V(T, 3 * D)), ("dkvi", V(I, 2 * D)), ("dqT", V(D, T)), ("dO", V(T, D)),
        ("dOT", V(D, T)), ("delta", V(HEADS, 1, T, d=f32)), ("aqkv", V(D, 3 * D, d=f32)), ("aout", V(D, D, d=f32)),
        ("aup", V(D, F, d=f32)), ("adn", V(F, D, d=f32)),
    ]
    if direct:
        outs += [
            ("oq0", S((R, 3 * HC), f32), None), ("oq1", S((R, 3 * HC), f32), None), ("orr", S((R, D + F), f32), None),
            ("od", S((RD, D), f32), None), ("small", S((8, D), f32), None), ("nsq", S((8, 128), f32), None),
            ("stats", S((2, D), f32), None), ("gains", S((8, D), f32), None),
        ]
        dims = (4, 2, 2, 2)
        dma = pltpu.SemaphoreType.DMA
        scratch += [
            ("img", V(n * I, D)), ("wq", V(D, 3 * D)), ("wr", V(D, D + F)), ("wd", V(F, D)), ("wn", V(32 * 16, 128)),
            ("st", V(32, 8, 128, d=f32)), ("terms", V(8, D, d=f32)), ("tb", V(10, 8, D, d=f32)),
            ("gq0", V(*dims, R, 3 * HC)), ("gq1", V(*dims, R, 3 * HC)), ("gr", V(*dims, R, D + F)), ("gd", V(*dims, RD, D)),
            ("bq0", Scatter.bufs(R, 3 * HC)), ("bq1", Scatter.bufs(R, 3 * HC)), ("br", Scatter.bufs(R, D + F)),
            ("bd", Scatter.bufs(RD, D)),
            ("isem", dma), ("gs", dma((8, Gather.SLOTS))), ("cs", dma((10, Scatter.SLOTS))), ("ps", dma((4, 32))),
        ]
        extra = dict(collective_id=0, has_side_effects=True)
    else:
        outs += [
            ("gq0", S((D, 3 * HC), bf), None), ("gq1", S((D, 3 * HC), bf), None), ("gr", S((D, D + F), bf), None),
            ("gd", S((F, D), bf), None), ("terms", S((8, D), f32), None),
        ]
        extra = {}
    names = ("counts",) + tuple(k for k, _ in ins) + tuple(k for k, _, _ in outs) + tuple(k for k, _ in scratch)
    return pl.pallas_call(
        functools.partial(tables_kernel, direct, names),
        out_shape=[s for _, s, _ in outs],
        grid_spec=pltpu.PrefetchScalarGridSpec(
            num_scalar_prefetch=1,
            grid=(n,),
            in_specs=[b for _, b in ins],
            out_specs=[whole(s.shape) if b is None else b for _, s, b in outs],
            scratch_shapes=[a for _, a in scratch],
        ),
        compiler_params=pltpu.CompilerParams(vmem_limit_bytes=63 * 2**20, **extra),
        name="tables",
    )(counts, tag, img, cot, *params)


def update_kernel(
    place, gz_ref, img_ref, stats_ref, gains_ref, small_ref, nsq_ref, oq0, oq1, orr, od,
    w0, w1, w2, w3, w4, f0, f1, f2, f3, f4, v0, v1, v2, v3, v4,
    gimg_ref, norm_ref, *outs
):
    D = gz_ref.shape[1]
    total_rows = place[1].astype(f32)
    gb = gains_ref[4:5, :]
    k = stats_ref[1:2, :] * gb
    gsum = small_ref[4:5, :]
    bsum = small_ref[5:6, :]
    hat = (img_ref[...].astype(f32) - stats_ref[0:1, :]) * stats_ref[1:2, :]
    gimg_ref[...] = k * (gz_ref[...].astype(f32) - bsum / total_rows - hat * (gsum / total_rows))

    @pl.when(pl.program_id(0) == 0)
    def _():
        total_norm = jnp.sqrt(nsq_ref[0:1, 0:1])
        norm_ref[...] = total_norm
        factor = CLIP_AT / jnp.maximum(total_norm, CLIP_AT)
        cols = w4.shape[1]
        row = lax.broadcasted_iota(jnp.int32, (D, cols), 0)
        col = lax.broadcasted_iota(jnp.int32, (D, cols), 1)
        pick = (row == col + place[0] * cols).astype(f32)
        own = lax.dot_general(
            small_ref[...], pick, (((1,), (0,)), ((), ())), precision=lax.Precision.HIGHEST, preferred_element_type=f32
        )[0:6]
        hc = D // 2
        oq = [o[:, j * hc : (j + 1) * hc] for j in range(3) for o in (oq0, oq1)]
        grads = (jnp.concatenate(oq, 1), orr[:, 0:D], orr[:, D:], od[...], own)
        rates = (RATE_MATRIX, RATE_OUTPUT, RATE_MATRIX, RATE_MATRIX, RATE_NORMS)
        for i, (g, w, f, v) in enumerate(zip(grads, (w0, w1, w2, w3, w4), (f0, f1, f2, f3, f4), (v0, v1, v2, v3, v4))):
            clip = g * factor
            moment = BETA_FIRST * f[...] + (1.0 - BETA_FIRST) * clip
            square = BETA_SECOND * v[...] + (1.0 - BETA_SECOND) * clip * clip
            u = (moment / (1.0 - BETA_FIRST**STEP)) / (jnp.sqrt(square / (1.0 - BETA_SECOND**STEP)) + ADAM_EPS)
            if i < 4:
                new = w[...] - rates[i] * (u + DECAY_RATE * w[...])
            else:
                new = w[...] - rates[i] * u
            outs[i][...] = clip
            outs[5 + i][...] = moment
            outs[10 + i][...] = square
            outs[15 + i][...] = new
            outs[20 + i][...] = new.astype(bf)


def update(place, gz, img, stats, gains, small, nsq, owned, masters, firsts, seconds, steps):
    rows, D = gz.shape
    block = rows // steps

    def whole(a):
        return pl.BlockSpec(a.shape, lambda t, *_: (0, 0))

    tile = pl.BlockSpec((block, D), lambda t, *_: (t, 0))
    small_in = (stats, gains, small, nsq) + tuple(owned) + tuple(masters) + tuple(firsts) + tuple(seconds)
    shapes = [jax.ShapeDtypeStruct(m.shape, f32) for m in masters] * 4 + [jax.ShapeDtypeStruct(m.shape, bf) for m in masters]
    one = jax.ShapeDtypeStruct((1, 1), f32)
    return pl.pallas_call(
        update_kernel,
        out_shape=[jax.ShapeDtypeStruct((rows, D), f32), one] + shapes,
        grid_spec=pltpu.PrefetchScalarGridSpec(
            num_scalar_prefetch=1,
            grid=(steps,),
            in_specs=[tile, tile] + [whole(a) for a in small_in],
            out_specs=[tile, whole(one)] + [whole(a) for a in shapes],
        ),
        compiler_params=pltpu.CompilerParams(vmem_limit_bytes=40 * 2**20),
        name="update",
    )(place, gz, img, *small_in)


def gather_any(img, wqkv, wout, wup, wdn, norm):
    full = lambda a, axis: lax.all_gather(a.astype(bf), AXES, axis=axis, tiled=True)
    gr = jnp.concatenate([full(wout, 0), full(wup, 0)], 1)
    gains = jnp.concatenate([full(norm, 1).astype(f32), jnp.zeros((2, img.shape[1]), f32)], 0)
    values = img.astype(f32)
    total = img.shape[0] * lax.axis_size(AXES)
    mean = lax.psum(jnp.sum(values, 0), AXES) / total
    centred = values - mean
    spread = lax.psum(jnp.sum(centred * centred, 0), AXES) / total
    return full(wqkv, 0), gr, full(wdn, 0), jnp.stack([mean, lax.rsqrt(spread + EPS)]), gains


def scatter_any(gq0, gq1, gr, gd, terms):
    part = lambda a: lax.psum_scatter(a.astype(f32), AXES, scatter_dimension=0, tiled=True)
    owned = [part(a) for a in (gq0, gq1, gr, gd)]
    small = lax.psum(terms, AXES)
    local = sum(jnp.sum(a * a) for a in owned)
    nsq = lax.psum(local, AXES) + jnp.sum(small * small)
    return *owned, small, jnp.full((8, 128), nsq, f32)


def shards(direct, tag_inputs, image_inputs, tag_counts, cotangent, *params):
    masters, firsts, seconds = params[0:5], params[5:10], params[10:15]
    tables = tag_counts.shape[0]
    devices = lax.axis_size(AXES)
    total_rows = image_inputs.shape[0] * devices
    if direct:
        mixed, gtags, gz, *owned, small, nsq, stats, gains = tables_call(
            True, tag_counts, tag_inputs, image_inputs, cotangent, masters
        )
    else:
        wq, wr, wd, stats, gains = gather_any(image_inputs, *masters)
        mixed, gtags, gz, *sums = tables_call(
            False, tag_counts, tag_inputs, image_inputs, cotangent, (stats, gains, wq, wr, wd)
        )
        *owned, small, nsq = scatter_any(*sums)
    place = jnp.stack([lax.axis_index(AXES), jnp.int32(total_rows)])
    gimg, norm, *rest = update(
        place, gz, image_inputs, stats, gains, small, nsq, owned, masters, firsts, seconds, tables
    )
    return (mixed, gtags, gimg, norm.reshape(()), *rest)


def solution(mesh):
    rows = P(AXES, None)
    state = (rows, rows, rows, rows, P(None, AXES))
    direct = dict(mesh.shape) == {"wide": 16, "narrow": 2}
    return jax.shard_map(
        functools.partial(shards, direct),
        mesh=mesh,
        in_specs=(rows, rows, P(AXES), rows) + state * 3,
        out_specs=(rows, rows, rows, P()) + state * 5,
        check_vma=False,
    )
```

```python
import functools
import math

import jax
import jax.numpy as jnp
from jax import lax
from jax.experimental import pallas as pl
from jax.experimental.pallas import tpu as pltpu
from jax.sharding import PartitionSpec as P

f32 = jnp.float32
bf = jnp.bfloat16
MESH = pl.DeviceIdType.MESH
HEADS = 8
STEP = 10
EPS = 1e-05
NEG = -1000000000.0
CLIP_AT = 1.0
BETA_FIRST = 0.9
BETA_SECOND = 0.999
ADAM_EPS = 1e-08
RATE_MATRIX = 0.05
RATE_OUTPUT = 1.0
RATE_NORMS = 0.5
DECAY_RATE = 0.1
GC = math.sqrt(2 / math.pi)
GA = 0.044715
AXES = ("wide", "narrow")
VM = pl.BlockSpec(memory_space=pltpu.VMEM)


def dg(a, b, ca, cb):
    return lax.dot_general(a, b, (((ca,), (cb,)), ((), ())), preferred_element_type=f32)


class Place:
    def __init__(self):
        self.w = lax.axis_index("wide")
        self.c = lax.axis_index("narrow")
        self.x = lax.rem(self.w, 2)
        self.y = lax.rem(self.w // 2, 2)
        self.z = self.w // 4
        self.d = self.w * 2 + self.c
        self.to_x = (self.w + 1 - 2 * self.x, self.c)
        self.to_y = (self.w + 2 - 4 * self.y, self.c)
        self.sib = (self.w, 1 - self.c)

    def to_z(self, k):
        return (lax.rem(self.w + 4 * k, 16), self.c)

    def peer(self, k):
        d = lax.rem(self.d + k, 32)
        return (d // 2, lax.rem(d, 2))


def greet(me):
    bar = pltpu.get_barrier_semaphore()
    near = (me.sib, me.to_x, me.to_y, me.to_z(1), me.to_z(2), me.to_z(3))
    for dev in near:
        pl.semaphore_signal(bar, inc=1, device_id=dev, device_id_type=MESH)
    pl.semaphore_wait(bar, len(near))


def remote(src, dst, ss, rs, dev):
    return pltpu.make_async_remote_copy(
        src_ref=src, dst_ref=dst, send_sem=ss, recv_sem=rs, device_id=dev, device_id_type=MESH
    )


def mo(a, n):
    return pl.multiple_of(a, n)


class Gather:
    SLOTS = 35

    def __init__(self, me, g, ss, rs, split):
        self.me, self.g, self.ss, self.rs = me, g, ss, rs
        self.rows = g.shape[0] // 32
        n = g.shape[1]
        self.h = n // 2 if split else n
        self.split = split
        self.sent = []

    def ref(self, kz, pos, part=None, c=None):
        me = self.me
        z = lax.rem(me.z + 4 - kz, 4)
        y = me.y if pos in (0, 1) else 1 - me.y
        x = me.x if pos in (0, 2) else 1 - me.x
        d = z * 8 + y * 4 + x * 2 + (me.c if c is None else c)
        rows = pl.ds(mo(d * self.rows, self.rows), self.rows)
        if part is None:
            return self.g.at[rows]
        return self.g.at[rows, pl.ds(part * self.h, self.h)]

    def go(self, kz, pos, part, slot, dev):
        ref = self.ref(kz, pos, part)
        remote(ref, ref, self.ss.at[slot], self.rs.at[slot], dev).start()
        self.sent.append((kz, pos, part, slot))

    def got(self, slot, *key, **kw):
        ref = self.ref(*key, **kw)
        remote(ref, ref, self.ss.at[slot], self.rs.at[slot], self.me.sib).wait_recv()

    def start(self):
        me = self.me
        for k in (2, 1, 3):
            self.go(0, 0, None, k - 1, me.to_z(k))
        self.go(0, 0, None, 3, me.to_x)
        self.go(0, 0, None, 7, me.to_y)
        self.go(0, 0, None, 19, me.sib)

    def column(self):
        me = self.me
        for k in (1, 3, 2):
            self.got(k - 1, k, 0)
            self.go(k, 0, None, 3 + k, me.to_x)
            self.go(k, 0, None, 7 + k, me.to_y)
            self.go(k, 0, None, 19 + k, me.sib)

    def plane(self):
        me = self.me
        for k in (0, 1, 3, 2):
            self.got(3 + k, k, 1)
            self.go(k, 1, 0, 11 + k, me.to_y)
            self.go(k, 1, None, 23 + k, me.sib)
            self.got(7 + k, k, 2)
            if self.split:
                self.go(k, 2, 1, 15 + k, me.to_x)
            self.go(k, 2, None, 27 + k, me.sib)

    def corner(self):
        me = self.me
        for k in (0, 1, 3, 2):
            self.got(11 + k, k, 3, 0)
            if self.split:
                self.got(15 + k, k, 3, 1)
            self.go(k, 3, None, 31 + k, me.sib)

    def finish(self):
        for pos in range(4):
            for k in range(4):
                self.got(19 + 4 * pos + k, k, pos, c=1 - self.me.c)
        for kz, pos, part, slot in self.sent:
            ref = self.ref(kz, pos, part)
            remote(ref, ref, self.ss.at[slot], self.rs.at[slot], self.me.sib).wait_send()


def push_all(me, g, ss, rs):
    for k in range(1, 32):
        remote(g.at[me.d], g.at[me.d], ss.at[k], rs.at[k], me.peer(k)).start()


def push_done(me, g, ss, rs):
    for k in range(1, 32):
        remote(g.at[me.d], g.at[me.d], ss.at[k], rs.at[k], me.sib).wait_send()
        src = lax.rem(me.d + 32 - k, 32)
        remote(g.at[src], g.at[src], ss.at[k], rs.at[k], me.sib).wait_recv()


class Scatter:
    SLOTS = 8

    def __init__(self, me, g, out, bufs, sems):
        self.me, self.g, self.out, (self.ss, self.rs) = me, g, out, sems
        self.r0, self.r1a, self.r1b, self.r2a, self.r2b, self.s2, self.r3 = bufs
        self.s0, self.s1a, self.s1b = self.r0, self.r1a, self.r1b
        self.h = g.shape[-1] // 256 * 128

    @staticmethod
    def bufs(R, N):
        h = N // 256 * 128
        v = lambda *s: pltpu.VMEM(s, bf)
        return [
            v(4, 2, 2, R, N), v(4, 2, R, h), v(4, 2, R, N - h), v(4, R, h), v(4, R, N - h), v(4, R, N), v(3, R, N),
        ]

    def hop(self, slot):
        me, h = self.me, self.h
        n = self.g.shape[-1] - h
        if slot == 0:
            src, dst, dev = self.g.at[:, :, :, 1 - me.c], self.r0, me.sib
        elif slot == 1:
            src, dst, dev = self.s0.at[:, :, 1 - me.x, :, pl.ds(0, h)], self.r1a, me.to_x
        elif slot == 2:
            src, dst, dev = self.s0.at[:, 1 - me.y, :, :, pl.ds(h, n)], self.r1b, me.to_y
        elif slot == 3:
            src, dst, dev = self.s1a.at[:, 1 - me.y], self.r2a, me.to_y
        elif slot == 4:
            src, dst, dev = self.s1b.at[:, 1 - me.x], self.r2b, me.to_x
        else:
            k = slot - 4
            src, dst, dev = self.s2.at[lax.rem(me.z + k, 4)], self.r3.at[k - 1], me.to_z(k)
        return remote(src, dst, self.ss.at[slot], self.rs.at[slot], dev)

    def core(self):
        self.hop(0).start()

    def plane1(self):
        me = self.me
        self.hop(0).wait_recv()

        def add(i, _):
            k = (i // 4, lax.rem(i // 2, 2), lax.rem(i, 2))
            self.s0[k] = (self.g[k + (me.c,)].astype(f32) + self.r0[k].astype(f32)).astype(bf)
            return 0

        lax.fori_loop(0, 16, add, 0)
        self.hop(1).start()
        self.hop(2).start()

    def plane2(self):
        me, h = self.me, self.h
        n = self.g.shape[-1] - h
        self.hop(1).wait_recv()
        self.hop(2).wait_recv()

        def add(i, _):
            z, k = i // 2, lax.rem(i, 2)
            a = self.s0[z, k, me.x, :, pl.ds(0, h)].astype(f32) + self.r1a[z, k].astype(f32)
            self.s1a[z, k] = a.astype(bf)
            b = self.s0[z, me.y, k, :, pl.ds(h, n)].astype(f32) + self.r1b[z, k].astype(f32)
            self.s1b[z, k] = b.astype(bf)
            return 0

        lax.fori_loop(0, 8, add, 0)
        self.hop(3).start()
        self.hop(4).start()

    def column(self):
        me, h = self.me, self.h
        self.hop(3).wait_recv()
        self.hop(4).wait_recv()
        for z in range(4):
            self.s2[z, :, 0:h] = (self.s1a[z, me.y].astype(f32) + self.r2a[z].astype(f32)).astype(bf)
            self.s2[z, :, h:] = (self.s1b[z, me.x].astype(f32) + self.r2b[z].astype(f32)).astype(bf)
        for k in (2, 1, 3):
            self.hop(4 + k).start()

    def finish(self):
        acc = self.s2[self.me.z].astype(f32)
        for k in (1, 2, 3):
            self.hop(4 + k).wait_recv()
            acc += self.r3[k - 1].astype(f32)
        self.out[...] = acc
        for slot in range(8):
            self.hop(slot).wait_send()
        return jnp.sum(acc * acc)


class Sums:
    def __init__(self, me, tb, ss, rs, rows=0):
        self.me, self.tb, self.ss, self.rs, self.rows = me, tb, ss, rs, rows

    def hop(self, slot):
        me = self.me
        src, dst, dev = ((0, 1, me.sib), (2, 3, me.to_x), (4, 5, me.to_y))[slot] if slot < 3 else (
            6 + me.z, 6 + me.z, me.to_z(slot - 2)
        )
        return remote(self.tb.at[src], self.tb.at[dst], self.ss.at[slot], self.rs.at[slot], dev)

    def merge(self, dst, at, rows):
        n = len(at)
        parts = [self.tb[a] for a in at]
        total = parts[0] + parts[1] if n == 2 else (parts[0] + parts[1]) + (parts[2] + parts[3])
        if not self.rows:
            dst[...] = total
            return
        mean = total[6:7] / n
        off = [p[6:7] - mean for p in parts]
        squares = off[0] * off[0] + off[1] * off[1]
        if n == 4:
            squares += off[2] * off[2] + off[3] * off[3]
        dst[0:6] = total[0:6]
        dst[6:7] = mean
        dst[7:8] = total[7:8] + rows * squares

    def step(self, i):
        if i > 0:
            self.hop(i - 1).wait_recv()
            at = 2 * i if i < 3 else 6 + self.me.z
            self.merge(self.tb.at[at], (2 * i - 2, 2 * i - 1), self.rows * 2 ** (i - 1))
        for slot in (i,) if i < 3 else (3, 4, 5):
            self.hop(slot).start()

    def finish(self, dst):
        for k in (1, 2, 3):
            at = self.tb.at[6 + lax.rem(self.me.z + 4 - k, 4)]
            remote(at, at, self.ss.at[2 + k], self.rs.at[2 + k], self.me.sib).wait_recv()
        for slot in range(6):
            self.hop(slot).wait_send()
        self.merge(dst, (6, 7, 8, 9), self.rows * 8)


class Refs:
    pass


def tables_kernel(direct, names, *refs):
    r = Refs()
    for name, ref in zip(names, refs, strict=True):
        setattr(r, name, ref)
    t = pl.program_id(0)
    first = t == 0
    last = t == pl.num_programs(0) - 1
    T, D = r.tag.shape
    I = r.imglow.shape[0]
    NK = T + I
    hd = D // HEADS
    F = r.plow.shape[1]
    r.hidlow, r.rlow, r.hplow = (r.dqkv.at[:, i * D : (i + 1) * D] for i in range(3))
    r.act = r.dkvi.at[0:T]
    r.dqT = r.attT
    count = r.counts[t]
    half = HEADS // 4
    HC = D // 2
    if direct:
        me = Place()
        gat = [
            Gather(me, r.wq, r.gs.at[0], r.gs.at[1], True),
            Gather(me, r.wr, r.gs.at[2], r.gs.at[3], True),
            Gather(me, r.wd, r.gs.at[4], r.gs.at[5], True),
        ]
        sems = [(r.cs.at[2 * i], r.cs.at[2 * i + 1]) for i in range(7)]
        sq0 = Scatter(me, r.gq0, r.oq0, r.bq0, sems[0])
        sq1 = Scatter(me, r.gq1, r.oq1, r.bq1, sems[1])
        sr0 = Scatter(me, r.gr0, r.or0, r.br0, sems[2])
        sr1 = Scatter(me, r.gr1, r.or1, r.br1, sems[3])
        sd = Scatter(me, r.gd, r.od, r.bd, sems[4])
        sm = Sums(me, r.tb, *sems[5])
        ss = Sums(me, r.sb, *sems[6], rows=r.img.shape[0])
    wout_ref = r.wr.at[:, 0:D]
    wup_ref = r.wr.at[:, D : D + F]

    def when_last(*steps):
        @pl.when(last)
        def _():
            for step in steps:
                step()

    def clear():
        for ref in (r.aqkv, r.aout, r.aup, r.adn, r.terms):
            ref[...] = jnp.zeros_like(ref)

    def enter():
        img_in = pltpu.make_async_copy(r.img_hbm, r.img, r.isem)
        img_in.start()
        R, RD = r.pqkv.shape[0], r.pdn.shape[0]
        own = pl.ds(mo(me.d * R, R), R)
        r.wq[own, :] = r.pqkv[...].astype(bf)
        r.wr[own, pl.ds(0, D)] = r.pout[...].astype(bf)
        r.wr[own, pl.ds(D, F)] = r.pup[...].astype(bf)
        r.wd[pl.ds(mo(me.d * RD, RD), RD), :] = r.pdn[...].astype(bf)
        greet(me)
        for g in gat:
            g.start()
        cols = D // 32
        lane = lax.broadcasted_iota(jnp.int32, (cols, D), 1)
        unit = lax.broadcasted_iota(jnp.int32, (cols, D), 0)
        at = (lane == unit + cols * me.d).astype(bf)
        r.sb[0, 0:6, :] = dg(r.pnorm[...].astype(bf), at, 1, 0)
        img_in.wait()
        rows = r.img.shape[0]
        part = 112 if rows % 112 == 0 else I

        def over_rows(f):
            def step(i, acc):
                return acc + f(r.img[pl.ds(mo(i * part, 16), part), :].astype(f32))

            return jnp.sum(lax.fori_loop(0, rows // part, step, jnp.zeros((8, D), f32)), 0, keepdims=True)

        def fold(a):
            return jnp.sum(a.reshape(-1, 8, D), 0)

        mean_d = over_rows(fold) / rows
        m2 = over_rows(lambda a: fold((a - mean_d) * (a - mean_d)))
        r.sb[0, 6:7, :] = mean_d
        r.sb[0, 7:8, :] = m2
        ss.step(0)
        clear()
        ss.step(1)
        gat[0].column()
        ss.step(2)
        gat[0].plane()
        ss.step(3)
        gat[1].column()
        gat[2].column()
        gat[0].corner()
        ss.finish(r.gains)
        r.stats[0:1, :] = r.gains[6:7, :]
        r.stats[1:2, :] = lax.rsqrt(r.gains[7:8, :] / (rows * 32) + EPS)
        gat[0].finish()

    def gather_step(k):
        for g in gat[1:]:
            (g.plane, g.corner, g.finish)[k]()

    pl.when(first)(enter if direct else clear)

    img_ref = r.img.at[pl.ds(mo(t * I, 16), I)] if direct else r.img
    mean = r.stats[0:1, :]
    inv = r.stats[1:2, :]
    g1, b1, g2 = r.gains[0:1, :], r.gains[1:2, :], r.gains[2:3, :]
    b2, gb, bb = r.gains[3:4, :], r.gains[4:5, :], r.gains[5:6, :]
    img_parts = ((0, 256), (256, 256), (512, I - 512))

    for r0, rl in img_parts:
        img_hat = (img_ref[r0 : r0 + rl, :].astype(f32) - mean) * inv
        r.imglow[r0 : r0 + rl, :] = (img_hat * gb + bb).astype(bf)
    for r0 in range(0, T, 256):
        q = dg(r.tag[r0 : r0 + 256, :], r.wq[:, 0:D], 1, 0).astype(bf) * bf(1.0 / math.sqrt(hd))
        r.q[r0 : r0 + 256, :] = q
        r.qT[:, r0 : r0 + 256] = q.T
    key_parts = tuple((r0, 256) for r0 in range(0, T, 256)) + tuple((T + r0, rl) for r0, rl in img_parts)
    for j, dst in enumerate((r.kall, r.vall)):
        w = r.wq[:, (j + 1) * D : (j + 2) * D]
        for k0, kl in key_parts:
            rows = r.tag[k0 : k0 + kl, :] if k0 < T else r.imglow[k0 - T : k0 - T + kl, :]
            a = dg(rows, w, 1, 0).astype(bf)
            dst[k0 : k0 + kl, :] = a
            if j == 1:
                r.xT[:, k0 : k0 + kl] = a.T
    for ref, k0 in ((r.bias0, 0), (r.bias1, 256)):
        ji = k0 + lax.broadcasted_iota(jnp.int32, ref.shape, 0)
        ii = k0 + lax.broadcasted_iota(jnp.int32, ref.shape, 1)
        ref[...] = jnp.where((ji <= ii) & (ji < count), 3e38, NEG).astype(bf)

    if direct:
        pl.when(first)(functools.partial(gather_step, 0))

    chunks = [(0, 256, 0), (256, 256, 256), (512, 256, 0), (768, 256, 0), (1024, NK - 1024, 0)]
    nc = len(chunks)
    row64 = lax.broadcasted_iota(jnp.int32, (2 * hd, 1), 0)
    lane64 = lax.broadcasted_iota(jnp.int32, (1, 2 * hd), 1)

    def own_rows(a, b):
        return jnp.where((row64 < hd) if b == 0 else (row64 >= hd), a, jnp.zeros_like(a))

    def own_lanes(a, b):
        return jnp.where((lane64 < hd) if b == 0 else (lane64 >= hd), a, jnp.zeros_like(a))

    def fullq(a, q0, fill):
        if q0 == 0:
            return a
        return jnp.concatenate([jnp.full((a.shape[0], q0), fill, a.dtype), a], 1)

    def e_at(h, c):
        k0, kl, q0 = chunks[c]
        if q0:
            return r.e1.at[h]
        return r.e.at[h, 0:kl] if k0 == 0 else r.e.at[h, k0 - 256 : k0 - 256 + kl]

    def score(p, b, c, qz):
        k0, kl, q0 = chunks[c]
        ps = pl.ds(mo(p * 2 * hd, 2 * hd), 2 * hd)
        s = dg(r.kall[k0 : k0 + kl, ps], qz[:, q0:], 1, 0)
        if k0 < T:
            s = jnp.minimum(s, (r.bias1 if q0 else r.bias0)[...].astype(f32))
        r.s[k0 : k0 + kl, q0:] = s
        return fullq(jnp.max(s, 0, keepdims=True), q0, NEG)

    def query(p, b):
        return own_rows(r.qT[pl.ds(mo(p * 2 * hd, 2 * hd), 2 * hd), :], b)

    def weigh(p, b, c, m):
        k0, kl, q0 = chunks[c]
        e = jnp.exp(r.s[k0 : k0 + kl, q0:] - m[:, q0:])
        l = jnp.sum(e, 0, keepdims=True)
        e = e.astype(bf)
        e_at(2 * p + b, c)[...] = e
        o = dg(r.xT[pl.ds(mo(p * 2 * hd + b * hd, hd), hd), k0 : k0 + kl], e, 1, 0)
        return fullq(o, q0, 0.0), fullq(l, q0, 0.0)

    def head(p, b, m, following):
        qz = None if following is None else query(*following)
        m2 = None
        o = None
        for c in range(nc):
            oc, lc = weigh(p, b, c, m)
            o, l = (oc, lc) if o is None else (o + oc, l + lc)
            if following is not None:
                mc = score(*following, c, qz)
                m2 = mc if m2 is None else jnp.maximum(m2, mc)
        rl = 1.0 / l
        o = o * rl
        hs = pl.ds(mo(p * 2 * hd + b * hd, hd), hd)
        r.attT[hs, :] = o.astype(bf)
        r.rl[2 * p + b] = rl
        return m2

    def fwd_pair(p, m):
        m = head(p, 0, m, (p, 1))
        m = head(p, 1, m, (jnp.minimum(p + 1, HEADS // 2 - 1), 0))
        if direct:
            pl.when(first & (p == 1))(functools.partial(gather_step, 1))
            pl.when(first & (p == HEADS // 2 - 1))(functools.partial(gather_step, 2))
        return m

    qz = query(0, 0)
    m = None
    for c in range(nc):
        mc = score(0, 0, c, qz)
        m = mc if m is None else jnp.maximum(m, mc)
    lax.fori_loop(0, HEADS // 2, fwd_pair, m)

    RC = 256
    zero = jnp.zeros((1, D), f32)

    def rows_part(r0):
        rs = pl.ds(r0, RC)
        hp = r.tag[rs, :].astype(f32) + dg(r.attT[:, rs], wout_ref[...], 0, 0)
        yield
        c = hp - jnp.mean(hp, -1, keepdims=True)
        inv1 = lax.rsqrt(jnp.mean(c * c, -1, keepdims=True) + EPS)
        hat1 = c * inv1
        hidden = hat1 * g1 + b1
        hl = hidden.astype(bf)
        r.hidlow[rs, :] = hl
        yield
        pre = dg(hl, wup_ref[...], 1, 0)
        yield
        p2 = pre * pre
        th = jnp.tanh(GC * (pre + GA * (p2 * pre)))
        act = (0.5 * pre * (1.0 + th)).astype(bf)
        r.act[rs, :] = act
        gp = 0.5 * (1.0 + th) + 0.5 * pre * (1.0 - th * th) * (GC * (1.0 + 3 * GA * p2))
        yield
        resid = hidden + dg(act, r.wd[...], 1, 0)
        yield
        c = resid - jnp.mean(resid, -1, keepdims=True)
        inv2 = lax.rsqrt(jnp.mean(c * c, -1, keepdims=True) + EPS)
        hat2 = c * inv2
        r.mixed[rs, :] = (hat2 * g2 + b2).astype(bf)
        rows = r0 + lax.broadcasted_iota(jnp.int32, (RC, 1), 0)
        go = jnp.where(rows < count, r.cot[rs, :].astype(f32), 0.0)
        r.terms[2:3, :] += jnp.sum(go * hat2, 0, keepdims=True)
        r.terms[3:4, :] += jnp.sum(go, 0, keepdims=True)
        s = go * g2
        gr = inv2 * (s - jnp.mean(s, -1, keepdims=True) - hat2 * jnp.mean(s * hat2, -1, keepdims=True))
        rlow = gr.astype(bf)
        r.rlow[rs, :] = rlow
        yield
        gact = dg(rlow, r.wd[...], 1, 1)
        yield
        plow = (gact * gp).astype(bf)
        r.plow[rs, :] = plow
        yield
        gh = gr + dg(plow, wup_ref[...], 1, 1)
        yield
        r.terms[0:1, :] += jnp.sum(gh * hat1, 0, keepdims=True)
        r.terms[1:2, :] += jnp.sum(gh, 0, keepdims=True)
        s = gh * g1
        ghp = inv1 * (s - jnp.mean(s, -1, keepdims=True) - hat1 * jnp.mean(s * hat1, -1, keepdims=True))
        r.gtags[rs, :] = ghp
        hpl = ghp.astype(bf)
        r.hplow[rs, :] = hpl
        yield
        r.dOT[:, rs] = dg(hpl, wout_ref[...], 1, 1).astype(bf).T
        yield

    parts = [rows_part(r0) for r0 in range(0, T, RC)]
    for i in range(12 + len(parts) - 1):
        for j, part in enumerate(parts):
            if 0 <= i - j < 12:
                next(part, None)
    for h in range(HEADS):
        hs = slice(h * hd, (h + 1) * hd)
        d = r.dOT[hs, :].astype(f32) * r.rl[h]
        r.dOT[hs, :] = d.astype(bf)
        r.delta[h] = jnp.sum(d * r.attT[hs, :].astype(f32), 0, keepdims=True)
    r.dO[...] = r.dOT[...].T
    for k0, kl in key_parts:
        r.xT[:, k0 : k0 + kl] = r.kall[k0 : k0 + kl, :].T

    def put(dst, acc, r0, rn, c0, cn, add, col=None):
        rs = pl.ds(r0, rn)
        new = acc[rs, c0 : c0 + cn] + add
        acc[rs, c0 : c0 + cn] = new
        col = c0 if col is None else col
        low = new.astype(bf)
        if direct:
            R = dst.shape[4]
            nz = rn // (8 * R)
            dst[pl.ds(r0 // (8 * R), nz), :, :, :, :, col : col + cn] = low.reshape(nz, 2, 2, 2, R, cn)
        else:
            dst[rs, col : col + cn] = low

    for r0 in range(0, F, 256):
        put(r.gd, r.adn, r0, 256, 0, D, dg(r.act[:, r0 : r0 + 256], r.rlow[...], 0, 0))
    for r0 in range(0, D, 256):
        put(r.gr0, r.aout, r0, 256, 0, D, dg(r.attT[r0 : r0 + 256, :], r.hplow[...], 1, 0))
        for c0, cn, dst, col in ((0, 256, r.gr0, D), (256, 512, r.gr1, 0), (768, F - 768, r.gr1, 512)):
            put(dst, r.aup, r0, 256, c0, cn, dg(r.hidlow[:, r0 : r0 + 256], r.plow[:, c0 : c0 + cn], 0, 0), col)
    when_last(sd.core, sr0.core, sr1.core, sd.plane1) if direct else None

    def bwd_pair(p, _):
        p128 = mo(p * 2 * hd, 2 * hd)
        ps = pl.ds(p128, 2 * hd)
        dq = [None, None]
        ops = [(own_rows(r.dOT[ps, :], b), own_lanes(r.dO[:, ps], b), own_lanes(r.q[:, ps], b)) for b in range(2)]
        kc = pl.ds(mo(D + p128, 128), 2 * hd)
        vc = pl.ds(mo(2 * D + p128, 128), 2 * hd)
        for c in range(nc):
            k0, kl, q0 = chunks[c]
            ks = slice(k0, k0 + kl)
            dk = None
            for b in range(2):
                h = 2 * p + b
                hs = pl.ds(mo(p * 2 * hd + b * hd, hd), hd)
                dOz, dOl, ql = ops[b]
                dp = dg(r.vall[ks, ps], dOz[:, q0:], 1, 0)
                e = e_at(h, c)[...]
                ds = (e.astype(f32) * (dp - r.delta[h][:, q0:])).astype(bf)
                dvc = dg(e, dOl[q0:, :], 1, 0)
                dkc = dg(ds, ql[q0:, :], 1, 0)
                dqc = fullq(dg(r.xT[hs, ks], ds, 1, 0), q0, 0.0)
                dk, dv = (dkc, dvc) if dk is None else (dk + dkc, dv + dvc)
                dq[b] = dqc if dq[b] is None else dq[b] + dqc
            if k0 < T:
                r.dqkv[ks, kc] = dk.astype(bf)
                r.dqkv[ks, vc] = dv.astype(bf)
            else:
                si = slice(k0 - T, k0 - T + kl)
                r.dkvi[si, ps] = dk.astype(bf)
                r.dkvi[si, kc] = dv.astype(bf)
        for b in range(2):
            hs = pl.ds(mo(p * 2 * hd + b * hd, hd), hd)
            r.dqT[hs, :] = (dq[b] * (1.0 / math.sqrt(hd))).astype(bf)
        if direct:
            for k, steps in enumerate(
                ((sr0.plane1, sr1.plane1), (sd.plane2,), (sr1.plane2, sq0.plane1, sd.column), (sr0.column,))
            ):

                @pl.when(last & (p == k))
                def _():
                    for step in steps:
                        step()

        return 0

    for i, gq in enumerate((r.gq0, r.gq1)):
        lax.fori_loop(i * half, (i + 1) * half, bwd_pair, 0)
        hc = slice(i * HC, (i + 1) * HC)
        r.dqkv[:, hc] = r.dqT[hc, :].T
        for r0 in range(0, D, 256):
            rs = slice(r0, r0 + 256)
            x = r.tag[:, rs]
            put(gq, r.aqkv, r0, 256, i * HC, HC, dg(x, r.dqkv[:, hc], 0, 0), 0)
            for j in (1, 2):
                cs = slice(j * D + i * HC, j * D + (i + 1) * HC)
                ci = slice(cs.start - D, cs.stop - D)
                add = dg(x, r.dqkv[:, cs], 0, 0) + dg(r.imglow[:, rs], r.dkvi[:, ci], 0, 0)
                put(gq, r.aqkv, r0, 256, cs.start, HC, add, j * HC)
        if direct:
            when_last(*((sq0.core, sr0.plane2), (sq1.core,))[i])

    sg = jnp.zeros((1, D), f32)
    sb = sg
    for r0, rl in img_parts:
        rs = slice(r0, r0 + rl)
        gz = dg(r.dkvi[rs, :], r.wq[:, D:], 1, 1)
        r.gz[rs, :] = gz.astype(bf)
        hat = (img_ref[rs, :].astype(f32) - mean) * inv
        sg += jnp.sum(gz * hat, 0, keepdims=True)
        sb += jnp.sum(gz, 0, keepdims=True)
    r.terms[4:5, :] += sg
    r.terms[5:6, :] += sb
    if direct:

        @pl.when(last)
        def _():
            r.tb[0] = r.terms[...]
            sm.step(0)
            sq0.plane2()

    for r0 in range(0, T, 256):
        r.gtags[r0 : r0 + 256, :] += dg(r.dqkv[r0 : r0 + 256, :], r.wq[...], 1, 1)

    if direct:

        @pl.when(last)
        def _():
            sq1.plane1()
            sm.step(1)
            sr1.column()
            sq = sd.finish()
            sq += sr0.finish()
            sm.step(2)
            sq0.column()
            sq += sr1.finish()
            sq1.plane2()
            sm.step(3)
            sq += sq0.finish()
            sq1.column()
            sm.finish(r.small)
            tot = r.small[...]
            sq += sq1.finish()
            r.nb[me.d] = jnp.full((1, 128), sq, f32)
            push_all(me, r.nb, r.ps.at[0], r.ps.at[1])
            push_done(me, r.nb, r.ps.at[0], r.ps.at[1])
            r.nsq[...] = jnp.broadcast_to(jnp.sum(r.nb[...], 0) + jnp.sum(tot * tot), (8, 128))


def tables_call(direct, counts, tag, img, cot, params):
    n = counts.shape[0]
    T, I, D = tag.shape[0] // n, img.shape[0] // n, tag.shape[1]
    NK = T + I
    HC = D // 2
    V = lambda *s, d=bf: pltpu.VMEM(s, d)
    S = jax.ShapeDtypeStruct

    def row(a, b):
        return pl.BlockSpec((a, b), lambda t, *_: (t, 0))

    def whole(shape, **kw):
        return pl.BlockSpec(shape, lambda t, *_: (0,) * len(shape), **kw)

    one = dict(pipeline_mode=pl.Buffered(1))
    if direct:
        F = params[2].shape[1]
        R, RD = params[0].shape[0], params[3].shape[0]
        ins = [("tag", row(T, D)), ("img_hbm", pl.BlockSpec(memory_space=pl.ANY)), ("cot", row(T, D))]
        ins += [(k, whole(a.shape, **one)) for k, a in zip(("pqkv", "pout", "pup", "pdn", "pnorm"), params)]
    else:
        F = params[4].shape[0]
        ins = [("tag", row(T, D)), ("img", row(I, D)), ("cot", row(T, D))]
        ins += [(k, whole(a.shape, **one)) for k, a in zip(("stats", "gains", "wq", "wr", "wd"), params)]
    outs = [
        ("mixed", S((n * T, D), bf), row(T, D)),
        ("gtags", S((n * T, D), f32), row(T, D)),
        ("gz", S((n * I, D), bf), row(I, D)),
    ]
    scratch = [
        ("imglow", V(I, D)), ("kall", V(NK, D)), ("vall", V(NK, D)), ("xT", V(D, NK)),
        ("q", V(T, D)), ("qT", V(D, T)), ("bias0", V(256, T)), ("bias1", V(256, T - 256)), ("s", V(NK, T, d=f32)),
        ("e", V(HEADS, NK - 256, T)), ("e1", V(HEADS, 256, T - 256)), ("attT", V(D, T)),
        ("rl", V(HEADS, 1, T, d=f32)), ("plow", V(T, F)),
        ("dqkv", V(T, 3 * D)), ("dkvi", V(I, 2 * D)), ("dO", V(T, D)),
        ("dOT", V(D, T)), ("delta", V(HEADS, 1, T, d=f32)), ("aqkv", V(D, 3 * D, d=f32)), ("aout", V(D, D, d=f32)),
        ("aup", V(D, F, d=f32)), ("adn", V(F, D, d=f32)),
    ]
    if direct:
        outs += [
            ("oq0", S((R, 3 * HC), f32), None), ("oq1", S((R, 3 * HC), f32), None), ("or0", S((R, 3 * HC), f32), None),
            ("or1", S((R, D + F - 3 * HC), f32), None), ("od", S((RD, D), f32), None), ("small", S((8, D), f32), None), ("nsq", S((8, 128), f32), None),
            ("stats", S((2, D), f32), None), ("gains", S((8, D), f32), None),
        ]
        dims = (4, 2, 2, 2)
        dma = pltpu.SemaphoreType.DMA
        scratch += [
            ("img", V(n * I, D)), ("wq", V(D, 3 * D)), ("wr", V(D, D + F)), ("wd", V(F, D)), ("sb", V(10, 8, D, d=f32)),
            ("nb", V(32, 1, 128, d=f32)), ("terms", V(8, D, d=f32)), ("tb", V(10, 8, D, d=f32)),
            ("gq0", V(*dims, R, 3 * HC)), ("gq1", V(*dims, R, 3 * HC)), ("gr0", V(*dims, R, 3 * HC)),
            ("gr1", V(*dims, R, D + F - 3 * HC)), ("gd", V(*dims, RD, D)),
            ("bq0", Scatter.bufs(R, 3 * HC)), ("bq1", Scatter.bufs(R, 3 * HC)), ("br0", Scatter.bufs(R, 3 * HC)),
            ("br1", Scatter.bufs(R, D + F - 3 * HC)),
            ("bd", Scatter.bufs(RD, D)),
            ("isem", dma), ("gs", dma((6, Gather.SLOTS))), ("cs", dma((14, Scatter.SLOTS))), ("ps", dma((2, 32))),
        ]
        extra = dict(collective_id=0, has_side_effects=True)
    else:
        outs += [
            ("gq0", S((D, 3 * HC), bf), None), ("gq1", S((D, 3 * HC), bf), None), ("gr0", S((D, 3 * HC), bf), None),
            ("gr1", S((D, D + F - 3 * HC), bf), None),
            ("gd", S((F, D), bf), None), ("terms", S((8, D), f32), None),
        ]
        extra = {}
    names = ("counts",) + tuple(k for k, _ in ins) + tuple(k for k, _, _ in outs) + tuple(k for k, _ in scratch)
    return pl.pallas_call(
        functools.partial(tables_kernel, direct, names),
        out_shape=[s for _, s, _ in outs],
        grid_spec=pltpu.PrefetchScalarGridSpec(
            num_scalar_prefetch=1,
            grid=(n,),
            in_specs=[b for _, b in ins],
            out_specs=[whole(s.shape) if b is None else b for _, s, b in outs],
            scratch_shapes=[a for _, a in scratch],
        ),
        compiler_params=pltpu.CompilerParams(vmem_limit_bytes=63 * 2**20, **extra),
        name="tables",
    )(counts, tag, img, cot, *params)


def update_kernel(n_params, parts, place, gz_in, img_in, stats_ref, gains_ref, small_ref, nsq_ref, *refs):
    n_in = 5 + 3 * n_params
    n_out = 5 * n_params
    hbm_in, (mixed_in, gtags_in), refs = refs[:n_in], refs[n_in : n_in + 2], refs[n_in + 2 :]
    (mixed_out, gtags_out, gimg_out, norm_ref), refs = refs[:4], refs[4:]
    hbm_out, refs = refs[:n_out], refs[n_out:]
    ins, outs, refs = refs[:n_in], refs[n_in : n_in + n_out], refs[n_in + n_out :]
    mixed, gtags, gz, img, gimg, in_sem, out_sem, pass_sem, part_sem = refs
    rows, D = gz.shape
    copy = pltpu.make_async_copy

    def part(i):
        at = pl.ds(i * (rows // parts), rows // parts)
        return at, copy(gz_in.at[at], gz.at[at], part_sem.at[0, i]), copy(img_in.at[at], img.at[at], part_sem.at[1, i])

    def given(i):
        at = pl.ds(i * (rows // parts), rows // parts)
        return copy(gimg.at[at], gimg_out.at[at], part_sem.at[2, i])

    for i in range(parts):
        _, a, b = part(i)
        a.start()
        b.start()
    for i, (a, b) in enumerate(((gtags_in, gtags), (mixed_in, mixed))):
        copy(a, b, pass_sem.at[i]).start()
    for i, (a, b) in enumerate(zip(hbm_in, ins)):
        copy(a, b, in_sem.at[i]).start()

    total_rows = place[1].astype(f32)
    gb = gains_ref[4:5, :]
    k = stats_ref[1:2, :] * gb
    gsum = small_ref[4:5, :] / total_rows
    bsum = small_ref[5:6, :] / total_rows
    for i in range(parts):
        at, a, b = part(i)
        a.wait()
        b.wait()
        hat = (img[at, :].astype(f32) - stats_ref[0:1, :]) * stats_ref[1:2, :]
        gimg[at, :] = k * (gz[at, :].astype(f32) - bsum - hat * gsum)
        given(i).start()
    for i, (a, b, c) in enumerate(((gtags_in, gtags, gtags_out), (mixed_in, mixed, mixed_out))):
        copy(a, b, pass_sem.at[i]).wait()
        copy(b, c, pass_sem.at[2 + i]).start()

    for i, (a, b) in enumerate(zip(hbm_in, ins)):
        copy(a, b, in_sem.at[i]).wait()
    oq0, oq1, or0, or1, od = ins[:5]
    masters, firsts, seconds = (ins[5 + n_params * i : 5 + n_params * (i + 1)] for i in range(3))
    total_norm = jnp.sqrt(nsq_ref[0:1, 0:1])
    norm_ref[...] = total_norm
    factor = CLIP_AT / jnp.maximum(total_norm, CLIP_AT)
    cols = masters[4].shape[1]
    row = lax.broadcasted_iota(jnp.int32, (D, cols), 0)
    col = lax.broadcasted_iota(jnp.int32, (D, cols), 1)
    pick = (row == col + place[0] * cols).astype(f32)
    own = lax.dot_general(
        small_ref[...], pick, (((1,), (0,)), ((), ())), precision=lax.Precision.HIGHEST, preferred_element_type=f32
    )[0:6]
    hc = D // 2
    oq = [o[:, j * hc : (j + 1) * hc] for j in range(3) for o in (oq0, oq1)]
    grads = (jnp.concatenate(oq, 1), or0[:, 0:D], jnp.concatenate([or0[:, D:], or1[...]], 1), od[...], own)
    rates = (RATE_MATRIX, RATE_OUTPUT, RATE_MATRIX, RATE_MATRIX, RATE_NORMS)
    for i, (g, w, f, v) in enumerate(zip(grads, masters, firsts, seconds)):
        clip = g * factor
        moment = BETA_FIRST * f[...] + (1.0 - BETA_FIRST) * clip
        square = BETA_SECOND * v[...] + (1.0 - BETA_SECOND) * clip * clip
        u = (moment / (1.0 - BETA_FIRST**STEP)) / (jnp.sqrt(square / (1.0 - BETA_SECOND**STEP)) + ADAM_EPS)
        if i < 4:
            new = w[...] - rates[i] * (u + DECAY_RATE * w[...])
        else:
            new = w[...] - rates[i] * u
        for j, value in enumerate((clip, moment, square, new, new.astype(bf))):
            at = 5 * j + i
            outs[at][...] = value
            copy(outs[at], hbm_out[at], out_sem.at[at]).start()

    for i in range(n_out):
        copy(outs[i], hbm_out[i], out_sem.at[i]).wait()
    for i, (b, c) in enumerate(((gtags, gtags_out), (mixed, mixed_out))):
        copy(b, c, pass_sem.at[2 + i]).wait()
    for i in range(parts):
        given(i).wait()


def update(place, mixed, gtags, gz, img, stats, gains, small, nsq, owned, masters, firsts, seconds):
    rows = gz.shape[0]
    parts = 7 if rows % 112 == 0 else 3
    anywhere = pl.BlockSpec(memory_space=pl.ANY)
    windows = (stats, gains, small, nsq)
    manual = tuple(owned) + tuple(masters) + tuple(firsts) + tuple(seconds)
    shapes = [jax.ShapeDtypeStruct(m.shape, f32) for m in masters] * 4 + [jax.ShapeDtypeStruct(m.shape, bf) for m in masters]
    gimg = jax.ShapeDtypeStruct(gz.shape, f32)
    dma = pltpu.SemaphoreType.DMA
    passed = [jax.ShapeDtypeStruct(a.shape, a.dtype) for a in (mixed, gtags)]
    return pl.pallas_call(
        functools.partial(update_kernel, len(masters), parts),
        out_shape=passed + [gimg, jax.ShapeDtypeStruct((1, 1), f32)] + shapes,
        in_specs=[pl.BlockSpec(memory_space=pltpu.SMEM)] + [anywhere] * 2 + [VM] * 4 + [anywhere] * (len(manual) + 2),
        out_specs=[anywhere] * 3 + [VM] + [anywhere] * len(shapes),
        scratch_shapes=[pltpu.VMEM(a.shape, a.dtype) for a in manual + tuple(shapes) + tuple(passed) + (gz, img, gimg)]
        + [dma((len(manual),)), dma((len(shapes),)), dma((4,)), dma((3, parts))],
        compiler_params=pltpu.CompilerParams(vmem_limit_bytes=63 * 2**20),
        name="update",
    )(place, gz, img, *windows, *manual, mixed, gtags)


def gather_any(img, wqkv, wout, wup, wdn, norm):
    full = lambda a, axis: lax.all_gather(a.astype(bf), AXES, axis=axis, tiled=True)
    gr = jnp.concatenate([full(wout, 0), full(wup, 0)], 1)
    gains = jnp.concatenate([full(norm, 1).astype(f32), jnp.zeros((2, img.shape[1]), f32)], 0)
    values = img.astype(f32)
    total = img.shape[0] * lax.axis_size(AXES)
    mean = lax.psum(jnp.sum(values, 0), AXES) / total
    centred = values - mean
    spread = lax.psum(jnp.sum(centred * centred, 0), AXES) / total
    return full(wqkv, 0), gr, full(wdn, 0), jnp.stack([mean, lax.rsqrt(spread + EPS)]), gains


def scatter_any(gq0, gq1, gr0, gr1, gd, terms):
    part = lambda a: lax.psum_scatter(a.astype(f32), AXES, scatter_dimension=0, tiled=True)
    owned = [part(a) for a in (gq0, gq1, gr0, gr1, gd)]
    small = lax.psum(terms, AXES)
    local = sum(jnp.sum(a * a) for a in owned)
    nsq = lax.psum(local, AXES) + jnp.sum(small * small)
    return *owned, small, jnp.full((8, 128), nsq, f32)


def shards(direct, tag_inputs, image_inputs, tag_counts, cotangent, *params):
    masters, firsts, seconds = params[0:5], params[5:10], params[10:15]
    tables = tag_counts.shape[0]
    devices = lax.axis_size(AXES)
    total_rows = image_inputs.shape[0] * devices
    if direct:
        mixed, gtags, gz, *owned, small, nsq, stats, gains = tables_call(
            True, tag_counts, tag_inputs, image_inputs, cotangent, masters
        )
    else:
        wq, wr, wd, stats, gains = gather_any(image_inputs, *masters)
        mixed, gtags, gz, *sums = tables_call(
            False, tag_counts, tag_inputs, image_inputs, cotangent, (stats, gains, wq, wr, wd)
        )
        *owned, small, nsq = scatter_any(*sums)
    place = jnp.stack([lax.axis_index(AXES), jnp.int32(total_rows)])
    mixed, gtags, gimg, norm, *rest = update(
        place, mixed, gtags, gz, image_inputs, stats, gains, small, nsq, owned, masters, firsts, seconds
    )
    return (mixed, gtags, gimg, norm.reshape(()), *rest)


def solution(mesh):
    rows = P(AXES, None)
    state = (rows, rows, rows, rows, P(None, AXES))
    direct = dict(mesh.shape) == {"wide": 16, "narrow": 2}
    return jax.shard_map(
        functools.partial(shards, direct),
        mesh=mesh,
        in_specs=(rows, rows, P(AXES), rows) + state * 3,
        out_specs=(rows, rows, rows, P()) + state * 5,
        check_vma=False,
    )
```

```python
import functools
import math

import jax
import jax.numpy as jnp
from jax import lax
from jax.experimental import pallas as pl
from jax.experimental.pallas import tpu as pltpu
from jax.sharding import PartitionSpec as P

f32 = jnp.float32
bf = jnp.bfloat16
MESH = pl.DeviceIdType.MESH
HEADS = 8
STEP = 10
EPS = 1e-05
NEG = -1000000000.0
CLIP_AT = 1.0
BETA_FIRST = 0.9
BETA_SECOND = 0.999
ADAM_EPS = 1e-08
RATE_MATRIX = 0.05
RATE_OUTPUT = 1.0
RATE_NORMS = 0.5
DECAY_RATE = 0.1
GC = math.sqrt(2 / math.pi)
GA = 0.044715
AXES = ("wide", "narrow")
VM = pl.BlockSpec(memory_space=pltpu.VMEM)


def dg(a, b, ca, cb):
    return lax.dot_general(a, b, (((ca,), (cb,)), ((), ())), preferred_element_type=f32)


class Place:
    def __init__(self):
        self.w = lax.axis_index("wide")
        self.c = lax.axis_index("narrow")
        self.x = lax.rem(self.w, 2)
        self.y = lax.rem(self.w // 2, 2)
        self.z = self.w // 4
        self.d = self.w * 2 + self.c
        self.to_x = (self.w + 1 - 2 * self.x, self.c)
        self.to_y = (self.w + 2 - 4 * self.y, self.c)
        self.to_d = (self.w + 3 - 2 * self.x - 4 * self.y, self.c)
        self.sib = (self.w, 1 - self.c)

    def to_z(self, k):
        return (lax.rem(self.w + 4 * k, 16), self.c)

    def peer(self, k):
        d = lax.rem(self.d + k, 32)
        return (d // 2, lax.rem(d, 2))


def greet(me):
    bar = pltpu.get_barrier_semaphore()
    near = (me.sib, me.to_x, me.to_y, me.to_d, me.to_z(1), me.to_z(2), me.to_z(3))
    for dev in near:
        pl.semaphore_signal(bar, inc=1, device_id=dev, device_id_type=MESH)
    pl.semaphore_wait(bar, len(near))


def remote(src, dst, ss, rs, dev):
    return pltpu.make_async_remote_copy(
        src_ref=src, dst_ref=dst, send_sem=ss, recv_sem=rs, device_id=dev, device_id_type=MESH
    )


def mo(a, n):
    return pl.multiple_of(a, n)


class Gather:
    SLOTS = 23

    def __init__(self, me, g, ss, rs):
        self.me, self.g, self.ss, self.rs = me, g, ss, rs
        self.h = g.shape[-1] // 2
        self.sent = []

    def ref(self, k, pos, part=None, c=None):
        me = self.me
        z = slice(None) if k is None else lax.rem(me.z + 4 - k, 4)
        y = me.y if pos in (0, 1) else 1 - me.y
        x = me.x if pos in (0, 2) else 1 - me.x
        at = (z, y, x, me.c if c is None else c)
        return self.g.at[at] if part is None else self.g.at[at + (slice(None), pl.ds(part * self.h, self.h))]

    def go(self, k, pos, part, slot, dev):
        ref = self.ref(k, pos, part)
        remote(ref, ref, self.ss.at[slot], self.rs.at[slot], dev).start()
        self.sent.append((k, pos, part, slot))

    def got(self, slot, *key, **kw):
        ref = self.ref(*key, **kw)
        remote(ref, ref, self.ss.at[slot], self.rs.at[slot], self.me.sib).wait_recv()

    def start(self):
        me = self.me
        for k in (2, 1, 3):
            self.go(0, 0, None, k - 1, me.to_z(k))
        self.go(0, 0, None, 3, me.to_x)
        self.go(0, 0, None, 7, me.to_y)

    def share(self, pos):
        self.go(None, pos, None, 19 + pos, self.me.sib)

    def column(self, *ks):
        me = self.me
        for k in ks:
            self.got(k - 1, k, 0)
            self.go(k, 0, None, 3 + k, me.to_x)
            self.go(k, 0, None, 7 + k, me.to_y)

    def plane(self, *ks):
        me = self.me
        for k in ks:
            self.got(3 + k, k, 1)
            self.go(k, 1, 0, 11 + k, me.to_y)
            self.got(7 + k, k, 2)
            self.go(k, 2, 1, 15 + k, me.to_x)

    def corner(self, *ks):
        for k in ks:
            self.got(11 + k, k, 3, 0)
            self.got(15 + k, k, 3, 1)

    def finish(self):
        for pos in range(4):
            self.got(19 + pos, None, pos, c=1 - self.me.c)
        for k, pos, part, slot in self.sent:
            ref = self.ref(k, pos, part)
            remote(ref, ref, self.ss.at[slot], self.rs.at[slot], self.me.sib).wait_send()


def push_all(me, g, ss, rs):
    for k in range(1, 32):
        remote(g.at[me.d], g.at[me.d], ss, rs, me.peer(k)).start()
    all_of = remote(g.at[pl.ds(0, 31)], g.at[pl.ds(0, 31)], ss, rs, me.sib)
    all_of.wait_send()
    all_of.wait_recv()


class Scatter:
    SLOTS = 8

    def __init__(self, me, g, out, bufs, sems):
        self.me, self.g, self.out, (self.ss, self.rs) = me, g, out, sems
        self.r0, self.r1a, self.r1b, self.r2a, self.r2b, self.s2, self.r3 = bufs
        self.s0, self.s1a, self.s1b = self.r0, self.r1a, self.r1b
        self.h = g.shape[-1] // 256 * 128

    @staticmethod
    def bufs(R, N):
        h = N // 256 * 128
        v = lambda *s: pltpu.VMEM(s, bf)
        return [
            v(4, 2, 2, R, N), v(4, 2, R, h), v(4, 2, R, N - h), v(4, R, h), v(4, R, N - h), v(4, R, N), v(3, R, N),
        ]

    def hop(self, slot):
        me = self.me
        if slot in (1, 2):
            h = self.h
            n = self.g.shape[-1] - h
        if slot == 0:
            src, dst, dev = self.g.at[:, :, :, 1 - me.c], self.r0, me.sib
        elif slot == 1:
            src, dst, dev = self.s0.at[:, :, 1 - me.x, :, pl.ds(0, h)], self.r1a, me.to_x
        elif slot == 2:
            src, dst, dev = self.s0.at[:, 1 - me.y, :, :, pl.ds(h, n)], self.r1b, me.to_y
        elif slot == 3:
            src, dst, dev = self.s1a.at[:, 1 - me.y], self.r2a, me.to_y
        elif slot == 4:
            src, dst, dev = self.s1b.at[:, 1 - me.x], self.r2b, me.to_x
        else:
            k = slot - 4
            src, dst, dev = self.s2.at[lax.rem(me.z + k, 4)], self.r3.at[k - 1], me.to_z(k)
        return remote(src, dst, self.ss.at[slot], self.rs.at[slot], dev)

    def core(self):
        self.hop(0).start()

    slots = tuple(range(8))

    def first_sum(self):
        me = self.me
        self.hop(0).wait_recv()

        for z in range(4):
            self.s0[z] = self.g[z, :, :, me.c] + self.r0[z]

    def plane1(self):
        self.first_sum()
        self.hop(1).start()
        self.hop(2).start()

    def plane2(self):
        me, h = self.me, self.h
        n = self.g.shape[-1] - h
        self.hop(1).wait_recv()
        self.hop(2).wait_recv()

        for z in range(4):
            self.s1a[z] = self.s0[z, :, me.x, :, pl.ds(0, h)] + self.r1a[z]
            self.s1b[z] = self.s0[z, me.y, :, :, pl.ds(h, n)] + self.r1b[z]
        self.hop(3).start()
        self.hop(4).start()

    def column(self):
        me, h = self.me, self.h
        self.hop(3).wait_recv()
        self.hop(4).wait_recv()
        for z in range(4):
            self.s2[z, :, 0:h] = self.s1a[z, me.y] + self.r2a[z]
            self.s2[z, :, h:] = self.s1b[z, me.x] + self.r2b[z]
        for k in (2, 1, 3):
            self.hop(4 + k).start()

    def finish(self):
        acc = self.s2[self.me.z].astype(f32)
        for k in (1, 2, 3):
            self.hop(4 + k).wait_recv()
            acc += self.r3[k - 1].astype(f32)
        self.out[...] = acc
        for slot in self.slots:
            self.hop(slot).wait_send()
        return jnp.sum(acc * acc)


class ScatterPlane(Scatter):
    def __init__(self, me, g, out, bufs, sems):
        self.me, self.g, self.out, (self.ss, self.rs) = me, g, out, sems
        self.r0, self.rp, self.s2, self.r3 = bufs
        self.s0 = self.r0

    @staticmethod
    def bufs(R, N):
        v = lambda *s: pltpu.VMEM(s, bf)
        return [v(4, 2, 2, R, N), v(3, 4, R, N), v(4, R, N), v(3, R, N)]

    def hop(self, slot):
        me = self.me
        if slot in (0, 5, 6, 7):
            return Scatter.hop(self, slot)
        y = me.y if slot == 1 else 1 - me.y
        x = me.x if slot == 2 else 1 - me.x
        dev = (me.to_x, me.to_y, me.to_d)[slot - 1]
        return remote(self.s0.at[:, y, x], self.rp.at[slot - 1], self.ss.at[slot], self.rs.at[slot], dev)

    def plane1(self):
        self.first_sum()
        for slot in (3, 1, 2):
            self.hop(slot).start()

    def column(self):
        me = self.me
        for slot in (1, 2, 3):
            self.hop(slot).wait_recv()
        for z in range(4):
            total = self.s0[z, me.y, me.x].astype(f32)
            for i in range(3):
                total += self.rp[i, z].astype(f32)
            self.s2[z] = total.astype(bf)
        for k in (2, 1, 3):
            self.hop(4 + k).start()

    slots = (0, 1, 2, 3, 5, 6, 7)


class Sums:
    def __init__(self, me, tb, ss, rs, rows=0):
        self.me, self.tb, self.ss, self.rs, self.rows = me, tb, ss, rs, rows

    def hop(self, slot):
        me = self.me
        if slot == 0:
            src, dst, dev = 0, 1, me.sib
        elif slot < 4:
            src = dst = 2 + me.y * 2 + me.x
            dev = (me.to_x, me.to_y, me.to_d)[slot - 1]
        else:
            src = dst = 6 + me.z
            dev = me.to_z(slot - 3)
        return remote(self.tb.at[src], self.tb.at[dst], self.ss.at[slot], self.rs.at[slot], dev)

    def arrived(self, slot):
        me = self.me
        y = me.y if slot == 1 else 1 - me.y
        x = me.x if slot == 2 else 1 - me.x
        at = 1 if slot == 0 else 2 + y * 2 + x if slot < 4 else 6 + lax.rem(me.z + 7 - slot, 4)
        at = self.tb.at[at]
        remote(at, at, self.ss.at[slot], self.rs.at[slot], me.sib).wait_recv()

    def merge(self, dst, at, rows):
        n = len(at)
        parts = [self.tb[a] for a in at]
        total = parts[0] + parts[1] if n == 2 else (parts[0] + parts[1]) + (parts[2] + parts[3])
        if not self.rows:
            dst[...] = total
            return
        mean = total[6:7] / n
        off = [p[6:7] - mean for p in parts]
        squares = off[0] * off[0] + off[1] * off[1]
        if n == 4:
            squares += off[2] * off[2] + off[3] * off[3]
        dst[0:6] = total[0:6]
        dst[6:7] = mean
        dst[7:8] = total[7:8] + rows * squares

    def step(self, i):
        me = self.me
        if i == 1:
            self.arrived(0)
            self.merge(self.tb.at[2 + me.y * 2 + me.x], (0, 1), self.rows)
        if i == 2:
            for slot in (1, 2, 3):
                self.arrived(slot)
            self.merge(self.tb.at[6 + me.z], (2, 3, 4, 5), self.rows * 2)
        for slot in ((0,), (3, 1, 2), (4, 5, 6))[i]:
            self.hop(slot).start()

    def finish(self, dst):
        for slot in (4, 5, 6):
            self.arrived(slot)
        for slot in range(7):
            self.hop(slot).wait_send()
        self.merge(dst, (6, 7, 8, 9), self.rows * 8)


class Refs:
    pass


def tables_kernel(direct, names, *refs):
    r = Refs()
    for name, ref in zip(names, refs, strict=True):
        setattr(r, name, ref)
    t = pl.program_id(0)
    first = t == 0
    last = t == pl.num_programs(0) - 1
    T, D = r.tag.shape
    I = r.imglow.shape[0]
    NK = T + I
    hd = D // HEADS
    F = r.plow.shape[1]
    r.hidlow, r.rlow, r.hplow = (r.dqkv.at[:, i * D : (i + 1) * D] for i in range(3))
    r.act = r.dkvi.at[0:T]
    r.dqT = r.attT
    count = r.counts[t]
    HC = D // 2
    if direct:
        me = Place()
        gq, gw = Gather(me, r.wq, r.gs.at[0], r.gs.at[1]), Gather(me, r.ww, r.gs.at[2], r.gs.at[3])
        sems = [(r.cs.at[2 * i], r.cs.at[2 * i + 1]) for i in range(8)]
        sq0 = Scatter(me, r.gq0, r.oq0, r.bq0, sems[0])
        sq1 = Scatter(me, r.gq1, r.oq1, r.bq1, sems[1])
        sq2 = ScatterPlane(me, r.gq2, r.oq2, r.bq2, sems[7])
        sr0 = Scatter(me, r.gr0, r.or0, r.br0, sems[2])
        sr1 = Scatter(me, r.gr1, r.or1, r.br1, sems[3])
        sd = Scatter(me, r.gd, r.od, r.bd, sems[4])
        sm = Sums(me, r.tb, *sems[5])
        ss = Sums(me, r.sb, *sems[6], rows=r.img.shape[0])
    def cols(ref, a, b):
        if not direct:
            return ref[:, a:b]
        return ref[:, :, :, :, :, a:b].reshape(D, b - a)

    def w_qkv(a, b):
        return cols(r.wq, a, b)

    def w_out():
        return cols(r.ww if direct else r.wr, 0, D)

    def w_up():
        return cols(r.ww if direct else r.wr, D, D + F)

    def w_down():
        if not direct:
            return r.wd[...]
        halves = [r.ww[:, :, :, :, :, a : a + D] for a in (D + F, 2 * D + F)]
        return jnp.stack(halves, 4).reshape(F, D)

    def when_last(*steps):
        @pl.when(last)
        def _():
            for step in steps:
                step()

    def clear():
        for ref in (r.aqkv, r.aout, r.aup, r.adn, r.terms):
            ref[...] = jnp.zeros_like(ref)

    def enter():
        img_in = pltpu.make_async_copy(r.img_hbm, r.img, r.isem)
        img_in.start()
        R, RD = r.pqkv.shape[0], r.pdn.shape[0]
        own = (me.z, me.y, me.x, me.c)
        r.wq[own + (slice(None), pl.ds(0, D))] = r.pqkv[:, 0:D].astype(bf)
        for p in range(HEADS // 2):
            for j in (0, 1):
                at = (j + 1) * D + p * 2 * hd
                to = pl.ds(D + (2 * p + j) * 2 * hd, 2 * hd)
                r.wq[own + (slice(None), to)] = r.pqkv[:, at : at + 2 * hd].astype(bf)
        greet(me)
        gq.start()
        for at, part in ((0, r.pout[...]), (D, r.pup[...]), (D + F, r.pdn[0:R, :]), (2 * D + F, r.pdn[R:RD, :])):
            r.ww[own + (slice(None), pl.ds(at, part.shape[1]))] = part.astype(bf)
        gw.start()
        share = D // 32
        lane = lax.broadcasted_iota(jnp.int32, (share, D), 1)
        unit = lax.broadcasted_iota(jnp.int32, (share, D), 0)
        at = (lane == unit + share * me.d).astype(bf)
        r.sb[0, 0:6, :] = dg(r.pnorm[...].astype(bf), at, 1, 0)
        img_in.wait()
        rows = r.img.shape[0]
        part = 112 if rows % 112 == 0 else I

        def over_rows(f):
            def step(i, acc):
                return acc + f(r.img[pl.ds(mo(i * part, 16), part), :].astype(f32))

            return jnp.sum(lax.fori_loop(0, rows // part, step, jnp.zeros((8, D), f32)), 0, keepdims=True)

        def fold(a):
            return jnp.sum(a.reshape(-1, 8, D), 0)

        mean_d = over_rows(fold) / rows
        m2 = over_rows(lambda a: fold((a - mean_d) * (a - mean_d)))
        r.sb[0, 6:7, :] = mean_d
        r.sb[0, 7:8, :] = m2
        ss.step(0)
        clear()
        ss.step(1)
        gq.column(1, 3, 2)
        gq.share(0)
        ss.step(2)
        gq.plane(0, 1, 3, 2)
        gq.share(1)
        gq.share(2)
        gw.plane(0)
        gw.column(1)
        gq.corner(0, 1, 3, 2)
        gq.share(3)
        gw.column(3)
        ss.finish(r.gains)
        r.stats[0:1, :] = r.gains[6:7, :]
        r.stats[1:2, :] = lax.rsqrt(r.gains[7:8, :] / (rows * 32) + EPS)
        gq.finish()

    def gather_column():
        gw.column(2)
        gw.share(0)

    def gather_step(k):
        if k == 0:
            gw.plane(1, 3)
        if k == 1:
            gw.plane(2)
            gw.share(1)
            gw.share(2)
        if k == 2:
            gw.corner(0, 1, 3)
        if k == 3:
            gw.corner(2)
            gw.share(3)
            gw.finish()

    pl.when(first)(enter if direct else clear)

    img_ref = r.img.at[pl.ds(mo(t * I, 16), I)] if direct else r.img
    mean = r.stats[0:1, :]
    inv = r.stats[1:2, :]
    g1, b1, g2 = r.gains[0:1, :], r.gains[1:2, :], r.gains[2:3, :]
    b2, gb, bb = r.gains[3:4, :], r.gains[4:5, :], r.gains[5:6, :]
    img_parts = ((0, 256), (256, 256), (512, I - 512))

    for r0, rl in img_parts:
        img_hat = (img_ref[r0 : r0 + rl, :].astype(f32) - mean) * inv
        r.imglow[r0 : r0 + rl, :] = (img_hat * gb + bb).astype(bf)
    for r0 in range(0, T, 256):
        q = dg(r.tag[r0 : r0 + 256, :], w_qkv(0, D), 1, 0).astype(bf) * bf(1.0 / math.sqrt(hd))
        r.q[r0 : r0 + 256, :] = q
        r.qT[:, r0 : r0 + 256] = q.T
    key_parts = tuple((r0, 256) for r0 in range(0, T, 256)) + tuple((T + r0, rl) for r0, rl in img_parts)
    for k0, kl in key_parts:
        if direct and k0 == T:
            pl.when(first)(gather_column)
        rows = r.tag[k0 : k0 + kl, :] if k0 < T else r.imglow[k0 - T : k0 - T + kl, :]
        for p in range(HEADS // 2):
            a = dg(rows, w_qkv(D + p * 4 * hd, D + (p + 1) * 4 * hd), 1, 0).astype(bf)
            ps = slice(p * 2 * hd, (p + 1) * 2 * hd)
            r.kall[k0 : k0 + kl, ps] = a[:, 0 : 2 * hd]
            r.vall[k0 : k0 + kl, ps] = a[:, 2 * hd :]
            r.xT[ps, k0 : k0 + kl] = a[:, 2 * hd :].T
    for ref, k0 in ((r.bias0, 0), (r.bias1, 256)):
        ji = k0 + lax.broadcasted_iota(jnp.int32, ref.shape, 0)
        ii = k0 + lax.broadcasted_iota(jnp.int32, ref.shape, 1)
        ref[...] = jnp.where((ji <= ii) & (ji < count), 3e38, NEG).astype(bf)

    chunks = [(512, 400, 0), (0, 256, 0), (256, 256, 256), (912, NK - 912, 0)]
    nc = len(chunks)
    row64 = lax.broadcasted_iota(jnp.int32, (2 * hd, 1), 0)
    lane64 = lax.broadcasted_iota(jnp.int32, (1, 2 * hd), 1)

    def own_rows(a, b):
        return jnp.where((row64 < hd) if b == 0 else (row64 >= hd), a, jnp.zeros_like(a))

    def own_lanes(a, b):
        return jnp.where((lane64 < hd) if b == 0 else (lane64 >= hd), a, jnp.zeros_like(a))

    def fullq(a, q0, fill):
        if q0 == 0:
            return a
        return jnp.concatenate([jnp.full((a.shape[0], q0), fill, a.dtype), a], 1)

    def e_at(h, c):
        k0, kl, q0 = chunks[c]
        if q0:
            return r.e1.at[h]
        return r.e.at[h, 0:kl] if k0 == 0 else r.e.at[h, k0 - 256 : k0 - 256 + kl]

    def score(p, b, c, qz):
        k0, kl, q0 = chunks[c]
        ps = pl.ds(mo(p * 2 * hd, 2 * hd), 2 * hd)
        s = dg(r.kall[k0 : k0 + kl, ps], qz[:, q0:], 1, 0)
        if k0 < T:
            s = jnp.minimum(s, (r.bias1 if q0 else r.bias0)[...].astype(f32))
        r.s[k0 : k0 + kl, q0:] = s
        return fullq(jnp.max(s, 0, keepdims=True), q0, NEG)

    def query(p, b):
        return own_rows(r.qT[pl.ds(mo(p * 2 * hd, 2 * hd), 2 * hd), :], b)

    def weigh(p, b, c, m):
        k0, kl, q0 = chunks[c]
        e = jnp.exp(r.s[k0 : k0 + kl, q0:] - m[:, q0:])
        l = jnp.sum(e, 0, keepdims=True)
        e = e.astype(bf)
        e_at(2 * p + b, c)[...] = e
        o = dg(r.xT[pl.ds(mo(p * 2 * hd + b * hd, hd), hd), k0 : k0 + kl], e, 1, 0)
        return fullq(o, q0, 0.0), fullq(l, q0, 0.0)

    def head(p, b, m, following):
        qz = None if following is None else query(*following)
        m2 = None
        o = None
        for c in range(nc):
            oc, lc = weigh(p, b, c, m)
            o, l = (oc, lc) if o is None else (o + oc, l + lc)
            if following is not None:
                mc = score(*following, c, qz)
                m2 = mc if m2 is None else jnp.maximum(m2, mc)
        rl = 1.0 / l
        o = o * rl
        hs = pl.ds(mo(p * 2 * hd + b * hd, hd), hd)
        r.attT[hs, :] = o.astype(bf)
        r.rl[2 * p + b] = rl
        return m2

    def fwd_pair(hooks, p, m):
        m = head(p, 0, m, (p, 1))
        m = head(p, 1, m, (jnp.minimum(p + 1, HEADS // 2 - 1), 0))
        if hooks:
            for k in range(HEADS // 2):
                pl.when(p == k)(functools.partial(gather_step, k))
        return m

    def forward(hooks):
        qz = query(0, 0)
        m = None
        for c in range(nc):
            mc = score(0, 0, c, qz)
            m = mc if m is None else jnp.maximum(m, mc)
        lax.fori_loop(0, HEADS // 2, functools.partial(fwd_pair, hooks), m)

    if direct:
        pl.when(first)(functools.partial(forward, True))
        pl.when(jnp.logical_not(first))(functools.partial(forward, False))
    else:
        forward(False)

    RC = 256
    zero = jnp.zeros((1, D), f32)

    def rows_part(r0):
        rs = pl.ds(r0, RC)
        hp = r.tag[rs, :].astype(f32) + dg(r.attT[:, rs], w_out(), 0, 0)
        yield
        c = hp - jnp.mean(hp, -1, keepdims=True)
        inv1 = lax.rsqrt(jnp.mean(c * c, -1, keepdims=True) + EPS)
        hat1 = c * inv1
        hidden = hat1 * g1 + b1
        hl = hidden.astype(bf)
        r.hidlow[rs, :] = hl
        yield
        pre = dg(hl, w_up(), 1, 0)
        yield
        p2 = pre * pre
        th = jnp.tanh(GC * (pre + GA * (p2 * pre)))
        act = (0.5 * pre * (1.0 + th)).astype(bf)
        r.act[rs, :] = act
        gp = 0.5 * (1.0 + th) + 0.5 * pre * (1.0 - th * th) * (GC * (1.0 + 3 * GA * p2))
        yield
        resid = hidden + dg(act, w_down(), 1, 0)
        yield
        c = resid - jnp.mean(resid, -1, keepdims=True)
        inv2 = lax.rsqrt(jnp.mean(c * c, -1, keepdims=True) + EPS)
        hat2 = c * inv2
        r.mixed[rs, :] = (hat2 * g2 + b2).astype(bf)
        rows = r0 + lax.broadcasted_iota(jnp.int32, (RC, 1), 0)
        go = jnp.where(rows < count, r.cot[rs, :].astype(f32), 0.0)
        r.terms[2:3, :] += jnp.sum(go * hat2, 0, keepdims=True)
        r.terms[3:4, :] += jnp.sum(go, 0, keepdims=True)
        s = go * g2
        gr = inv2 * (s - jnp.mean(s, -1, keepdims=True) - hat2 * jnp.mean(s * hat2, -1, keepdims=True))
        rlow = gr.astype(bf)
        r.rlow[rs, :] = rlow
        yield
        gact = dg(rlow, w_down(), 1, 1)
        yield
        plow = (gact * gp).astype(bf)
        r.plow[rs, :] = plow
        yield
        gh = gr + dg(plow, w_up(), 1, 1)
        yield
        r.terms[0:1, :] += jnp.sum(gh * hat1, 0, keepdims=True)
        r.terms[1:2, :] += jnp.sum(gh, 0, keepdims=True)
        s = gh * g1
        ghp = inv1 * (s - jnp.mean(s, -1, keepdims=True) - hat1 * jnp.mean(s * hat1, -1, keepdims=True))
        r.ghp[rs, :] = ghp
        hpl = ghp.astype(bf)
        r.hplow[rs, :] = hpl
        yield
        r.dOT[:, rs] = dg(hpl, w_out(), 1, 1).astype(bf).T
        yield

    parts = [rows_part(r0) for r0 in range(0, T, RC)]
    for i in range(12 + len(parts) - 1):
        for j, part in enumerate(parts):
            if 0 <= i - j < 12:
                next(part, None)
    for h in range(HEADS):
        hs = slice(h * hd, (h + 1) * hd)
        d = r.dOT[hs, :].astype(f32) * r.rl[h]
        r.dOT[hs, :] = d.astype(bf)
        r.delta[h] = jnp.sum(d * r.attT[hs, :].astype(f32), 0, keepdims=True)
    r.dO[...] = r.dOT[...].T
    for k0, kl in key_parts:
        r.xT[:, k0 : k0 + kl] = r.kall[k0 : k0 + kl, :].T

    def put(dst, acc, r0, rn, c0, cn, add, col=None):
        rs = pl.ds(r0, rn)
        new = acc[rs, c0 : c0 + cn] + add
        acc[rs, c0 : c0 + cn] = new
        col = c0 if col is None else col
        low = new.astype(bf)
        if direct:
            R = dst.shape[4]
            nz = rn // (8 * R)
            dst[pl.ds(r0 // (8 * R), nz), :, :, :, :, col : col + cn] = low.reshape(nz, 2, 2, 2, R, cn)
        else:
            dst[rs, col : col + cn] = low

    for r0 in range(0, F, 256):
        put(r.gd, r.adn, r0, 256, 0, D, dg(r.act[:, r0 : r0 + 256], r.rlow[...], 0, 0))
    for r0 in range(0, D, 256):
        put(r.gr0, r.aout, r0, 256, 0, D, dg(r.attT[r0 : r0 + 256, :], r.hplow[...], 1, 0))
        for c0, cn, dst, col in ((0, 256, r.gr0, D), (256, 512, r.gr1, 0), (768, F - 768, r.gr1, 512)):
            put(dst, r.aup, r0, 256, c0, cn, dg(r.hidlow[:, r0 : r0 + 256], r.plow[:, c0 : c0 + cn], 0, 0), col)
    when_last(sr0.core, sr1.core, sd.core) if direct else None

    def bwd_pair(hooks, p, _):
        p128 = mo(p * 2 * hd, 2 * hd)
        ps = pl.ds(p128, 2 * hd)
        dq = [None, None]
        ops = [(own_rows(r.dOT[ps, :], b), own_lanes(r.dO[:, ps], b), own_lanes(r.q[:, ps], b)) for b in range(2)]
        tc = pl.ds(mo(D + 2 * p128, 256), 4 * hd)
        ic = pl.ds(mo(2 * p128, 256), 4 * hd)
        for c in range(nc):
            k0, kl, q0 = chunks[c]
            ks = slice(k0, k0 + kl)
            dk = None
            for b in range(2):
                h = 2 * p + b
                hs = pl.ds(mo(p * 2 * hd + b * hd, hd), hd)
                dOz, dOl, ql = ops[b]
                dp = dg(r.vall[ks, ps], dOz[:, q0:], 1, 0)
                e = e_at(h, c)[...]
                ds = (e.astype(f32) * (dp - r.delta[h][:, q0:])).astype(bf)
                dvc = dg(e, dOl[q0:, :], 1, 0)
                dkc = dg(ds, ql[q0:, :], 1, 0)
                dqc = fullq(dg(r.xT[hs, ks], ds, 1, 0), q0, 0.0)
                dk, dv = (dkc, dvc) if dk is None else (dk + dkc, dv + dvc)
                dq[b] = dqc if dq[b] is None else dq[b] + dqc
            dkv = jnp.concatenate([dk.astype(bf), dv.astype(bf)], 1)
            if k0 < T:
                r.dqkv[ks, tc] = dkv
            else:
                r.dkvi[k0 - T : k0 - T + kl, ic] = dkv
            if hooks and c == 1:
                at_pair(p, halfway)
        for b in range(2):
            hs = pl.ds(mo(p * 2 * hd + b * hd, hd), hd)
            r.dqT[hs, :] = (dq[b] * (1.0 / math.sqrt(hd))).astype(bf)
        if hooks:
            at_pair(p, after)
        for i in range(3):

            @pl.when(p == i + 1)
            def _():
                qkv_piece(i)
                if hooks:
                    (sq0, sq1, sq2)[i].core()

        return 0

    if direct:
        halfway = ((sr0.plane1,), (sd.plane1,), (sr1.plane2,), (sd.plane2, sr0.column, sq1.plane1))
        after = ((sr1.plane1,), (sr0.plane2,), (sq0.plane1,), (sr1.column,))

    def at_pair(p, todo):
        for k, steps in enumerate(todo):
            if steps:

                @pl.when(p == k)
                def _():
                    for step in steps:
                        step()

    def qkv_piece(i):
        gq = (r.gq0, r.gq1, r.gq2)[i]
        a, b = ((0, 2), (2, 3), (3, 4))[i]
        qc = slice(a * 2 * hd, b * 2 * hd)
        kc = slice(a * 4 * hd, b * 4 * hd)
        tc = slice(D + kc.start, D + kc.stop)
        n = qc.stop - qc.start
        r.dqkv[:, qc] = r.dqT[qc, :].T
        for r0 in range(0, D, 256):
            rs = slice(r0, r0 + 256)
            x = r.tag[:, rs]
            put(gq, r.aqkv, r0, 256, qc.start, n, dg(x, r.dqkv[:, qc], 0, 0), 0)
            add = dg(x, r.dqkv[:, tc], 0, 0) + dg(r.imglow[:, rs], r.dkvi[:, kc], 0, 0)
            put(gq, r.aqkv, r0, 256, tc.start, 2 * n, add, n)

    def backward(hooks):
        lax.fori_loop(0, HEADS // 2, functools.partial(bwd_pair, hooks), 0)

    if direct:
        pl.when(last)(functools.partial(backward, True))
        pl.when(jnp.logical_not(last))(functools.partial(backward, False))
    else:
        backward(False)


    sg = jnp.zeros((1, D), f32)
    sb = sg
    for r0, rl in img_parts:
        rs = slice(r0, r0 + rl)
        gz = dg(r.dkvi[rs, :], w_qkv(D, 3 * D), 1, 1)
        r.gz[rs, :] = gz.astype(bf)
        hat = (img_ref[rs, :].astype(f32) - mean) * inv
        sg += jnp.sum(gz * hat, 0, keepdims=True)
        sb += jnp.sum(gz, 0, keepdims=True)
    r.terms[4:5, :] += sg
    r.terms[5:6, :] += sb
    if direct:

        @pl.when(last)
        def _():
            r.tb[0] = r.terms[...]
            sm.step(0)
            sq0.plane2()

    for r0 in range(0, T, 256):
        total = r.ghp[r0 : r0 + 256, :] + dg(r.dqkv[r0 : r0 + 256, :], w_qkv(0, 3 * D), 1, 1)
        r.gtags[r0 : r0 + 256, :] = total.astype(bf)

    if direct:

        @pl.when(last)
        def _():
            sm.step(1)
            sq2.plane1()
            sd.column()
            sq = sr0.finish()
            sq1.plane2()
            sq += sr1.finish()
            sm.step(2)
            sq0.column()
            sq2.column()
            sq1.column()
            sq += sd.finish()
            sq += sq0.finish()
            sm.finish(r.small)
            sq += sq1.finish()
            tot = r.small[...]
            r.small[6:7, :] = jnp.full((1, D), me.d, jnp.int32).astype(f32)
            sq += sq2.finish()
            r.nb[me.d] = jnp.full((1, 128), sq, f32)
            push_all(me, r.nb, r.ps.at[0], r.ps.at[1])
            r.nsq[...] = jnp.broadcast_to(jnp.sum(r.nb[...], 0) + jnp.sum(tot * tot), (8, 128))


def tables_call(direct, counts, tag, img, cot, params):
    n = counts.shape[0]
    T, I, D = tag.shape[0] // n, img.shape[0] // n, tag.shape[1]
    NK = T + I
    HC = D // 2
    V = lambda *s, d=bf: pltpu.VMEM(s, d)
    S = jax.ShapeDtypeStruct

    def row(a, b):
        return pl.BlockSpec((a, b), lambda t, *_: (t, 0))

    def whole(shape, **kw):
        return pl.BlockSpec(shape, lambda t, *_: (0,) * len(shape), **kw)

    one = dict(pipeline_mode=pl.Buffered(1))
    if direct:
        F = params[2].shape[1]
        R, RD = params[0].shape[0], params[3].shape[0]
        ins = [("tag", row(T, D)), ("img_hbm", pl.BlockSpec(memory_space=pl.ANY)), ("cot", row(T, D))]
        ins += [(k, whole(a.shape, **one)) for k, a in zip(("pqkv", "pout", "pup", "pdn", "pnorm"), params)]
    else:
        F = params[4].shape[0]
        ins = [("tag", row(T, D)), ("img", row(I, D)), ("cot", row(T, D))]
        ins += [(k, whole(a.shape, **one)) for k, a in zip(("stats", "gains", "wq", "wr", "wd"), params)]
    outs = [
        ("mixed", S((n * T, D), bf), row(T, D)),
        ("gtags", S((n * T, D), bf), row(T, D)),
        ("gz", S((n * I, D), bf), row(I, D)),
    ]
    scratch = [
        ("imglow", V(I, D)), ("kall", V(NK, D)), ("vall", V(NK, D)), ("xT", V(D, NK)),
        ("q", V(T, D)), ("qT", V(D, T)), ("bias0", V(256, T)), ("bias1", V(256, T - 256)), ("s", V(NK, T, d=f32)),
        ("e", V(HEADS, NK - 256, T)), ("e1", V(HEADS, 256, T - 256)), ("attT", V(D, T)),
        ("rl", V(HEADS, 1, T, d=f32)), ("plow", V(T, F)), ("ghp", V(T, D, d=f32)),
        ("dqkv", V(T, 3 * D)), ("dkvi", V(I, 2 * D)), ("dO", V(T, D)),
        ("dOT", V(D, T)), ("delta", V(HEADS, 1, T, d=f32)), ("aqkv", V(D, 3 * D, d=f32)), ("aout", V(D, D, d=f32)),
        ("aup", V(D, F, d=f32)), ("adn", V(F, D, d=f32)),
    ]
    if direct:
        outs += [
            ("oq0", S((R, 3 * HC), f32), None), ("oq1", S((R, 3 * HC // 2), f32), None), ("oq2", S((R, 3 * HC // 2), f32), None), ("or0", S((R, 3 * HC), f32), None),
            ("or1", S((R, D + F - 3 * HC), f32), None), ("od", S((RD, D), f32), None), ("small", S((8, D), f32), None), ("nsq", S((8, 128), f32), None),
            ("stats", S((2, D), f32), None), ("gains", S((8, D), f32), None),
        ]
        dims = (4, 2, 2, 2)
        dma = pltpu.SemaphoreType.DMA
        scratch += [
            ("img", V(n * I, D)), ("wq", V(*dims, R, 3 * D)), ("ww", V(*dims, R, 3 * D + F)), ("sb", V(10, 8, D, d=f32)),
            ("nb", V(32, 1, 128, d=f32)), ("terms", V(8, D, d=f32)), ("tb", V(10, 8, D, d=f32)),
            ("gq0", V(*dims, R, 3 * HC)), ("gq1", V(*dims, R, 3 * HC // 2)), ("gq2", V(*dims, R, 3 * HC // 2)), ("gr0", V(*dims, R, 3 * HC)),
            ("gr1", V(*dims, R, D + F - 3 * HC)), ("gd", V(*dims, RD, D)),
            ("bq0", Scatter.bufs(R, 3 * HC)), ("bq1", Scatter.bufs(R, 3 * HC // 2)), ("bq2", ScatterPlane.bufs(R, 3 * HC // 2)), ("br0", Scatter.bufs(R, 3 * HC)),
            ("br1", Scatter.bufs(R, D + F - 3 * HC)),
            ("bd", Scatter.bufs(RD, D)),
            ("isem", dma), ("gs", dma((4, Gather.SLOTS))), ("cs", dma((16, Scatter.SLOTS))), ("ps", dma((2,))),
        ]
        extra = dict(collective_id=0, has_side_effects=True)
    else:
        outs += [
            ("gq0", S((D, 3 * HC), bf), None), ("gq1", S((D, 3 * HC // 2), bf), None), ("gq2", S((D, 3 * HC // 2), bf), None), ("gr0", S((D, 3 * HC), bf), None),
            ("gr1", S((D, D + F - 3 * HC), bf), None),
            ("gd", S((F, D), bf), None), ("terms", S((8, D), f32), None),
        ]
        extra = {}
    names = ("counts",) + tuple(k for k, _ in ins) + tuple(k for k, _, _ in outs) + tuple(k for k, _ in scratch)
    return pl.pallas_call(
        functools.partial(tables_kernel, direct, names),
        out_shape=[s for _, s, _ in outs],
        grid_spec=pltpu.PrefetchScalarGridSpec(
            num_scalar_prefetch=1,
            grid=(n,),
            in_specs=[b for _, b in ins],
            out_specs=[whole(s.shape) if b is None else b for _, s, b in outs],
            scratch_shapes=[a for _, a in scratch],
        ),
        compiler_params=pltpu.CompilerParams(vmem_limit_bytes=255 * 2**18, **extra),
        name="tables",
    )(counts, tag, img, cot, *params)


def update_kernel(n_params, parts, total_rows, gz_in, img_in, stats_ref, gains_ref, small_ref, nsq_ref, *refs):
    n_in = 6 + 3 * n_params
    n_out = 5 * n_params
    hbm_in, (mixed_in, gtags_in), refs = refs[:n_in], refs[n_in : n_in + 2], refs[n_in + 2 :]
    (mixed_out, gtags_out, gimg_out, norm_ref), refs = refs[:4], refs[4:]
    hbm_out, refs = refs[:n_out], refs[n_out:]
    ins, outs, refs = refs[:n_in], refs[n_in : n_in + n_out], refs[n_in + n_out :]
    mixed, gtags_low, gtags, gz, img, gimg, in_sem, out_sem, pass_sem, part_sem = refs
    rows, D = gz.shape
    copy = pltpu.make_async_copy

    def part(i):
        at = pl.ds(i * (rows // parts), rows // parts)
        return at, copy(gz_in.at[at], gz.at[at], part_sem.at[0, i]), copy(img_in.at[at], img.at[at], part_sem.at[1, i])

    def given(i):
        at = pl.ds(i * (rows // parts), rows // parts)
        return copy(gimg.at[at], gimg_out.at[at], part_sem.at[2, i])

    for i in range(parts):
        _, a, b = part(i)
        a.start()
        b.start()
    for i, (a, b) in enumerate(((gtags_in, gtags_low), (mixed_in, mixed))):
        copy(a, b, pass_sem.at[i]).start()
    for i, (a, b) in enumerate(zip(hbm_in, ins)):
        copy(a, b, in_sem.at[i]).start()

    gb = gains_ref[4:5, :]
    k = stats_ref[1:2, :] * gb
    gsum = small_ref[4:5, :] / total_rows
    bsum = small_ref[5:6, :] / total_rows
    for i in range(parts):
        at, a, b = part(i)
        a.wait()
        b.wait()
        hat = (img[at, :].astype(f32) - stats_ref[0:1, :]) * stats_ref[1:2, :]
        gimg[at, :] = k * (gz[at, :].astype(f32) - bsum - hat * gsum)
        given(i).start()
    copy(mixed_in, mixed, pass_sem.at[1]).wait()
    copy(mixed, mixed_out, pass_sem.at[3]).start()
    copy(gtags_in, gtags_low, pass_sem.at[0]).wait()
    gtags[...] = gtags_low[...].astype(f32)
    copy(gtags, gtags_out, pass_sem.at[2]).start()

    for i, (a, b) in enumerate(zip(hbm_in, ins)):
        copy(a, b, in_sem.at[i]).wait()
    oq0, oq1, oq2, or0, or1, od = ins[:6]
    masters, firsts, seconds = (ins[6 + n_params * i : 6 + n_params * (i + 1)] for i in range(3))
    total_norm = jnp.sqrt(nsq_ref[0:1, 0:1])
    norm_ref[...] = total_norm
    factor = CLIP_AT / jnp.maximum(total_norm, CLIP_AT)
    cols = masters[4].shape[1]
    row = lax.broadcasted_iota(jnp.int32, (D, cols), 0)
    col = lax.broadcasted_iota(jnp.int32, (D, cols), 1)
    first = small_ref[6:7, 0:cols].astype(jnp.int32) * cols
    pick = (row == col + first).astype(f32)
    own = lax.dot_general(
        small_ref[...], pick, (((1,), (0,)), ((), ())), precision=lax.Precision.HIGHEST, preferred_element_type=f32
    )[0:6]
    pc = D // 4
    oq = [oq0[:, 0 : 2 * pc], oq1[:, 0:pc], oq2[:, 0:pc]]
    for j in (0, 1):
        oq += [oq0[:, (2 + j) * pc : (3 + j) * pc], oq0[:, (4 + j) * pc : (5 + j) * pc]]
        oq += [o[:, (1 + j) * pc : (2 + j) * pc] for o in (oq1, oq2)]
    grads = (jnp.concatenate(oq, 1), or0[:, 0:D], jnp.concatenate([or0[:, D:], or1[...]], 1), od[...], own)
    rates = (RATE_MATRIX, RATE_OUTPUT, RATE_MATRIX, RATE_MATRIX, RATE_NORMS)
    for i, (g, w, f, v) in enumerate(zip(grads, masters, firsts, seconds)):
        clip = g * factor
        moment = BETA_FIRST * f[...] + (1.0 - BETA_FIRST) * clip
        square = BETA_SECOND * v[...] + (1.0 - BETA_SECOND) * clip * clip
        u = (moment / (1.0 - BETA_FIRST**STEP)) / (jnp.sqrt(square / (1.0 - BETA_SECOND**STEP)) + ADAM_EPS)
        if i < 4:
            new = w[...] - rates[i] * (u + DECAY_RATE * w[...])
        else:
            new = w[...] - rates[i] * u
        for j, value in enumerate((clip, moment, square, new, new.astype(bf))):
            at = 5 * j + i
            outs[at][...] = value
            copy(outs[at], hbm_out[at], out_sem.at[at]).start()

    for i in range(n_out):
        copy(outs[i], hbm_out[i], out_sem.at[i]).wait()
    for i, (b, c) in enumerate(((gtags, gtags_out), (mixed, mixed_out))):
        copy(b, c, pass_sem.at[2 + i]).wait()
    for i in range(parts):
        given(i).wait()


def update(total_rows, mixed, gtags, gz, img, stats, gains, small, nsq, owned, masters, firsts, seconds):
    rows = gz.shape[0]
    parts = 7 if rows % 112 == 0 else 3
    anywhere = pl.BlockSpec(memory_space=pl.ANY)
    windows = (stats, gains, small, nsq)
    manual = tuple(owned) + tuple(masters) + tuple(firsts) + tuple(seconds)
    shapes = [jax.ShapeDtypeStruct(m.shape, f32) for m in masters] * 4 + [jax.ShapeDtypeStruct(m.shape, bf) for m in masters]
    gimg = jax.ShapeDtypeStruct(gz.shape, f32)
    dma = pltpu.SemaphoreType.DMA
    passed = [jax.ShapeDtypeStruct(mixed.shape, bf), jax.ShapeDtypeStruct(gtags.shape, f32)]
    return pl.pallas_call(
        functools.partial(update_kernel, len(masters), parts, total_rows),
        out_shape=passed + [gimg, jax.ShapeDtypeStruct((1, 1), f32)] + shapes,
        in_specs=[anywhere] * 2 + [VM] * 4 + [anywhere] * (len(manual) + 2),
        out_specs=[anywhere] * 3 + [VM] + [anywhere] * len(shapes),
        scratch_shapes=[pltpu.VMEM(a.shape, a.dtype) for a in manual + tuple(shapes) + (mixed, gtags, passed[1], gz, img, gimg)]
        + [dma((len(manual),)), dma((len(shapes),)), dma((4,)), dma((3, parts))],
        compiler_params=pltpu.CompilerParams(vmem_limit_bytes=63 * 2**20),
        name="update",
    )(gz, img, *windows, *manual, mixed, gtags)


def gather_any(img, wqkv, wout, wup, wdn, norm):
    full = lambda a, axis: lax.all_gather(a.astype(bf), AXES, axis=axis, tiled=True)
    gr = jnp.concatenate([full(wout, 0), full(wup, 0)], 1)
    gains = jnp.concatenate([full(norm, 1).astype(f32), jnp.zeros((2, img.shape[1]), f32)], 0)
    values = img.astype(f32)
    total = img.shape[0] * lax.axis_size(AXES)
    mean = lax.psum(jnp.sum(values, 0), AXES) / total
    centred = values - mean
    spread = lax.psum(jnp.sum(centred * centred, 0), AXES) / total
    D = img.shape[1]
    wq = full(wqkv, 0)
    kv = [wq[:, D:].reshape(D, 2, HEADS // 2, -1)[:, j, p] for p in range(HEADS // 2) for j in (0, 1)]
    return jnp.concatenate([wq[:, 0:D]] + kv, 1), gr, full(wdn, 0), jnp.stack([mean, lax.rsqrt(spread + EPS)]), gains


def scatter_any(gq0, gq1, gq2, gr0, gr1, gd, terms):
    part = lambda a: lax.psum_scatter(a.astype(f32), AXES, scatter_dimension=0, tiled=True)
    owned = [part(a) for a in (gq0, gq1, gq2, gr0, gr1, gd)]
    small = lax.psum(terms, AXES)
    local = sum(jnp.sum(a * a) for a in owned)
    nsq = lax.psum(local, AXES) + jnp.sum(small * small)
    small = small.at[6].set(lax.axis_index(AXES).astype(f32))
    return *owned, small, jnp.full((8, 128), nsq, f32)


def shards(direct, tag_inputs, image_inputs, tag_counts, cotangent, *params):
    masters, firsts, seconds = params[0:5], params[5:10], params[10:15]
    tables = tag_counts.shape[0]
    devices = lax.axis_size(AXES)
    total_rows = image_inputs.shape[0] * devices
    if direct:
        mixed, gtags, gz, *owned, small, nsq, stats, gains = tables_call(
            True, tag_counts, tag_inputs, image_inputs, cotangent, masters
        )
    else:
        wq, wr, wd, stats, gains = gather_any(image_inputs, *masters)
        mixed, gtags, gz, *sums = tables_call(
            False, tag_counts, tag_inputs, image_inputs, cotangent, (stats, gains, wq, wr, wd)
        )
        *owned, small, nsq = scatter_any(*sums)
    mixed, gtags, gimg, norm, *rest = update(
        total_rows, mixed, gtags, gz, image_inputs, stats, gains, small, nsq, owned, masters, firsts, seconds
    )
    return (mixed, gtags, gimg, norm.reshape(()), *rest)


def solution(mesh):
    rows = P(AXES, None)
    state = (rows, rows, rows, rows, P(None, AXES))
    direct = dict(mesh.shape) == {"wide": 16, "narrow": 2}
    return jax.shard_map(
        functools.partial(shards, direct),
        mesh=mesh,
        in_specs=(rows, rows, P(AXES), rows) + state * 3,
        out_specs=(rows, rows, rows, P()) + state * 5,
        check_vma=False,
    )
```

```python
import functools
import math

import jax
import jax.numpy as jnp
from jax import lax
from jax.experimental import pallas as pl
from jax.experimental.pallas import tpu as pltpu
from jax.sharding import PartitionSpec as P

f32 = jnp.float32
bf = jnp.bfloat16
MESH = pl.DeviceIdType.MESH
HEADS = 8
STEP = 10
EPS = 1e-05
NEG = -1000000000.0
CLIP_AT = 1.0
BETA_FIRST = 0.9
BETA_SECOND = 0.999
ADAM_EPS = 1e-08
RATE_MATRIX = 0.05
RATE_OUTPUT = 1.0
RATE_NORMS = 0.5
DECAY_RATE = 0.1
GC = math.sqrt(2 / math.pi)
GA = 0.044715
AXES = ("wide", "narrow")
VM = pl.BlockSpec(memory_space=pltpu.VMEM)


def dg(a, b, ca, cb):
    return lax.dot_general(a, b, (((ca,), (cb,)), ((), ())), preferred_element_type=f32)


class Place:
    def __init__(self):
        self.w = lax.axis_index("wide")
        self.c = lax.axis_index("narrow")
        self.x = lax.rem(self.w, 2)
        self.y = lax.rem(self.w // 2, 2)
        self.z = self.w // 4
        self.d = self.w * 2 + self.c
        self.to_x = (self.w + 1 - 2 * self.x, self.c)
        self.to_y = (self.w + 2 - 4 * self.y, self.c)
        self.to_d = (self.w + 3 - 2 * self.x - 4 * self.y, self.c)
        self.sib = (self.w, 1 - self.c)

    def to_z(self, k):
        return (lax.rem(self.w + 4 * k, 16), self.c)

    def peer(self, k):
        d = lax.rem(self.d + k, 32)
        return (d // 2, lax.rem(d, 2))


def greet(me):
    bar = pltpu.get_barrier_semaphore()
    near = (me.sib, me.to_x, me.to_y, me.to_d, me.to_z(1), me.to_z(2), me.to_z(3))
    for dev in near:
        pl.semaphore_signal(bar, inc=1, device_id=dev, device_id_type=MESH)
    pl.semaphore_wait(bar, len(near))


def remote(src, dst, ss, rs, dev):
    return pltpu.make_async_remote_copy(
        src_ref=src, dst_ref=dst, send_sem=ss, recv_sem=rs, device_id=dev, device_id_type=MESH
    )


def mo(a, n):
    return pl.multiple_of(a, n)


class Gather:
    SLOTS = 23

    def __init__(self, me, g, ss, rs):
        self.me, self.g, self.ss, self.rs = me, g, ss, rs
        self.h = g.shape[-1] // 2
        self.sent = []

    def ref(self, k, pos, part=None, c=None):
        me = self.me
        z = slice(None) if k is None else lax.rem(me.z + 4 - k, 4)
        y = me.y if pos in (0, 1) else 1 - me.y
        x = me.x if pos in (0, 2) else 1 - me.x
        at = (z, y, x, me.c if c is None else c)
        return self.g.at[at] if part is None else self.g.at[at + (slice(None), pl.ds(part * self.h, self.h))]

    def go(self, k, pos, part, slot, dev):
        ref = self.ref(k, pos, part)
        remote(ref, ref, self.ss.at[slot], self.rs.at[slot], dev).start()
        self.sent.append((k, pos, part, slot))

    def got(self, slot, *key, **kw):
        ref = self.ref(*key, **kw)
        remote(ref, ref, self.ss.at[slot], self.rs.at[slot], self.me.sib).wait_recv()

    def start(self):
        me = self.me
        for k in (2, 1, 3):
            self.go(0, 0, None, k - 1, me.to_z(k))
        self.go(0, 0, None, 3, me.to_x)
        self.go(0, 0, None, 7, me.to_y)

    def share(self, pos):
        self.go(None, pos, None, 19 + pos, self.me.sib)

    def column(self, *ks):
        me = self.me
        for k in ks:
            self.got(k - 1, k, 0)
            self.go(k, 0, None, 3 + k, me.to_x)
            self.go(k, 0, None, 7 + k, me.to_y)

    def plane(self, *ks):
        me = self.me
        for k in ks:
            self.got(3 + k, k, 1)
            self.go(k, 1, 0, 11 + k, me.to_y)
            self.got(7 + k, k, 2)
            self.go(k, 2, 1, 15 + k, me.to_x)

    def corner(self, *ks):
        for k in ks:
            self.got(11 + k, k, 3, 0)
            self.got(15 + k, k, 3, 1)

    def finish(self):
        for pos in range(4):
            self.got(19 + pos, None, pos, c=1 - self.me.c)
        for k, pos, part, slot in self.sent:
            ref = self.ref(k, pos, part)
            remote(ref, ref, self.ss.at[slot], self.rs.at[slot], self.me.sib).wait_send()


def push_all(me, g, ss, rs):
    for k in range(1, 32):
        remote(g.at[me.d], g.at[me.d], ss, rs, me.peer(k)).start()
    all_of = remote(g.at[pl.ds(0, 31)], g.at[pl.ds(0, 31)], ss, rs, me.sib)
    all_of.wait_send()
    all_of.wait_recv()


class Scatter:
    SLOTS = 8

    def __init__(self, me, g, out, bufs, sems):
        self.me, self.g, self.out, (self.ss, self.rs) = me, g, out, sems
        self.r0, self.r1a, self.r1b, self.r2a, self.r2b, self.s2, self.r3 = bufs
        self.s0, self.s1a, self.s1b = self.r0, self.r1a, self.r1b
        self.h = g.shape[-1] // 256 * 128

    @staticmethod
    def bufs(R, N):
        h = N // 256 * 128
        v = lambda *s: pltpu.VMEM(s, bf)
        return [
            v(4, 2, 2, R, N), v(4, 2, R, h), v(4, 2, R, N - h), v(4, R, h), v(4, R, N - h), v(4, R, N), v(3, R, N),
        ]

    def hop(self, slot):
        me = self.me
        if slot in (1, 2):
            h = self.h
            n = self.g.shape[-1] - h
        if slot == 0:
            src, dst, dev = self.g.at[:, :, :, 1 - me.c], self.r0, me.sib
        elif slot == 1:
            src, dst, dev = self.s0.at[:, :, 1 - me.x, :, pl.ds(0, h)], self.r1a, me.to_x
        elif slot == 2:
            src, dst, dev = self.s0.at[:, 1 - me.y, :, :, pl.ds(h, n)], self.r1b, me.to_y
        elif slot == 3:
            src, dst, dev = self.s1a.at[:, 1 - me.y], self.r2a, me.to_y
        elif slot == 4:
            src, dst, dev = self.s1b.at[:, 1 - me.x], self.r2b, me.to_x
        else:
            k = slot - 4
            src, dst, dev = self.s2.at[lax.rem(me.z + k, 4)], self.r3.at[k - 1], me.to_z(k)
        return remote(src, dst, self.ss.at[slot], self.rs.at[slot], dev)

    def core(self):
        self.hop(0).start()

    slots = tuple(range(8))

    def first_sum(self):
        me = self.me
        self.hop(0).wait_recv()

        for z in range(4):
            self.s0[z] = self.g[z, :, :, me.c] + self.r0[z]

    def plane1(self):
        self.first_sum()
        self.hop(1).start()
        self.hop(2).start()

    def plane2(self):
        me, h = self.me, self.h
        n = self.g.shape[-1] - h
        self.hop(1).wait_recv()
        self.hop(2).wait_recv()

        for z in range(4):
            self.s1a[z] = self.s0[z, :, me.x, :, pl.ds(0, h)] + self.r1a[z]
            self.s1b[z] = self.s0[z, me.y, :, :, pl.ds(h, n)] + self.r1b[z]
        self.hop(3).start()
        self.hop(4).start()

    def column(self):
        me, h = self.me, self.h
        self.hop(3).wait_recv()
        self.hop(4).wait_recv()
        for z in range(4):
            self.s2[z, :, 0:h] = self.s1a[z, me.y] + self.r2a[z]
            self.s2[z, :, h:] = self.s1b[z, me.x] + self.r2b[z]
        for k in (2, 1, 3):
            self.hop(4 + k).start()

    def finish(self):
        acc = self.s2[self.me.z].astype(f32)
        for k in (1, 2, 3):
            self.hop(4 + k).wait_recv()
            acc += self.r3[k - 1].astype(f32)
        self.out[...] = acc
        for slot in self.slots:
            self.hop(slot).wait_send()
        return jnp.sum(acc * acc)


class ScatterPlane(Scatter):
    def __init__(self, me, g, out, bufs, sems):
        self.me, self.g, self.out, (self.ss, self.rs) = me, g, out, sems
        self.r0, self.rp, self.s2, self.r3 = bufs
        self.s0 = self.r0

    @staticmethod
    def bufs(R, N):
        v = lambda *s: pltpu.VMEM(s, bf)
        return [v(4, 2, 2, R, N), v(3, 4, R, N), v(4, R, N), v(3, R, N)]

    def hop(self, slot):
        me = self.me
        if slot in (0, 5, 6, 7):
            return Scatter.hop(self, slot)
        y = me.y if slot == 1 else 1 - me.y
        x = me.x if slot == 2 else 1 - me.x
        dev = (me.to_x, me.to_y, me.to_d)[slot - 1]
        return remote(self.s0.at[:, y, x], self.rp.at[slot - 1], self.ss.at[slot], self.rs.at[slot], dev)

    def plane1(self):
        self.first_sum()
        for slot in (3, 1, 2):
            self.hop(slot).start()

    def column(self):
        me = self.me
        for slot in (1, 2, 3):
            self.hop(slot).wait_recv()
        for z in range(4):
            total = self.s0[z, me.y, me.x].astype(f32)
            for i in range(3):
                total += self.rp[i, z].astype(f32)
            self.s2[z] = total.astype(bf)
        for k in (2, 1, 3):
            self.hop(4 + k).start()

    slots = (0, 1, 2, 3, 5, 6, 7)


class Sums:
    def __init__(self, me, tb, ss, rs, rows=0):
        self.me, self.tb, self.ss, self.rs, self.rows = me, tb, ss, rs, rows

    def hop(self, slot):
        me = self.me
        if slot == 0:
            src, dst, dev = 0, 1, me.sib
        elif slot < 4:
            src = dst = 2 + me.y * 2 + me.x
            dev = (me.to_x, me.to_y, me.to_d)[slot - 1]
        else:
            src = dst = 6 + me.z
            dev = me.to_z(slot - 3)
        return remote(self.tb.at[src], self.tb.at[dst], self.ss.at[slot], self.rs.at[slot], dev)

    def arrived(self, slot):
        me = self.me
        y = me.y if slot == 1 else 1 - me.y
        x = me.x if slot == 2 else 1 - me.x
        at = 1 if slot == 0 else 2 + y * 2 + x if slot < 4 else 6 + lax.rem(me.z + 7 - slot, 4)
        at = self.tb.at[at]
        remote(at, at, self.ss.at[slot], self.rs.at[slot], me.sib).wait_recv()

    def merge(self, dst, at, rows):
        n = len(at)
        parts = [self.tb[a] for a in at]
        total = parts[0] + parts[1] if n == 2 else (parts[0] + parts[1]) + (parts[2] + parts[3])
        if not self.rows:
            dst[...] = total
            return
        mean = total[6:7] / n
        off = [p[6:7] - mean for p in parts]
        squares = off[0] * off[0] + off[1] * off[1]
        if n == 4:
            squares += off[2] * off[2] + off[3] * off[3]
        dst[0:6] = total[0:6]
        dst[6:7] = mean
        dst[7:8] = total[7:8] + rows * squares

    def step(self, i):
        me = self.me
        if i == 1:
            self.arrived(0)
            self.merge(self.tb.at[2 + me.y * 2 + me.x], (0, 1), self.rows)
        if i == 2:
            for slot in (1, 2, 3):
                self.arrived(slot)
            self.merge(self.tb.at[6 + me.z], (2, 3, 4, 5), self.rows * 2)
        for slot in ((0,), (3, 1, 2), (4, 5, 6))[i]:
            self.hop(slot).start()

    def finish(self, dst):
        for slot in (4, 5, 6):
            self.arrived(slot)
        for slot in range(7):
            self.hop(slot).wait_send()
        self.merge(dst, (6, 7, 8, 9), self.rows * 8)


class Refs:
    pass


def tables_kernel(direct, names, *refs):
    r = Refs()
    for name, ref in zip(names, refs, strict=True):
        setattr(r, name, ref)
    t = pl.program_id(0)
    first = t == 0
    last = t == pl.num_programs(0) - 1
    T, D = r.tag.shape
    I = r.imglow.shape[0]
    NK = T + I
    hd = D // HEADS
    F = r.plow.shape[1]
    r.hidlow, r.rlow = (r.dqkv.at[:, i * D : (i + 1) * D] for i in range(2))
    r.act = r.dkvi.at[0:T]
    r.dqT = r.attT
    count = r.counts[t]
    HC = D // 2
    if direct:
        me = Place()
        gq, gw = Gather(me, r.wq, r.gs.at[0], r.gs.at[1]), Gather(me, r.ww, r.gs.at[2], r.gs.at[3])
        sems = [(r.cs.at[2 * i], r.cs.at[2 * i + 1]) for i in range(8)]
        sq0 = Scatter(me, r.gq0, r.oq0, r.bq0, sems[0])
        sq1 = Scatter(me, r.gq1, r.oq1, r.bq1, sems[1])
        sq2 = ScatterPlane(me, r.gq2, r.oq2, r.bq2, sems[7])
        sr0 = Scatter(me, r.gr0, r.or0, r.br0, sems[2])
        sr1 = Scatter(me, r.gr1, r.or1, r.br1, sems[3])
        sd = Scatter(me, r.gd, r.od, r.bd, sems[4])
        sm = Sums(me, r.tb, *sems[5])
        ss = Sums(me, r.sb, *sems[6], rows=r.img.shape[0])
    def cols(ref, a, b):
        if not direct:
            return ref[:, a:b]
        return ref[:, :, :, :, :, a:b].reshape(D, b - a)

    def w_qkv(a, b):
        return cols(r.wq, a, b)

    def w_out():
        return cols(r.ww if direct else r.wr, 0, D)

    def w_up():
        return cols(r.ww if direct else r.wr, D, D + F)

    def w_down():
        if not direct:
            return r.wd[...]
        halves = [r.ww[:, :, :, :, :, a : a + D] for a in (D + F, 2 * D + F)]
        return jnp.stack(halves, 4).reshape(F, D)

    def when_last(*steps):
        @pl.when(last)
        def _():
            for step in steps:
                step()

    def clear():
        for ref in (r.aqkv, r.aout, r.aup, r.adn, r.terms):
            ref[...] = jnp.zeros_like(ref)

    def enter():
        img_in = pltpu.make_async_copy(r.img_hbm, r.img, r.isem)
        img_in.start()
        R, RD = r.pqkv.shape[0], r.pdn.shape[0]
        own = (me.z, me.y, me.x, me.c)
        r.wq[own + (slice(None), pl.ds(0, D))] = r.pqkv[:, 0:D].astype(bf)
        for p in range(HEADS // 2):
            for j in (0, 1):
                at = (j + 1) * D + p * 2 * hd
                to = pl.ds(D + (2 * p + j) * 2 * hd, 2 * hd)
                r.wq[own + (slice(None), to)] = r.pqkv[:, at : at + 2 * hd].astype(bf)
        greet(me)
        gq.start()
        for at, part in ((0, r.pout[...]), (D, r.pup[...]), (D + F, r.pdn[0:R, :]), (2 * D + F, r.pdn[R:RD, :])):
            r.ww[own + (slice(None), pl.ds(at, part.shape[1]))] = part.astype(bf)
        gw.start()
        share = D // 32
        lane = lax.broadcasted_iota(jnp.int32, (share, D), 1)
        unit = lax.broadcasted_iota(jnp.int32, (share, D), 0)
        at = (lane == unit + share * me.d).astype(bf)
        r.sb[0, 0:6, :] = dg(r.pnorm[...].astype(bf), at, 1, 0)
        img_in.wait()
        rows = r.img.shape[0]
        part = 112 if rows % 112 == 0 else I

        def over_rows(f):
            def step(i, acc):
                return acc + f(r.img[pl.ds(mo(i * part, 16), part), :].astype(f32))

            return jnp.sum(lax.fori_loop(0, rows // part, step, jnp.zeros((8, D), f32)), 0, keepdims=True)

        def fold(a):
            return jnp.sum(a.reshape(-1, 8, D), 0)

        mean_d = over_rows(fold) / rows
        m2 = over_rows(lambda a: fold((a - mean_d) * (a - mean_d)))
        r.sb[0, 6:7, :] = mean_d
        r.sb[0, 7:8, :] = m2
        ss.step(0)
        clear()
        ss.step(1)
        gq.column(1, 3, 2)
        gq.share(0)
        ss.step(2)
        gq.plane(0, 1, 3, 2)
        gq.share(1)
        gq.share(2)
        gw.plane(0)
        gw.column(1)
        gq.corner(0, 1, 3, 2)
        gq.share(3)
        gw.column(3)
        ss.finish(r.gains)
        r.stats[0:1, :] = r.gains[6:7, :]
        r.stats[1:2, :] = lax.rsqrt(r.gains[7:8, :] / (rows * 32) + EPS)
        gq.finish()

    def gather_column():
        gw.column(2)
        gw.share(0)

    def gather_step(k):
        if k == 0:
            gw.plane(1, 3)
        if k == 1:
            gw.plane(2)
            gw.share(1)
            gw.share(2)
        if k == 2:
            gw.corner(0, 1, 3)
        if k == 3:
            gw.corner(2)
            gw.share(3)
            gw.finish()

    pl.when(first)(enter if direct else clear)

    img_ref = r.img.at[pl.ds(mo(t * I, 16), I)] if direct else r.img
    mean = r.stats[0:1, :]
    inv = r.stats[1:2, :]
    g1, b1, g2 = r.gains[0:1, :], r.gains[1:2, :], r.gains[2:3, :]
    b2, gb, bb = r.gains[3:4, :], r.gains[4:5, :], r.gains[5:6, :]
    img_parts = ((0, 256), (256, 256), (512, I - 512))

    for r0, rl in img_parts:
        img_hat = (img_ref[r0 : r0 + rl, :].astype(f32) - mean) * inv
        r.imglow[r0 : r0 + rl, :] = (img_hat * gb + bb).astype(bf)
    for r0 in range(0, T, 256):
        q = dg(r.tag[r0 : r0 + 256, :], w_qkv(0, D), 1, 0).astype(bf) * bf(1.0 / math.sqrt(hd))
        r.q[r0 : r0 + 256, :] = q
        r.qT[:, r0 : r0 + 256] = q.T
    key_parts = tuple((r0, 256) for r0 in range(0, T, 256)) + tuple((T + r0, rl) for r0, rl in img_parts)
    for k0, kl in key_parts:
        if direct and k0 == T:
            pl.when(first)(gather_column)
        rows = r.tag[k0 : k0 + kl, :] if k0 < T else r.imglow[k0 - T : k0 - T + kl, :]
        for p in range(HEADS // 2):
            a = dg(rows, w_qkv(D + p * 4 * hd, D + (p + 1) * 4 * hd), 1, 0).astype(bf)
            ps = slice(p * 2 * hd, (p + 1) * 2 * hd)
            r.kall[k0 : k0 + kl, ps] = a[:, 0 : 2 * hd]
            r.vall[k0 : k0 + kl, ps] = a[:, 2 * hd :]
            r.xT[ps, k0 : k0 + kl] = a[:, 2 * hd :].T
    for ref, k0 in ((r.bias0, 0), (r.bias1, 256)):
        ji = k0 + lax.broadcasted_iota(jnp.int32, ref.shape, 0)
        ii = k0 + lax.broadcasted_iota(jnp.int32, ref.shape, 1)
        ref[...] = jnp.where((ji <= ii) & (ji < count), 3e38, NEG).astype(bf)

    chunks = [(512, 400, 0), (0, 256, 0), (256, 256, 256), (912, NK - 912, 0)]
    nc = len(chunks)
    row64 = lax.broadcasted_iota(jnp.int32, (2 * hd, 1), 0)
    lane64 = lax.broadcasted_iota(jnp.int32, (1, 2 * hd), 1)

    def own_rows(a, b):
        return jnp.where((row64 < hd) if b == 0 else (row64 >= hd), a, jnp.zeros_like(a))

    def own_lanes(a, b):
        return jnp.where((lane64 < hd) if b == 0 else (lane64 >= hd), a, jnp.zeros_like(a))

    def fullq(a, q0, fill):
        if q0 == 0:
            return a
        return jnp.concatenate([jnp.full((a.shape[0], q0), fill, a.dtype), a], 1)

    def e_at(h, c):
        k0, kl, q0 = chunks[c]
        if q0:
            return r.e1.at[h]
        return r.e.at[h, 0:kl] if k0 == 0 else r.e.at[h, k0 - 256 : k0 - 256 + kl]

    def score(p, b, c, qz):
        k0, kl, q0 = chunks[c]
        ps = pl.ds(mo(p * 2 * hd, 2 * hd), 2 * hd)
        s = dg(r.kall[k0 : k0 + kl, ps], qz[:, q0:], 1, 0)
        if k0 < T:
            s = jnp.minimum(s, (r.bias1 if q0 else r.bias0)[...].astype(f32))
        r.s[k0 : k0 + kl, q0:] = s
        return fullq(jnp.max(s, 0, keepdims=True), q0, NEG)

    def query(p, b):
        return own_rows(r.qT[pl.ds(mo(p * 2 * hd, 2 * hd), 2 * hd), :], b)

    def weigh(p, b, c, m):
        k0, kl, q0 = chunks[c]
        e = jnp.exp(r.s[k0 : k0 + kl, q0:] - m[:, q0:])
        l = jnp.sum(e, 0, keepdims=True)
        e = e.astype(bf)
        e_at(2 * p + b, c)[...] = e
        o = dg(r.xT[pl.ds(mo(p * 2 * hd + b * hd, hd), hd), k0 : k0 + kl], e, 1, 0)
        return fullq(o, q0, 0.0), fullq(l, q0, 0.0)

    def head(p, b, m, following):
        qz = None if following is None else query(*following)
        m2 = None
        o = None
        for c in range(nc):
            oc, lc = weigh(p, b, c, m)
            o, l = (oc, lc) if o is None else (o + oc, l + lc)
            if following is not None:
                mc = score(*following, c, qz)
                m2 = mc if m2 is None else jnp.maximum(m2, mc)
        rl = 1.0 / l
        o = o * rl
        hs = pl.ds(mo(p * 2 * hd + b * hd, hd), hd)
        r.attT[hs, :] = o.astype(bf)
        r.rl[2 * p + b] = rl
        return m2

    def fwd_pair(hooks, p, m):
        m = head(p, 0, m, (p, 1))
        m = head(p, 1, m, (jnp.minimum(p + 1, HEADS // 2 - 1), 0))
        if hooks:
            for k in range(HEADS // 2):
                pl.when(p == k)(functools.partial(gather_step, k))
        return m

    def forward(hooks):
        qz = query(0, 0)
        m = None
        for c in range(nc):
            mc = score(0, 0, c, qz)
            m = mc if m is None else jnp.maximum(m, mc)
        lax.fori_loop(0, HEADS // 2, functools.partial(fwd_pair, hooks), m)

    if direct:
        pl.when(first)(functools.partial(forward, True))
        pl.when(jnp.logical_not(first))(functools.partial(forward, False))
    else:
        forward(False)

    RC = 256
    zero = jnp.zeros((1, D), f32)

    def rows_part(r0):
        rs = pl.ds(r0, RC)
        hp = r.tag[rs, :].astype(f32) + dg(r.attT[:, rs], w_out(), 0, 0)
        yield
        c = hp - jnp.mean(hp, -1, keepdims=True)
        inv1 = lax.rsqrt(jnp.mean(c * c, -1, keepdims=True) + EPS)
        hat1 = c * inv1
        hidden = hat1 * g1 + b1
        hl = hidden.astype(bf)
        r.hidlow[rs, :] = hl
        yield
        pre = dg(hl, w_up(), 1, 0)
        yield
        p2 = pre * pre
        th = jnp.tanh(GC * (pre + GA * (p2 * pre)))
        act = (0.5 * pre * (1.0 + th)).astype(bf)
        r.act[rs, :] = act
        gp = 0.5 * (1.0 + th) + 0.5 * pre * (1.0 - th * th) * (GC * (1.0 + 3 * GA * p2))
        yield
        resid = hidden + dg(act, w_down(), 1, 0)
        yield
        c = resid - jnp.mean(resid, -1, keepdims=True)
        inv2 = lax.rsqrt(jnp.mean(c * c, -1, keepdims=True) + EPS)
        hat2 = c * inv2
        r.mixed[rs, :] = (hat2 * g2 + b2).astype(bf)
        rows = r0 + lax.broadcasted_iota(jnp.int32, (RC, 1), 0)
        go = jnp.where(rows < count, r.cot[rs, :].astype(f32), 0.0)
        r.terms[2:3, :] += jnp.sum(go * hat2, 0, keepdims=True)
        r.terms[3:4, :] += jnp.sum(go, 0, keepdims=True)
        s = go * g2
        gr = inv2 * (s - jnp.mean(s, -1, keepdims=True) - hat2 * jnp.mean(s * hat2, -1, keepdims=True))
        rlow = gr.astype(bf)
        r.rlow[rs, :] = rlow
        yield
        gact = dg(rlow, w_down(), 1, 1)
        yield
        plow = (gact * gp).astype(bf)
        r.plow[rs, :] = plow
        yield
        gh = gr + dg(plow, w_up(), 1, 1)
        yield
        r.terms[0:1, :] += jnp.sum(gh * hat1, 0, keepdims=True)
        r.terms[1:2, :] += jnp.sum(gh, 0, keepdims=True)
        s = gh * g1
        ghp = inv1 * (s - jnp.mean(s, -1, keepdims=True) - hat1 * jnp.mean(s * hat1, -1, keepdims=True))
        hpl = ghp.astype(bf)
        r.hplow[rs, :] = hpl
        yield
        r.dOT[:, rs] = dg(hpl, w_out(), 1, 1).astype(bf).T
        yield

    parts = [rows_part(r0) for r0 in range(0, T, RC)]
    for i in range(12 + len(parts) - 1):
        for j, part in enumerate(parts):
            if 0 <= i - j < 12:
                next(part, None)
    for h in range(HEADS):
        hs = slice(h * hd, (h + 1) * hd)
        d = r.dOT[hs, :].astype(f32) * r.rl[h]
        r.dOT[hs, :] = d.astype(bf)
        r.delta[h] = jnp.sum(d * r.attT[hs, :].astype(f32), 0, keepdims=True)
    r.dO[...] = r.dOT[...].T
    for k0, kl in key_parts:
        r.xT[:, k0 : k0 + kl] = r.kall[k0 : k0 + kl, :].T

    def put(dst, acc, r0, rn, c0, cn, add, col=None):
        rs = pl.ds(r0, rn)
        new = acc[rs, c0 : c0 + cn] + add
        acc[rs, c0 : c0 + cn] = new
        col = c0 if col is None else col
        low = new.astype(bf)
        if direct:
            R = dst.shape[4]
            nz = rn // (8 * R)
            dst[pl.ds(r0 // (8 * R), nz), :, :, :, :, col : col + cn] = low.reshape(nz, 2, 2, 2, R, cn)
        else:
            dst[rs, col : col + cn] = low

    for r0 in range(0, F, 256):
        put(r.gd, r.adn, r0, 256, 0, D, dg(r.act[:, r0 : r0 + 256], r.rlow[...], 0, 0))
    for r0 in range(0, D, 256):
        put(r.gr0, r.aout, r0, 256, 0, D, dg(r.attT[r0 : r0 + 256, :], r.hplow[...], 1, 0))
        for c0, cn, dst, col in ((0, 256, r.gr0, D), (256, 512, r.gr1, 0), (768, F - 768, r.gr1, 512)):
            put(dst, r.aup, r0, 256, c0, cn, dg(r.hidlow[:, r0 : r0 + 256], r.plow[:, c0 : c0 + cn], 0, 0), col)
    when_last(sr0.core, sr1.core, sd.core) if direct else None

    def bwd_pair(hooks, p, _):
        p128 = mo(p * 2 * hd, 2 * hd)
        ps = pl.ds(p128, 2 * hd)
        dq = [None, None]
        ops = [(own_rows(r.dOT[ps, :], b), own_lanes(r.dO[:, ps], b), own_lanes(r.q[:, ps], b)) for b in range(2)]
        tc = pl.ds(mo(D + 2 * p128, 256), 4 * hd)
        ic = pl.ds(mo(2 * p128, 256), 4 * hd)
        for c in range(nc):
            k0, kl, q0 = chunks[c]
            ks = slice(k0, k0 + kl)
            dps = [dg(r.vall[ks, ps], ops[b][0][:, q0:], 1, 0) for b in range(2)]
            es = [e_at(2 * p + b, c)[...] for b in range(2)]
            dv = dg(es[0], ops[0][1][q0:, :], 1, 0) + dg(es[1], ops[1][1][q0:, :], 1, 0)
            dss = [(es[b].astype(f32) * (dps[b] - r.delta[2 * p + b][:, q0:])).astype(bf) for b in range(2)]
            dk = dg(dss[0], ops[0][2][q0:, :], 1, 0) + dg(dss[1], ops[1][2][q0:, :], 1, 0)
            for b in range(2):
                hs = pl.ds(mo(p * 2 * hd + b * hd, hd), hd)
                dqc = fullq(dg(r.xT[hs, ks], dss[b], 1, 0), q0, 0.0)
                dq[b] = dqc if dq[b] is None else dq[b] + dqc
            dkv = jnp.concatenate([dk.astype(bf), dv.astype(bf)], 1)
            if k0 < T:
                r.dqkv[ks, tc] = dkv
            else:
                r.dkvi[k0 - T : k0 - T + kl, ic] = dkv
            if hooks and c == 1:
                at_pair(p, halfway)
        for b in range(2):
            hs = pl.ds(mo(p * 2 * hd + b * hd, hd), hd)
            r.dqT[hs, :] = (dq[b] * (1.0 / math.sqrt(hd))).astype(bf)
        if hooks:
            at_pair(p, after)
        for i in range(3):

            @pl.when(p == i + 1)
            def _():
                qkv_piece(i)
                if hooks:
                    (sq0, sq1, sq2)[i].core()

        return 0

    if direct:
        halfway = ((sr0.plane1,), (sd.plane1,), (sr1.plane2,), (sd.plane2, sr0.column, sq1.plane1))
        after = ((sr1.plane1,), (sr0.plane2,), (sq0.plane1,), (sr1.column,))

    def at_pair(p, todo):
        for k, steps in enumerate(todo):
            if steps:

                @pl.when(p == k)
                def _():
                    for step in steps:
                        step()

    def qkv_piece(i):
        gq = (r.gq0, r.gq1, r.gq2)[i]
        a, b = ((0, 2), (2, 3), (3, 4))[i]
        qc = slice(a * 2 * hd, b * 2 * hd)
        kc = slice(a * 4 * hd, b * 4 * hd)
        tc = slice(D + kc.start, D + kc.stop)
        n = qc.stop - qc.start
        r.dqkv[:, qc] = r.dqT[qc, :].T
        for r0 in range(0, D, 256):
            rs = slice(r0, r0 + 256)
            x = r.tag[:, rs]
            put(gq, r.aqkv, r0, 256, qc.start, n, dg(x, r.dqkv[:, qc], 0, 0), 0)
            add = dg(x, r.dqkv[:, tc], 0, 0) + dg(r.imglow[:, rs], r.dkvi[:, kc], 0, 0)
            put(gq, r.aqkv, r0, 256, tc.start, 2 * n, add, n)

    def backward(hooks):
        lax.fori_loop(0, HEADS // 2, functools.partial(bwd_pair, hooks), 0)

    if direct:
        pl.when(last)(functools.partial(backward, True))
        pl.when(jnp.logical_not(last))(functools.partial(backward, False))
    else:
        backward(False)


    sg = jnp.zeros((1, D), f32)
    sb = sg
    for r0, rl in img_parts:
        rs = slice(r0, r0 + rl)
        gz = dg(r.dkvi[rs, :], w_qkv(D, 3 * D), 1, 1)
        r.gz[rs, :] = gz.astype(bf)
        hat = (img_ref[rs, :].astype(f32) - mean) * inv
        sg += jnp.sum(gz * hat, 0, keepdims=True)
        sb += jnp.sum(gz, 0, keepdims=True)
    r.terms[4:5, :] += sg
    r.terms[5:6, :] += sb
    if direct:

        @pl.when(last)
        def _():
            r.tb[0] = r.terms[...]
            sm.step(0)
            sq0.plane2()

    for r0 in range(0, T, 256):
        total = r.hplow[r0 : r0 + 256, :].astype(f32) + dg(r.dqkv[r0 : r0 + 256, :], w_qkv(0, 3 * D), 1, 1)
        r.gtags[r0 : r0 + 256, :] = total.astype(bf)

    if direct:

        @pl.when(last)
        def _():
            sm.step(1)
            sq2.plane1()
            sd.column()
            sq = sr0.finish()
            sq1.plane2()
            sq += sr1.finish()
            sm.step(2)
            sq0.column()
            sq2.column()
            sq1.column()
            sq += sd.finish()
            sq += sq0.finish()
            sm.finish(r.small)
            sq += sq1.finish()
            tot = r.small[...]
            r.small[6:7, :] = jnp.full((1, D), me.d, jnp.int32).astype(f32)
            sq += sq2.finish()
            r.nb[me.d] = jnp.full((1, 128), sq, f32)
            push_all(me, r.nb, r.ps.at[0], r.ps.at[1])
            r.nsq[...] = jnp.broadcast_to(jnp.sum(r.nb[...], 0) + jnp.sum(tot * tot), (8, 128))


def tables_call(direct, counts, tag, img, cot, params):
    n = counts.shape[0]
    T, I, D = tag.shape[0] // n, img.shape[0] // n, tag.shape[1]
    NK = T + I
    HC = D // 2
    V = lambda *s, d=bf: pltpu.VMEM(s, d)
    S = jax.ShapeDtypeStruct

    def row(a, b):
        return pl.BlockSpec((a, b), lambda t, *_: (t, 0))

    def whole(shape, **kw):
        return pl.BlockSpec(shape, lambda t, *_: (0,) * len(shape), **kw)

    one = dict(pipeline_mode=pl.Buffered(1))
    if direct:
        F = params[2].shape[1]
        R, RD = params[0].shape[0], params[3].shape[0]
        ins = [("tag", row(T, D)), ("img_hbm", pl.BlockSpec(memory_space=pl.ANY)), ("cot", row(T, D))]
        ins += [(k, whole(a.shape, **one)) for k, a in zip(("pqkv", "pout", "pup", "pdn", "pnorm"), params)]
    else:
        F = params[4].shape[0]
        ins = [("tag", row(T, D)), ("img", row(I, D)), ("cot", row(T, D))]
        ins += [(k, whole(a.shape, **one)) for k, a in zip(("stats", "gains", "wq", "wr", "wd"), params)]
    outs = [
        ("mixed", S((n * T, D), bf), row(T, D)),
        ("gtags", S((n * T, D), bf), row(T, D)),
        ("gz", S((n * I, D), bf), row(I, D)),
    ]
    scratch = [
        ("imglow", V(I, D)), ("kall", V(NK, D)), ("vall", V(NK, D)), ("xT", V(D, NK)),
        ("q", V(T, D)), ("qT", V(D, T)), ("bias0", V(256, T)), ("bias1", V(256, T - 256)), ("s", V(NK, T, d=f32)),
        ("e", V(HEADS, NK - 256, T)), ("e1", V(HEADS, 256, T - 256)), ("attT", V(D, T)),
        ("rl", V(HEADS, 1, T, d=f32)), ("plow", V(T, F)), ("hplow", V(T, D)),
        ("dqkv", V(T, 3 * D)), ("dkvi", V(I, 2 * D)), ("dO", V(T, D)),
        ("dOT", V(D, T)), ("delta", V(HEADS, 1, T, d=f32)), ("aqkv", V(D, 3 * D, d=f32)), ("aout", V(D, D, d=f32)),
        ("aup", V(D, F, d=f32)), ("adn", V(F, D, d=f32)),
    ]
    if direct:
        outs += [
            ("oq0", S((R, 3 * HC), f32), None), ("oq1", S((R, 3 * HC // 2), f32), None), ("oq2", S((R, 3 * HC // 2), f32), None), ("or0", S((R, 3 * HC), f32), None),
            ("or1", S((R, D + F - 3 * HC), f32), None), ("od", S((RD, D), f32), None), ("small", S((8, D), f32), None), ("nsq", S((8, 128), f32), None),
            ("stats", S((2, D), f32), None), ("gains", S((8, D), f32), None),
        ]
        dims = (4, 2, 2, 2)
        dma = pltpu.SemaphoreType.DMA
        scratch += [
            ("img", V(n * I, D)), ("wq", V(*dims, R, 3 * D)), ("ww", V(*dims, R, 3 * D + F)), ("sb", V(10, 8, D, d=f32)),
            ("nb", V(32, 1, 128, d=f32)), ("terms", V(8, D, d=f32)), ("tb", V(10, 8, D, d=f32)),
            ("gq0", V(*dims, R, 3 * HC)), ("gq1", V(*dims, R, 3 * HC // 2)), ("gq2", V(*dims, R, 3 * HC // 2)), ("gr0", V(*dims, R, 3 * HC)),
            ("gr1", V(*dims, R, D + F - 3 * HC)), ("gd", V(*dims, RD, D)),
            ("bq0", Scatter.bufs(R, 3 * HC)), ("bq1", Scatter.bufs(R, 3 * HC // 2)), ("bq2", ScatterPlane.bufs(R, 3 * HC // 2)), ("br0", Scatter.bufs(R, 3 * HC)),
            ("br1", Scatter.bufs(R, D + F - 3 * HC)),
            ("bd", Scatter.bufs(RD, D)),
            ("isem", dma), ("gs", dma((4, Gather.SLOTS))), ("cs", dma((16, Scatter.SLOTS))), ("ps", dma((2,))),
        ]
        extra = dict(collective_id=0, has_side_effects=True)
    else:
        outs += [
            ("gq0", S((D, 3 * HC), bf), None), ("gq1", S((D, 3 * HC // 2), bf), None), ("gq2", S((D, 3 * HC // 2), bf), None), ("gr0", S((D, 3 * HC), bf), None),
            ("gr1", S((D, D + F - 3 * HC), bf), None),
            ("gd", S((F, D), bf), None), ("terms", S((8, D), f32), None),
        ]
        extra = {}
    names = ("counts",) + tuple(k for k, _ in ins) + tuple(k for k, _, _ in outs) + tuple(k for k, _ in scratch)
    return pl.pallas_call(
        functools.partial(tables_kernel, direct, names),
        out_shape=[s for _, s, _ in outs],
        grid_spec=pltpu.PrefetchScalarGridSpec(
            num_scalar_prefetch=1,
            grid=(n,),
            in_specs=[b for _, b in ins],
            out_specs=[whole(s.shape) if b is None else b for _, s, b in outs],
            scratch_shapes=[a for _, a in scratch],
        ),
        compiler_params=pltpu.CompilerParams(vmem_limit_bytes=255 * 2**18, **extra),
        name="tables",
    )(counts, tag, img, cot, *params)


def update_kernel(n_params, parts, total_rows, gz_in, img_in, stats_ref, gains_ref, small_ref, nsq_ref, *refs):
    n_in = 6 + 3 * n_params
    n_out = 5 * n_params
    hbm_in, (mixed_in, gtags_in), refs = refs[:n_in], refs[n_in : n_in + 2], refs[n_in + 2 :]
    (mixed_out, gtags_out, gimg_out, norm_ref), refs = refs[:4], refs[4:]
    hbm_out, refs = refs[:n_out], refs[n_out:]
    ins, outs, refs = refs[:n_in], refs[n_in : n_in + n_out], refs[n_in + n_out :]
    mixed, gtags_low, gtags, gz, img, gimg, in_sem, out_sem, pass_sem, part_sem = refs
    rows, D = gz.shape
    copy = pltpu.make_async_copy

    def part(i):
        at = pl.ds(i * (rows // parts), rows // parts)
        return at, copy(gz_in.at[at], gz.at[at], part_sem.at[0, i]), copy(img_in.at[at], img.at[at], part_sem.at[1, i])

    def given(i):
        at = pl.ds(i * (rows // parts), rows // parts)
        return copy(gimg.at[at], gimg_out.at[at], part_sem.at[2, i])

    for i in range(parts):
        _, a, b = part(i)
        a.start()
        b.start()
    for i, (a, b) in enumerate(((gtags_in, gtags_low), (mixed_in, mixed))):
        copy(a, b, pass_sem.at[i]).start()
    for i, (a, b) in enumerate(zip(hbm_in, ins)):
        copy(a, b, in_sem.at[i]).start()

    gb = gains_ref[4:5, :]
    k = stats_ref[1:2, :] * gb
    gsum = small_ref[4:5, :] / total_rows
    bsum = small_ref[5:6, :] / total_rows
    for i in range(parts):
        at, a, b = part(i)
        a.wait()
        b.wait()
        hat = (img[at, :].astype(f32) - stats_ref[0:1, :]) * stats_ref[1:2, :]
        gimg[at, :] = k * (gz[at, :].astype(f32) - bsum - hat * gsum)
        given(i).start()
    copy(mixed_in, mixed, pass_sem.at[1]).wait()
    copy(mixed, mixed_out, pass_sem.at[3]).start()
    copy(gtags_in, gtags_low, pass_sem.at[0]).wait()
    gtags[...] = gtags_low[...].astype(f32)
    copy(gtags, gtags_out, pass_sem.at[2]).start()

    for i, (a, b) in enumerate(zip(hbm_in, ins)):
        copy(a, b, in_sem.at[i]).wait()
    oq0, oq1, oq2, or0, or1, od = ins[:6]
    masters, firsts, seconds = (ins[6 + n_params * i : 6 + n_params * (i + 1)] for i in range(3))
    total_norm = jnp.sqrt(nsq_ref[0:1, 0:1])
    norm_ref[...] = total_norm
    factor = CLIP_AT / jnp.maximum(total_norm, CLIP_AT)
    cols = masters[4].shape[1]
    row = lax.broadcasted_iota(jnp.int32, (D, cols), 0)
    col = lax.broadcasted_iota(jnp.int32, (D, cols), 1)
    first = small_ref[6:7, 0:cols].astype(jnp.int32) * cols
    pick = (row == col + first).astype(f32)
    own = lax.dot_general(
        small_ref[...], pick, (((1,), (0,)), ((), ())), precision=lax.Precision.HIGHEST, preferred_element_type=f32
    )[0:6]
    pc = D // 4
    oq = [oq0[:, 0 : 2 * pc], oq1[:, 0:pc], oq2[:, 0:pc]]
    for j in (0, 1):
        oq += [oq0[:, (2 + j) * pc : (3 + j) * pc], oq0[:, (4 + j) * pc : (5 + j) * pc]]
        oq += [o[:, (1 + j) * pc : (2 + j) * pc] for o in (oq1, oq2)]
    grads = (jnp.concatenate(oq, 1), or0[:, 0:D], jnp.concatenate([or0[:, D:], or1[...]], 1), od[...], own)
    rates = (RATE_MATRIX, RATE_OUTPUT, RATE_MATRIX, RATE_MATRIX, RATE_NORMS)
    for i, (g, w, f, v) in enumerate(zip(grads, masters, firsts, seconds)):
        clip = g * factor
        moment = BETA_FIRST * f[...] + (1.0 - BETA_FIRST) * clip
        square = BETA_SECOND * v[...] + (1.0 - BETA_SECOND) * clip * clip
        u = (moment / (1.0 - BETA_FIRST**STEP)) / (jnp.sqrt(square / (1.0 - BETA_SECOND**STEP)) + ADAM_EPS)
        if i < 4:
            new = w[...] - rates[i] * (u + DECAY_RATE * w[...])
        else:
            new = w[...] - rates[i] * u
        for j, value in enumerate((clip, moment, square, new, new.astype(bf))):
            at = 5 * j + i
            outs[at][...] = value
            copy(outs[at], hbm_out[at], out_sem.at[at]).start()

    for i in range(n_out):
        copy(outs[i], hbm_out[i], out_sem.at[i]).wait()
    for i, (b, c) in enumerate(((gtags, gtags_out), (mixed, mixed_out))):
        copy(b, c, pass_sem.at[2 + i]).wait()
    for i in range(parts):
        given(i).wait()


def update(total_rows, mixed, gtags, gz, img, stats, gains, small, nsq, owned, masters, firsts, seconds):
    rows = gz.shape[0]
    parts = 7 if rows % 112 == 0 else 3
    anywhere = pl.BlockSpec(memory_space=pl.ANY)
    windows = (stats, gains, small, nsq)
    manual = tuple(owned) + tuple(masters) + tuple(firsts) + tuple(seconds)
    shapes = [jax.ShapeDtypeStruct(m.shape, f32) for m in masters] * 4 + [jax.ShapeDtypeStruct(m.shape, bf) for m in masters]
    gimg = jax.ShapeDtypeStruct(gz.shape, f32)
    dma = pltpu.SemaphoreType.DMA
    passed = [jax.ShapeDtypeStruct(mixed.shape, bf), jax.ShapeDtypeStruct(gtags.shape, f32)]
    return pl.pallas_call(
        functools.partial(update_kernel, len(masters), parts, total_rows),
        out_shape=passed + [gimg, jax.ShapeDtypeStruct((1, 1), f32)] + shapes,
        in_specs=[anywhere] * 2 + [VM] * 4 + [anywhere] * (len(manual) + 2),
        out_specs=[anywhere] * 3 + [VM] + [anywhere] * len(shapes),
        scratch_shapes=[pltpu.VMEM(a.shape, a.dtype) for a in manual + tuple(shapes) + (mixed, gtags, passed[1], gz, img, gimg)]
        + [dma((len(manual),)), dma((len(shapes),)), dma((4,)), dma((3, parts))],
        compiler_params=pltpu.CompilerParams(vmem_limit_bytes=63 * 2**20),
        name="update",
    )(gz, img, *windows, *manual, mixed, gtags)


def gather_any(img, wqkv, wout, wup, wdn, norm):
    full = lambda a, axis: lax.all_gather(a.astype(bf), AXES, axis=axis, tiled=True)
    gr = jnp.concatenate([full(wout, 0), full(wup, 0)], 1)
    gains = jnp.concatenate([full(norm, 1).astype(f32), jnp.zeros((2, img.shape[1]), f32)], 0)
    values = img.astype(f32)
    total = img.shape[0] * lax.axis_size(AXES)
    mean = lax.psum(jnp.sum(values, 0), AXES) / total
    centred = values - mean
    spread = lax.psum(jnp.sum(centred * centred, 0), AXES) / total
    D = img.shape[1]
    wq = full(wqkv, 0)
    kv = [wq[:, D:].reshape(D, 2, HEADS // 2, -1)[:, j, p] for p in range(HEADS // 2) for j in (0, 1)]
    return jnp.concatenate([wq[:, 0:D]] + kv, 1), gr, full(wdn, 0), jnp.stack([mean, lax.rsqrt(spread + EPS)]), gains


def scatter_any(gq0, gq1, gq2, gr0, gr1, gd, terms):
    part = lambda a: lax.psum_scatter(a.astype(f32), AXES, scatter_dimension=0, tiled=True)
    owned = [part(a) for a in (gq0, gq1, gq2, gr0, gr1, gd)]
    small = lax.psum(terms, AXES)
    local = sum(jnp.sum(a * a) for a in owned)
    nsq = lax.psum(local, AXES) + jnp.sum(small * small)
    small = small.at[6].set(lax.axis_index(AXES).astype(f32))
    return *owned, small, jnp.full((8, 128), nsq, f32)


def shards(direct, tag_inputs, image_inputs, tag_counts, cotangent, *params):
    masters, firsts, seconds = params[0:5], params[5:10], params[10:15]
    tables = tag_counts.shape[0]
    devices = lax.axis_size(AXES)
    total_rows = image_inputs.shape[0] * devices
    if direct:
        mixed, gtags, gz, *owned, small, nsq, stats, gains = tables_call(
            True, tag_counts, tag_inputs, image_inputs, cotangent, masters
        )
    else:
        wq, wr, wd, stats, gains = gather_any(image_inputs, *masters)
        mixed, gtags, gz, *sums = tables_call(
            False, tag_counts, tag_inputs, image_inputs, cotangent, (stats, gains, wq, wr, wd)
        )
        *owned, small, nsq = scatter_any(*sums)
    mixed, gtags, gimg, norm, *rest = update(
        total_rows, mixed, gtags, gz, image_inputs, stats, gains, small, nsq, owned, masters, firsts, seconds
    )
    return (mixed, gtags, gimg, norm.reshape(()), *rest)


def solution(mesh):
    rows = P(AXES, None)
    state = (rows, rows, rows, rows, P(None, AXES))
    direct = dict(mesh.shape) == {"wide": 16, "narrow": 2}
    return jax.shard_map(
        functools.partial(shards, direct),
        mesh=mesh,
        in_specs=(rows, rows, P(AXES), rows) + state * 3,
        out_specs=(rows, rows, rows, P()) + state * 5,
        check_vma=False,
    )
```
